256 devices in a mesh: dp: 32 (over x, z), cent: 8 (over y, core).
Axes of the slice: x: 4, y: 4, z: 8, core: 2. Of those that a mesh axis runs over, the one named last changes fastest.
Arguments:
- embeddings: bfloat16 [16384, 1024], P('dp'), may hold values from -20 to 20
- centroids: bfloat16 [32768, 1024], P(('cent', 'dp')), may hold values from -0.5 to 0.5
- masses: float32 [32768], P(('cent', 'dp')), may hold values from 0.05 to 2
Outputs:
- new_centroids: float32 [32768, 1024], P(('cent', 'dp'))
- new_masses: float32 [32768], P(('cent', 'dp'))
- row_energy: float32 [16384], P('dp')
The draws below stay inside these ranges and needn't reach their ends.
All inputs are finite; a program needn't handle non-finite values.
Results may differ from the reference program's by a relative error of at most 0.0023.
Values may be sent and summed in bfloat16 or wider, within the bound.
No kernel may reach another device: no remote copies, remote signals or barrier semaphores. Data moves between devices by JAX's collectives and lax.ppermute only.
A program may use at most 128 MiB of HBM per device.

```python
import math
import jax
import jax.numpy as jnp
from jax import lax

D = 1024
K = 32768
TOKENS = 16384


def centroid_table(key, spread):
    normal = jnp.clip(jax.random.normal(key, (K, D), jnp.float32), -5.0, 5.0) / math.sqrt(D)
    position = jnp.arange(K) % (K // 8)
    paired = (position == 0) | (position == 1)
    level = jax.random.uniform(jax.random.fold_in(key, 11), (K, 1), jnp.float32, -0.5, 0.5)
    scales = jnp.where(paired[:, None], 1.0, jnp.exp(level * math.log(spread)))
    table = normal * scales
    mixed = table
    return jnp.where((position == 1)[:, None], mixed, table)


def draw_centroids(key, part):
    table = centroid_table(key, 1.0)
    return jnp.clip(table, -0.5, 0.5).astype(jnp.bfloat16)


def draw_embeddings(key, part):
    own_key = jax.random.fold_in(key, 3)
    values = jnp.clip(jax.random.normal(own_key, (TOKENS, D), jnp.float32), -6.0, 6.0)
    return values.astype(jnp.bfloat16)


def level_of(key, dims, cuts, least, top_value):
    def one(axis_at, blocks):
        draws = jax.random.uniform(jax.random.fold_in(jax.random.fold_in(key, 6), axis_at), (blocks,), jnp.float32, least / len(cuts), top_value / len(cuts))
        return jnp.repeat(jnp.exp(draws), dims[axis_at] // blocks).reshape((-1,) + (1,) * (len(dims) - axis_at - 1))

    loudness = one(*cuts[0])
    for cut in cuts[1:]:
        loudness = loudness * one(*cut)
    return loudness


def setup_inputs(seed: int = 0) -> dict:
    key_list = jax.random.split(jax.random.key(seed), 4)
    embeddings = draw_embeddings(jax.random.fold_in(key_list[3], 71), 0)
    centroids = draw_centroids(jax.random.fold_in(key_list[3], 71), 0)
    masses = jnp.clip(jnp.exp(math.log(2.0) - 3.6888794 * jax.random.uniform(key_list[2], (K,), jnp.float32) ** level_of(key_list[2], (K,), ((0, 256),), -0.2, 0.2)), 0.05, 2.0)
    return {"embeddings": embeddings, "centroids": centroids, "masses": masses}


def reference(embeddings, centroids, masses):
    wide = centroids.astype(jnp.float32)
    squares = jnp.sum(jnp.square(wide), axis=1)
    block_rows = math.gcd(TOKENS, 512)
    blocks = embeddings.reshape(TOKENS // block_rows, block_rows, D)
    flipped = centroids.T

    def step(carry, rows):
        sums, counts = carry
        logits = 2.0 * jnp.dot(rows, flipped, preferred_element_type=jnp.float32) - squares[None, :]
        highest = jnp.max(logits, axis=1)
        total = jnp.sum(jnp.exp(logits - highest[:, None]), axis=1)
        energy = highest + jnp.log(total)
        weights = jnp.exp(logits - energy[:, None])
        counts = counts + jnp.sum(weights, axis=0)
        sums = sums + jnp.dot(weights.astype(jnp.bfloat16).T, rows, preferred_element_type=jnp.float32)
        return (sums, counts), energy

    start = (jnp.zeros((K, D), jnp.float32), jnp.zeros((K,), jnp.float32))
    (sums, counts), energies = lax.scan(step, start, blocks)
    row_energy = energies.reshape(TOKENS)
    new_masses = masses + counts
    new_centroids = (masses[:, None] * wide + sums) / new_masses[:, None]
    return new_centroids, new_masses, row_energy
```

```python
import jax
import jax.numpy as jnp
from jax import lax
from jax.sharding import Mesh, PartitionSpec as P

NX, NZ, NY, NC = 4, 8, 4, 2
BF16, F32 = jnp.bfloat16, jnp.float32


def shift(value, axis, size, by):
    return lax.ppermute(value, axis, [(i, (i + by) % size) for i in range(size)])


def across_y(value):
    pairs = []
    for y in range(NY):
        pairs.append((y * NC, (y + 1) % NY * NC))
        pairs.append((y * NC + 1, (y - 1) % NY * NC + 1))
    return lax.ppermute(value, ("y", "c"), pairs)


def gather_rows(embeddings, y, c):
    rows = embeddings.shape[0]
    quarter = rows // NY
    half = quarter // 2

    def own(place):
        start = lax.rem(place + NY, NY) * quarter
        return lax.dynamic_slice_in_dim(embeddings, start, quarter, 0)

    first = own(y + c)
    second = own(jnp.where(c == 0, y - 1, y + 2))
    groups = [[first, second]]
    back = ahead = first
    for step in range(1, NZ // 2):
        back = shift(back, "z", NZ, 1)
        ahead = shift(ahead, "z", NZ, -1)
        groups.append([back, across_y(back), ahead, across_y(ahead)])
    back = shift(back[:half], "z", NZ, 1)
    ahead = shift(ahead[half:], "z", NZ, -1)
    groups.append([back, ahead, across_y(back), across_y(ahead)])
    return groups


def combine(parts):
    stack = jnp.stack(parts)
    high = jnp.max(stack, axis=0)
    return high + jnp.log(jnp.sum(jnp.exp(stack - high[None]), axis=0))


def shards(embeddings, centroids, masses):
    x, z, y, c = (lax.axis_index(a) for a in ("x", "z", "y", "c"))
    rows, width = embeddings.shape
    quarter = rows // NY
    mine_n = centroids.shape[0]

    near = [centroids] + [shift(centroids, "x", NX, -d) for d in range(1, NX)]
    mine = jnp.concatenate(near)
    table = jnp.concatenate([mine, shift(mine, "c", NC, 1)])
    squares = jnp.sum(jnp.square(table.astype(F32)), axis=1)

    g = gather_rows(embeddings, y, c)
    b1, b2, b3 = g[1], g[2], g[3]
    pieces = g[0] + b1[2:] + b2[2:] + b3[2:] + g[4] + b3[:2] + b2[:2] + b1[:2]
    slab = jnp.concatenate(pieces)

    logits = 2.0 * lax.dot_general(
        table, slab, (((1,), (1,)), ((), ())), preferred_element_type=F32
    ) - squares[:, None]
    high = jnp.max(logits, axis=0)
    local = high + jnp.log(jnp.sum(jnp.exp(logits - high[None, :]), axis=0))

    local = local.reshape(NZ, 2, quarter)
    parts = [local]
    for d in range(1, NZ):
        parts.append(jnp.roll(shift(local, "z", NZ, d), -d, axis=0))
    local = combine(parts)
    other = shift(local, "c", NC, 1)
    low = jnp.where(c == 0, local, other)
    top = jnp.where(c == 0, other, local)
    four = jnp.stack([low[:, 0], top[:, 0], top[:, 1], low[:, 1]], axis=1)
    parts = [four]
    for d in range(1, NY):
        parts.append(jnp.roll(shift(four, "y", NY, d), -d, axis=1))
    four = combine(parts)
    energy = jnp.where(c == 0, four[:, jnp.array([0, 3])], four[:, jnp.array([1, 2])]).reshape(-1)
    own = jnp.concatenate([four[0], four[0]])
    row_energy = lax.dynamic_slice_in_dim(own, lax.rem(NY - y, NY), NY, 0).reshape(-1)

    weights = jnp.exp(logits - energy[None, :])
    counts = jnp.sum(weights, axis=1)
    sums = jnp.dot(weights.astype(BF16), slab, preferred_element_type=F32)

    part = NX * mine_n
    sums = sums[:part] + shift(sums[part:].astype(BF16), "c", NC, 1).astype(F32)
    counts = counts[:part] + shift(counts[part:], "c", NC, 1)
    total, count = sums[:mine_n], counts[:mine_n]
    for d in range(1, NX):
        lot = slice(d * mine_n, (d + 1) * mine_n)
        total = total + shift(sums[lot].astype(BF16), "x", NX, d).astype(F32)
        count = count + shift(counts[lot], "x", NX, d)
    new_masses = masses + count
    new_centroids = (masses[:, None] * centroids.astype(F32) + total) / new_masses[:, None]
    return new_centroids, new_masses, row_energy


def solution(mesh):
    grid = Mesh(mesh.devices.reshape(NX, NZ, NY, NC), ("x", "z", "y", "c"))
    rows, cents = ("x", "z"), ("y", "c", "x", "z")
    return jax.shard_map(
        shards,
        mesh=grid,
        in_specs=(P(rows, None), P(cents, None), P(cents)),
        out_specs=(P(cents, None), P(cents), P(rows)),
        check_vma=False,
    )
```

```python
import functools

import jax
import jax.numpy as jnp
from jax import lax
from jax.experimental import pallas as pl
from jax.experimental.pallas import tpu as pltpu
from jax.sharding import Mesh, PartitionSpec as P

NX, NZ, NY, NC = 4, 8, 4, 2
BF16, F32 = jnp.bfloat16, jnp.float32
TAIL = 16
ORDER = (2, 1, 3, 0)
VMEM_LIMIT = 30 * 1024 * 1024


def shift_x(value, by):
    return lax.ppermute(value, "x", [(i, (i + by) % NX) for i in range(NX)])


def swap_cores(value):
    return lax.ppermute(value, "c", [(0, 1), (1, 0)])


def along_z(value, by):
    pairs = []
    for z in range(NZ):
        pairs.append((z * NC, (z + by) % NZ * NC))
        pairs.append((z * NC + 1, (z - by) % NZ * NC + 1))
    return lax.ppermute(value, ("z", "c"), pairs)


def along_y(value, by):
    pairs = []
    for y in range(NY):
        pairs.append((y * NC, (y + by) % NY * NC))
        pairs.append((y * NC + 1, (y - by) % NY * NC + 1))
    return lax.ppermute(value, ("y", "c"), pairs)


def swap_halves(value):
    pairs = []
    for y in range(NY):
        pairs.append((y * NC, (y ^ 1) * NC))
        pairs.append((y * NC + 1, (y + 1 if y % 2 else y - 1) % NY * NC + 1))
    return lax.ppermute(value, ("y", "c"), pairs)


def pick(place, first, second):
    return jnp.where(place == 0, first, second)


def combine(parts):
    high = functools.reduce(jnp.maximum, parts)
    return high + jnp.log(sum(jnp.exp(p - high) for p in parts))


def energies(local, h, y, z, c):
    steps = [local[0]] + [pick(h, v, v[::-1]) for v in local[1:]]
    mine = jnp.concatenate([v.reshape(-1, v.shape[-1]) for v in steps])
    other = swap_cores(mine)

    def split(flat):
        out, at = [], 0
        for v in steps:
            n = v.shape[0] * v.shape[1]
            out.append(flat[at : at + n].reshape(v.shape))
            at += n
        return out

    back, ahead = split(pick(c, mine, other)), split(pick(c, other, mine))
    both = lambda k: jnp.concatenate([back[k], ahead[k]], axis=1)
    block = jnp.stack([both(0), ahead[1], ahead[2], ahead[3], both(4), back[3], back[2], back[1]])

    none = jnp.full_like(block, -1e30)
    parts = [pick(c, block, none)]
    for d in range(1, 4):
        got = along_z(block, d)
        parts.append(pick(c, jnp.roll(got, -d, axis=0), jnp.roll(got, d, axis=0)))
    parts.append(pick(c, jnp.roll(along_z(block, 4), 4, axis=0), none))
    part = combine(parts)
    block = combine([part, swap_cores(part)])

    parts = [pick(c, block, none), along_y(block, 1), pick(c, along_y(block, 2), none)]
    part = combine(parts)
    block = combine([part, swap_cores(part)])

    own = lambda v: pick(c, v[:, :1], v[:, 1:])
    out = [own(block[0])]
    for k in range(1, 4):
        v = pick(c, block[NZ - k], block[k])
        out.append(pick(h, v, v[::-1]))
    v = own(block[4])
    out.append(pick(h, v, v[::-1]))
    return jnp.concatenate([v.reshape(1, -1) for v in out], axis=1), block[0].reshape(-1)


def turned(column):
    n = column.shape[0]
    return jnp.transpose(jnp.broadcast_to(column, (n, n)))


def write_message(message, at, total, row):
    n, width = total.shape
    message[at : at + n, :] = total.astype(BF16)
    high = row.astype(BF16)
    tail = [high, (row - high.astype(F32)).astype(BF16)]
    if width > 2 * n:
        tail.append(jnp.zeros((TAIL, width - 2 * n), BF16))
    message[at + n : at + n + TAIL, :] = jnp.concatenate(tail, axis=1)


def read_message(message, at, n):
    total = message[at : at + n, :].astype(F32)
    tail = message[at + n : at + n + TAIL, :].astype(F32)
    return total, tail[:, :n] + tail[:, n : 2 * n]


def weigh_kernel(sizes, energy, *refs):
    pieces = len(sizes)
    logits, slab = refs[:pieces], refs[pieces : 2 * pieces]
    message, keep, keep_count = refs[2 * pieces :]
    n, width = keep.shape
    counts, sets, at = None, [], 0
    for p, size in enumerate(sizes):
        w = jnp.exp(logits[p][...] - energy[:, at : at + size])
        at += size
        for cut in range(0, size, sizes[-1]):
            part = w[:, cut : cut + sizes[-1]]
            counts = part if counts is None else counts + part
        sets.append(w.astype(BF16))
    column = jnp.sum(counts, axis=1, keepdims=True)
    tile = min(256, width)
    totals = []
    for at in range(0, width, tile):
        acc = None
        for p in range(pieces):
            if sizes[p] < sizes[1] and p == pieces - 1:
                continue
            w, rows = sets[p], slab[p][:, at : at + tile]
            if sizes[p] < sizes[1]:
                w = jnp.concatenate([w, sets[p + 1]], axis=1)
                rows = jnp.concatenate([rows, slab[p + 1][:, at : at + tile]])
            term = jnp.dot(w, rows, preferred_element_type=F32)
            acc = term if acc is None else acc + term
        keep[:, at : at + tile] = acc[:n]
        totals.append(acc[n:])
    keep_count[...] = turned(column[:n])[:TAIL]
    write_message(message, 0, jnp.concatenate(totals, axis=1), turned(column[n:])[:TAIL])


def weigh(first, count, logits, energy, slab):
    span, width = logits[0].shape[0] // NX, slab[0].shape[1]
    n = span // NC
    sizes = tuple(p.shape[0] for p in slab)
    block = lambda rows, cols: pl.BlockSpec((rows, cols), lambda i: (i, 0))
    whole = lambda v: pl.BlockSpec(v.shape, lambda i: (0, 0))
    return pl.pallas_call(
        functools.partial(weigh_kernel, sizes),
        grid=(count,),
        in_specs=[whole(energy)]
        + [pl.BlockSpec((span, p.shape[1]), lambda i: (i + first, 0)) for p in logits]
        + [whole(p) for p in slab],
        out_specs=(block(n + TAIL, width), block(n, width), block(TAIL, n)),
        out_shape=(
            jax.ShapeDtypeStruct((count * (n + TAIL), width), BF16),
            jax.ShapeDtypeStruct((count * n, width), F32),
            jax.ShapeDtypeStruct((count * TAIL, n), F32),
        ),
        compiler_params=pltpu.CompilerParams(vmem_limit_bytes=VMEM_LIMIT),
        cost_estimate=pl.CostEstimate(
            flops=2 * count * span * sum(sizes) * width,
            bytes_accessed=4 * count * span * sum(sizes) + 2 * sum(sizes) * width,
            transcendentals=count * span * sum(sizes),
        ),
    )(energy, *logits, *slab)


def call(kernel, out_shape, *args):
    return pl.pallas_call(
        kernel,
        out_shape=out_shape,
        compiler_params=pltpu.CompilerParams(vmem_limit_bytes=VMEM_LIMIT),
    )(*args)


def add_kernel(n, got, keep, keep_count, *messages):
    for i, message in enumerate(messages):
        total, row = read_message(got, i * (n + TAIL), n)
        total = total + keep[i * n : (i + 1) * n, :]
        write_message(message, 0, total, row + keep_count[i * TAIL : (i + 1) * TAIL, :])


def add(got, keep, keep_count):
    n = keep_count.shape[1]
    shape = jax.ShapeDtypeStruct((n + TAIL, got.shape[1]), BF16)
    return call(functools.partial(add_kernel, n), (shape,) * (NX - 1), got, keep, keep_count)


def update_kernel(n, keep, keep_count, got, one, two, three, masses, centroids, new_centroids, new_masses):
    total, row = keep[...], keep_count[...]
    for message in (got, one, two, three):
        t, r = read_message(message, 0, n)
        total, row = total + t, row + r
    mass = masses[...]
    new = mass + row[:1]
    new_masses[...] = new
    column = lambda v: jnp.transpose(jnp.broadcast_to(v, (n, n)))[:, :1]
    new_centroids[...] = (column(mass) * centroids[...].astype(F32) + total) / column(new)


def update(keep, keep_count, got, others, masses, centroids):
    n, width = centroids.shape
    out = (jax.ShapeDtypeStruct((n, width), F32), jax.ShapeDtypeStruct((1, n), F32))
    return call(
        functools.partial(update_kernel, n), out, keep, keep_count, got, *others, masses.reshape(1, n), centroids
    )


def shards(embeddings, centroids, masses):
    z, y, c = (lax.axis_index(a) for a in ("z", "y", "c"))
    rows, width = embeddings.shape
    half, sub = rows // 2, rows // 4
    h = lax.rem(y, 2)

    mine = lax.dynamic_slice_in_dim(embeddings, h * half, half, 0)
    stream = along_z(mine, 1)
    last = along_z(lax.dynamic_slice_in_dim(mine, c * sub, sub, 0), NZ // 2)
    own = lax.dynamic_slice_in_dim(embeddings.reshape(2, 2, sub, width), c, 1, 1).reshape(half, width)
    near = {d: shift_x(centroids, -d) for d in (1, 2, 3)}
    pieces = [own, stream, swap_halves(stream)]
    for step in range(2, NZ // 2):
        stream = along_z(stream, 1)
        pieces += [stream, swap_halves(stream)]
    pieces += [last, swap_halves(last)]

    near[0] = centroids
    mine = jnp.concatenate([near[d] for d in ORDER])
    other = swap_cores(mine)
    table = jnp.stack([mine.reshape(NX, -1, width), other.reshape(NX, -1, width)], axis=1).reshape(-1, width)
    squares = jnp.sum(jnp.square(table.astype(F32)), axis=1)[:, None]

    logits, local = [], []
    for piece in pieces:
        scores = 2.0 * lax.dot_general(table, piece, (((1,), (1,)), ((), ())), preferred_element_type=F32) - squares
        high = jnp.max(scores, axis=0)
        local.append(high + jnp.log(jnp.sum(jnp.exp(scores - high[None, :]), axis=0)))
        logits.append(scores)
    steps = [local[0].reshape(2, 1, sub)]
    steps += [jnp.stack(local[k : k + 2]).reshape(2, 2, sub) for k in (1, 3, 5)]
    steps += [jnp.stack(local[7:]).reshape(2, 1, sub)]
    energy, row_energy = energies(steps, h, y, z, c)

    message, keep, keep_count = weigh(0, NX - 1, logits, energy, pieces)
    sent = add(swap_cores(message), keep, keep_count)
    message, keep, keep_count = weigh(NX - 1, 1, logits, energy, pieces)
    others = [shift_x(m, d) for m, d in zip(sent, ORDER)]
    new_centroids, new_masses = update(keep, keep_count, swap_cores(message), others, masses, centroids)
    return new_centroids, new_masses.reshape(-1), row_energy


def solution(mesh):
    grid = Mesh(mesh.devices.reshape(NX, NZ, NY, NC), ("x", "z", "y", "c"))
    rows, cents = ("x", "z"), ("y", "c", "x", "z")
    return jax.shard_map(
        shards,
        mesh=grid,
        in_specs=(P(rows, None), P(cents, None), P(cents)),
        out_specs=(P(cents, None), P(cents), P(rows)),
        check_vma=False,
    )
```

```python
import functools

import jax
import jax.numpy as jnp
from jax import lax
from jax.experimental import pallas as pl
from jax.experimental.pallas import tpu as pltpu
from jax.sharding import Mesh, PartitionSpec as P

NX, NZ, NY, NC = 4, 8, 4, 2
BF16, F32 = jnp.bfloat16, jnp.float32
TAIL = 16
ORDER = (2, 1, 3, 0)
VMEM_LIMIT = 30 * 1024 * 1024
PIN = True


def shift_x(value, by):
    return lax.ppermute(value, "x", [(i, (i + by) % NX) for i in range(NX)])


def swap_cores(value):
    return lax.ppermute(value, "c", [(0, 1), (1, 0)])


def along_z(value, by):
    pairs = []
    for z in range(NZ):
        pairs.append((z * NC, (z + by) % NZ * NC))
        pairs.append((z * NC + 1, (z - by) % NZ * NC + 1))
    return lax.ppermute(value, ("z", "c"), pairs)


def swap_halves(value):
    pairs = []
    for y in range(NY):
        pairs.append((y * NC, (y ^ 1) * NC))
        pairs.append((y * NC + 1, (y + 1 if y % 2 else y - 1) % NY * NC + 1))
    return lax.ppermute(value, ("y", "c"), pairs)


def pick(place, first, second):
    return jnp.where(place == 0, first, second)


def combine(parts):
    high = functools.reduce(jnp.maximum, parts)
    return high + jnp.log(sum(jnp.exp(p - high) for p in parts))


def energies(local, z, c, h):
    rows = local.shape[1]
    got = lax.all_to_all(jnp.broadcast_to(local[None], (NY * NC,) + local.shape), ("y", "c"), 0, 0, tiled=True)
    got = got.reshape(NY, NC, *local.shape)

    def in_order(v, odd):
        steps = [v[0:2].reshape(2, 1, rows)]
        steps += [v[2 + 4 * k : 6 + 4 * k].reshape(2, 2, rows) for k in range(3)]
        steps += [v[14:16].reshape(2, 1, rows)]
        return [steps[0]] + [pick(odd, s, s[::-1]) for s in steps[1:]]

    def part(core):
        parts = []
        for y in range(NY):
            v = got[y, core]
            if y % 2:
                v = jnp.concatenate([v[0:2]] + [v[a:b] for k in range(3) for a, b in ((4 + 4 * k, 6 + 4 * k), (2 + 4 * k, 4 + 4 * k))] + [v[15:16], v[14:15]])
            parts.append(v)
        return in_order(combine(parts), 0)

    back, ahead = part(0), part(1)
    both = lambda k: jnp.concatenate([back[k], ahead[k]], axis=1)
    blocks = [both(0), ahead[1], ahead[2], ahead[3], both(4), back[3], back[2], back[1]]

    def wanted(by):
        at = lambda k: blocks[(by + k) % NZ]
        own = lambda v: pick(c, v[:, :1], v[:, 1:])
        out = [own(at(0))] + [pick(c, at(-k), at(k)) for k in range(1, 4)] + [own(at(4))]
        return jnp.concatenate([v.reshape(-1, rows) for v in out])

    lots = jnp.stack([wanted(d) for d in range(NZ)])
    lots = lax.dynamic_slice_in_dim(jnp.concatenate([lots, lots]), lax.rem(NZ - z, NZ), NZ, 0)
    got = lax.all_to_all(lots, "z", 0, 0, tiled=True)
    total = combine([got[i] for i in range(NZ)])
    other = swap_cores(total[:2])
    first, second = pick(c, total[:2], other), pick(c, other, total[:2])
    row_energy = jnp.stack([first, second], axis=1).reshape(-1)
    return jnp.concatenate([v.reshape(1, -1) for v in in_order(total, h)], axis=1), row_energy


def turned(column):
    n = column.shape[0]
    return jnp.transpose(jnp.broadcast_to(column, (n, n)))


def write_message(message, at, total, row):
    n, width = total.shape
    message[at : at + n, :] = total.astype(BF16)
    high = row.astype(BF16)
    tail = [high, (row - high.astype(F32)).astype(BF16)]
    if width > 2 * n:
        tail.append(jnp.zeros((TAIL, width - 2 * n), BF16))
    message[at + n : at + n + TAIL, :] = jnp.concatenate(tail, axis=1)


def read_message(message, at, n):
    total = message[at : at + n, :].astype(F32)
    tail = message[at + n : at + n + TAIL, :].astype(F32)
    return total, tail[:, :n] + tail[:, n : 2 * n]


def score_kernel(table, *refs):
    pieces, (logits, energy, high, total) = refs[:-4], refs[-4:]
    first = pl.program_id(0) == 0
    block = table[...]
    wide = block.astype(F32)
    squares = jnp.sum(wide * wide, axis=1, keepdims=True)
    at = 0
    for piece in pieces:
        span = slice(at, at + piece.shape[0])
        at += piece.shape[0]
        product = lax.dot_general(block, piece[...], (((1,), (1,)), ((), ())), preferred_element_type=F32)
        scores = 2.0 * product - squares
        logits[:, span] = scores
        top = jnp.max(scores, axis=0, keepdims=True)
        old = jnp.where(first, top, high[:, span])
        new = jnp.maximum(old, top)
        kept = jnp.where(first, 0.0, total[:, span]) * jnp.exp(old - new)
        added = kept + jnp.sum(jnp.exp(scores - new), axis=0, keepdims=True)
        high[:, span] = new
        total[:, span] = added
        energy[:, span] = new + jnp.log(added)


def score(table, pieces):
    (count, width), rows = table.shape, sum(p.shape[0] for p in pieces)
    tile = min(256, count)
    whole = lambda v: pl.BlockSpec(v.shape, lambda i: (0, 0))
    return pl.pallas_call(
        score_kernel,
        grid=(count // tile,),
        in_specs=[pl.BlockSpec((tile, width), lambda i: (i, 0))] + [whole(p) for p in pieces],
        out_specs=(pl.BlockSpec((tile, rows), lambda i: (i, 0)), pl.BlockSpec((1, rows), lambda i: (0, 0))),
        out_shape=(jax.ShapeDtypeStruct((count, rows), F32), jax.ShapeDtypeStruct((1, rows), F32)),
        scratch_shapes=[pltpu.VMEM((1, rows), F32), pltpu.VMEM((1, rows), F32)],
        compiler_params=pltpu.CompilerParams(vmem_limit_bytes=VMEM_LIMIT),
        cost_estimate=pl.CostEstimate(
            flops=4 * count * rows * width,
            bytes_accessed=4 * count * rows + 2 * (count + rows) * width,
            transcendentals=count * rows,
        ),
    )(table, *pieces)


def weigh_kernel(groups, sizes, energy, *refs):
    logits, slab = refs[: len(groups)], refs[len(groups) : len(groups) + len(sizes)]
    message, keep, keep_count = refs[len(groups) + len(sizes) :]
    n, width = keep.shape
    step = min(sizes)
    counts, sets, at = None, [], 0
    for p, size in enumerate(groups):
        w = jnp.exp(logits[p][...] - energy[:, at : at + size])
        at += size
        for cut in range(0, size, step):
            part = w[:, cut : cut + step]
            counts = part if counts is None else counts + part
            sets.append(part.astype(BF16))
    column = jnp.sum(counts, axis=1, keepdims=True)
    pairs = [jnp.concatenate(sets[p : p + 2], axis=1) for p in range(0, len(sets), 2)]
    tile = min(256, width)
    totals = []
    for at in range(0, width, tile):
        acc = None
        for p, pair in enumerate(pairs):
            if p < len(sizes) - 2:
                rows = slab[p][:, at : at + tile]
            else:
                rows = jnp.concatenate([slab[p][:, at : at + tile], slab[p + 1][:, at : at + tile]])
            term = jnp.dot(pair, rows, preferred_element_type=F32)
            acc = term if acc is None else acc + term
        keep[:, at : at + tile] = acc[:n]
        totals.append(acc[n:])
    keep_count[...] = turned(column[:n])[:TAIL]
    write_message(message, 0, jnp.concatenate(totals, axis=1), turned(column[n:])[:TAIL])


def weigh(first, count, logits, energy, slab):
    span, width = logits[0].shape[0] // NX, slab[0].shape[1]
    n = span // NC
    sizes = tuple(p.shape[0] for p in slab)
    block = lambda rows, cols: pl.BlockSpec((rows, cols), lambda i: (i, 0))
    whole = lambda v: pl.BlockSpec(v.shape, lambda i: (0, 0))
    return pl.pallas_call(
        functools.partial(weigh_kernel, tuple(v.shape[1] for v in logits), sizes),
        grid=(count,),
        in_specs=[whole(energy)]
        + [pl.BlockSpec((span, v.shape[1]), lambda i: (i + first, 0)) for v in logits]
        + [whole(p) for p in slab],
        out_specs=(block(n + TAIL, width), block(n, width), block(TAIL, n)),
        out_shape=(
            jax.ShapeDtypeStruct((count * (n + TAIL), width), BF16),
            jax.ShapeDtypeStruct((count * n, width), F32),
            jax.ShapeDtypeStruct((count * TAIL, n), F32),
        ),
        compiler_params=pltpu.CompilerParams(vmem_limit_bytes=VMEM_LIMIT),
        cost_estimate=pl.CostEstimate(
            flops=2 * count * span * sum(sizes) * width,
            bytes_accessed=4 * count * span * sum(sizes) + 2 * sum(sizes) * width,
            transcendentals=count * span * sum(sizes),
        ),
    )(energy, *logits, *slab)


def call(kernel, out_shape, *args):
    return pl.pallas_call(
        kernel,
        out_shape=out_shape,
        compiler_params=pltpu.CompilerParams(vmem_limit_bytes=VMEM_LIMIT),
    )(*args)


def add_kernel(n, got, keep, keep_count, *messages):
    for i, message in enumerate(messages):
        total, row = read_message(got, i * (n + TAIL), n)
        total = total + keep[i * n : (i + 1) * n, :]
        write_message(message, 0, total, row + keep_count[i * TAIL : (i + 1) * TAIL, :])


def add(got, keep, keep_count):
    n = keep_count.shape[1]
    shape = jax.ShapeDtypeStruct((n + TAIL, got.shape[1]), BF16)
    return call(functools.partial(add_kernel, n), (shape,) * (NX - 1), got, keep, keep_count)


def update_kernel(n, keep, keep_count, got, one, two, three, masses, centroids, new_centroids, new_masses):
    total, row = keep[...], keep_count[...]
    for message in (got, one, two, three):
        t, r = read_message(message, 0, n)
        total, row = total + t, row + r
    mass = masses[...]
    new = mass + row[:1]
    new_masses[...] = new
    column = lambda v: jnp.transpose(jnp.broadcast_to(v, (n, n)))[:, :1]
    new_centroids[...] = (column(mass) * centroids[...].astype(F32) + total) / column(new)


def update(keep, keep_count, got, others, masses, centroids):
    n, width = centroids.shape
    out = (jax.ShapeDtypeStruct((n, width), F32), jax.ShapeDtypeStruct((1, n), F32))
    return call(
        functools.partial(update_kernel, n), out, keep, keep_count, got, *others, masses.reshape(1, n), centroids
    )


def shards(embeddings, centroids, masses):
    z, y, c = (lax.axis_index(a) for a in ("z", "y", "c"))
    rows, width = embeddings.shape
    half, sub = rows // 2, rows // 4
    h = lax.rem(y, 2)

    mine = lax.dynamic_slice_in_dim(embeddings, h * half, half, 0)
    one = along_z(mine, 1)
    own = lax.dynamic_slice_in_dim(embeddings.reshape(2, 2, sub, width), c, 1, 1).reshape(half, width)
    two = along_z(one, 1)
    three = along_z(two, 1)
    four = along_z(lax.dynamic_slice_in_dim(three, c * sub, sub, 0), 1)

    held, _ = lax.optimization_barrier((centroids, one))
    near = {d: shift_x(held, -d) for d in (2, 1, 3)}
    near[0] = centroids
    mine = jnp.concatenate([near[d] for d in ORDER])
    other = swap_cores(mine)
    table = jnp.stack([mine.reshape(NX, -1, width), other.reshape(NX, -1, width)], axis=1).reshape(-1, width)

    in_vmem = lambda v: pltpu.with_memory_space_constraint(v, pltpu.VMEM) if PIN else v
    pieces = [own, one, swap_halves(one), two, swap_halves(two), three, swap_halves(three), four, swap_halves(four)]
    logits, local, at = [], [], 0
    for count in (3, 2, 1, 2, 1):
        scores, energy = score(table, pieces[at : at + count])
        at += count
        logits.append(in_vmem(scores))
        local.append(energy)
    energy, row_energy = energies(jnp.concatenate(local, axis=1).reshape(-1, sub), z, c, h)
    pieces = [in_vmem(p) for p in pieces]

    message, keep, keep_count = weigh(0, NX - 1, logits, energy, pieces)
    sent = add(swap_cores(message), keep, keep_count)
    message, keep, keep_count = weigh(NX - 1, 1, logits, energy, pieces)
    others = [shift_x(m, d) for m, d in zip(sent, ORDER)]
    new_centroids, new_masses = update(keep, keep_count, swap_cores(message), others, masses, centroids)
    return new_centroids, new_masses.reshape(-1), row_energy


def solution(mesh):
    grid = Mesh(mesh.devices.reshape(NX, NZ, NY, NC), ("x", "z", "y", "c"))
    rows, cents = ("x", "z"), ("y", "c", "x", "z")
    return jax.shard_map(
        shards,
        mesh=grid,
        in_specs=(P(rows, None), P(cents, None), P(cents)),
        out_specs=(P(cents, None), P(cents), P(rows)),
        check_vma=False,
    )
```

```python
import functools

import jax
import jax.numpy as jnp
from jax import lax
from jax.experimental import pallas as pl
from jax.experimental.pallas import tpu as pltpu
from jax.sharding import Mesh, PartitionSpec as P

NX, NZ, NY, NC = 4, 8, 4, 2
BF16, F32 = jnp.bfloat16, jnp.float32
TAIL = 16
ORDER = (2, 1, 3, 0)
VMEM_LIMIT = 30 * 1024 * 1024
PIN = True


def shift_x(value, by):
    return lax.ppermute(value, "x", [(i, (i + by) % NX) for i in range(NX)])


def swap_cores(value):
    return lax.ppermute(value, "c", [(0, 1), (1, 0)])


def along_z(value, by):
    pairs = []
    for z in range(NZ):
        pairs.append((z * NC, (z + by) % NZ * NC))
        pairs.append((z * NC + 1, (z - by) % NZ * NC + 1))
    return lax.ppermute(value, ("z", "c"), pairs)


def along_y(value, by):
    pairs = []
    for y in range(NY):
        pairs.append((y * NC, (y + by) % NY * NC))
        pairs.append((y * NC + 1, (y - by) % NY * NC + 1))
    return lax.ppermute(value, ("y", "c"), pairs)


def swap_halves(value):
    pairs = []
    for y in range(NY):
        pairs.append((y * NC, (y ^ 1) * NC))
        pairs.append((y * NC + 1, (y + 1 if y % 2 else y - 1) % NY * NC + 1))
    return lax.ppermute(value, ("y", "c"), pairs)


def pick(place, first, second):
    return jnp.where(place == 0, first, second)


def combine(parts):
    high = functools.reduce(jnp.maximum, parts)
    return high + jnp.log(sum(jnp.exp(p - high) for p in parts))


def energies(local, h, y, z, c):
    steps = [local[0]] + [pick(h, v, v[::-1]) for v in local[1:]]
    mine = jnp.concatenate([v.reshape(-1, v.shape[-1]) for v in steps])
    other = swap_cores(mine)

    def split(flat):
        out, at = [], 0
        for v in steps:
            n = v.shape[0] * v.shape[1]
            out.append(flat[at : at + n].reshape(v.shape))
            at += n
        return out

    back, ahead = split(pick(c, mine, other)), split(pick(c, other, mine))
    both = lambda k: jnp.concatenate([back[k], ahead[k]], axis=1)
    block = jnp.stack([both(0), ahead[1], ahead[2], ahead[3], both(4), back[3], back[2], back[1]])

    near = along_z(block, 1)
    near = pick(c, jnp.roll(near, -1, axis=0), jnp.roll(near, 1, axis=0))
    far = swap_cores(near)
    three = combine([block, near, far])
    got = along_z(pick(c, three, combine([block, far])), 3)
    got = pick(c, jnp.roll(got, -3, axis=0), jnp.roll(got, 3, axis=0))
    block = combine([three, got, swap_cores(got)])

    none = jnp.full_like(block, -1e30)
    parts = [pick(c, block, none), along_y(block, 1), pick(c, along_y(block, 2), none)]
    part = combine(parts)
    block = combine([part, swap_cores(part)])

    own = lambda v: pick(c, v[:, :1], v[:, 1:])
    out = [own(block[0])]
    for k in range(1, 4):
        v = pick(c, block[NZ - k], block[k])
        out.append(pick(h, v, v[::-1]))
    v = own(block[4])
    out.append(pick(h, v, v[::-1]))
    return jnp.concatenate([v.reshape(1, -1) for v in out], axis=1), block[0].reshape(-1)


def turned(column):
    n = column.shape[0]
    return jnp.transpose(jnp.broadcast_to(column, (n, n)))


def write_message(message, at, total, row):
    n, width = total.shape
    message[at : at + n, :] = total.astype(BF16)
    high = row.astype(BF16)
    tail = [high, (row - high.astype(F32)).astype(BF16)]
    if width > 2 * n:
        tail.append(jnp.zeros((TAIL, width - 2 * n), BF16))
    message[at + n : at + n + TAIL, :] = jnp.concatenate(tail, axis=1)


def read_message(message, at, n):
    total = message[at : at + n, :].astype(F32)
    tail = message[at + n : at + n + TAIL, :].astype(F32)
    return total, tail[:, :n] + tail[:, n : 2 * n]


def score_kernel(parts, sizes, *refs):
    table, pieces, (logits, energy) = refs[:parts], refs[parts:-2], refs[-2:]
    chunks = []
    for p in range(0, parts, NC):
        block = jnp.concatenate([table[p + i][...] for i in range(NC)])
        wide = block.astype(F32)
        chunks.append((block, jnp.sum(wide * wide, axis=1, keepdims=True)))
    span = chunks[0][0].shape[0]
    at = 0
    for piece, size in zip(pieces, sizes):
        rows, lot = piece[...], slice(at, at + size)
        at += size
        high = None
        for p, (block, squares) in enumerate(chunks):
            product = lax.dot_general(block, rows, (((1,), (1,)), ((), ())), preferred_element_type=F32)
            scores = 2.0 * product - squares
            logits[p * span : (p + 1) * span, lot] = scores
            top = jnp.max(scores, axis=0, keepdims=True)
            high = top if high is None else jnp.maximum(high, top)
        total = None
        for p in range(len(chunks)):
            part = jnp.sum(jnp.exp(logits[p * span : (p + 1) * span, lot] - high), axis=0, keepdims=True)
            total = part if total is None else total + part
        energy[:, lot] = high + jnp.log(total)


def score(table, pieces):
    count, width = sum(t.shape[0] for t in table), table[0].shape[1]
    sizes = tuple(p.shape[0] for p in pieces)
    rows = sum(sizes)
    return pl.pallas_call(
        functools.partial(score_kernel, len(table), sizes),
        out_shape=(
            pltpu.HBM((count, rows), F32) if PIN else jax.ShapeDtypeStruct((count, rows), F32),
            jax.ShapeDtypeStruct((1, rows), F32),
        ),
        compiler_params=pltpu.CompilerParams(vmem_limit_bytes=VMEM_LIMIT),
        cost_estimate=pl.CostEstimate(
            flops=4 * count * rows * width,
            bytes_accessed=4 * count * rows + 2 * (count + rows) * width,
            transcendentals=count * rows,
        ),
    )(*table, *pieces)


def weigh_kernel(groups, sizes, energy, *refs):
    logits, slab = refs[: len(groups)], refs[len(groups) : len(groups) + len(sizes)]
    message, keep, keep_count = refs[len(groups) + len(sizes) :]
    n, width = keep.shape
    step = min(sizes)
    counts, sets, at = None, [], 0
    for p, size in enumerate(groups):
        w = jnp.exp(logits[p][...] - energy[:, at : at + size])
        at += size
        for cut in range(0, size, step):
            part = w[:, cut : cut + step]
            counts = part if counts is None else counts + part
            sets.append(part.astype(BF16))
    column = jnp.sum(counts, axis=1, keepdims=True)
    pairs = [jnp.concatenate(sets[p : p + 2], axis=1) for p in range(0, len(sets), 2)]
    tile = min(256, width)
    totals = []
    for at in range(0, width, tile):
        acc = None
        for p, pair in enumerate(pairs):
            if p < len(sizes) - 2:
                rows = slab[p][:, at : at + tile]
            else:
                rows = jnp.concatenate([slab[p][:, at : at + tile], slab[p + 1][:, at : at + tile]])
            term = jnp.dot(pair, rows, preferred_element_type=F32)
            acc = term if acc is None else acc + term
        keep[:, at : at + tile] = acc[:n]
        totals.append(acc[n:])
    keep_count[...] = turned(column[:n])[:TAIL]
    write_message(message, 0, jnp.concatenate(totals, axis=1), turned(column[n:])[:TAIL])


def weigh(first, count, logits, energy, slab):
    span, width = logits[0].shape[0] // NX, slab[0].shape[1]
    n = span // NC
    sizes = tuple(p.shape[0] for p in slab)
    block = lambda rows, cols: pl.BlockSpec((rows, cols), lambda i: (i, 0))
    whole = lambda v: pl.BlockSpec(v.shape, lambda i: (0, 0))
    return pl.pallas_call(
        functools.partial(weigh_kernel, tuple(v.shape[1] for v in logits), sizes),
        grid=(count,),
        in_specs=[whole(energy)]
        + [pl.BlockSpec((span, v.shape[1]), lambda i: (i + first, 0)) for v in logits]
        + [whole(p) for p in slab],
        out_specs=(block(n + TAIL, width), block(n, width), block(TAIL, n)),
        out_shape=(
            jax.ShapeDtypeStruct((count * (n + TAIL), width), BF16),
            jax.ShapeDtypeStruct((count * n, width), F32),
            jax.ShapeDtypeStruct((count * TAIL, n), F32),
        ),
        compiler_params=pltpu.CompilerParams(vmem_limit_bytes=VMEM_LIMIT),
        cost_estimate=pl.CostEstimate(
            flops=2 * count * span * sum(sizes) * width,
            bytes_accessed=4 * count * span * sum(sizes) + 2 * sum(sizes) * width,
            transcendentals=count * span * sum(sizes),
        ),
    )(energy, *logits, *slab)


def call(kernel, out_shape, *args):
    return pl.pallas_call(
        kernel,
        out_shape=out_shape,
        compiler_params=pltpu.CompilerParams(vmem_limit_bytes=VMEM_LIMIT),
    )(*args)


def add_kernel(n, got, keep, keep_count, *messages):
    for i, message in enumerate(messages):
        total, row = read_message(got, i * (n + TAIL), n)
        total = total + keep[i * n : (i + 1) * n, :]
        write_message(message, 0, total, row + keep_count[i * TAIL : (i + 1) * TAIL, :])


def add(got, keep, keep_count):
    n = keep_count.shape[1]
    shape = jax.ShapeDtypeStruct((n + TAIL, got.shape[1]), BF16)
    return call(functools.partial(add_kernel, n), (shape,) * (NX - 1), got, keep, keep_count)


def update_kernel(n, keep, keep_count, got, one, two, three, masses, centroids, new_centroids, new_masses):
    total, row = keep[...], keep_count[...]
    for message in (got, one, two, three):
        t, r = read_message(message, 0, n)
        total, row = total + t, row + r
    mass = masses[...]
    new = mass + row[:1]
    new_masses[...] = new
    column = lambda v: jnp.transpose(jnp.broadcast_to(v, (n, n)))[:, :1]
    new_centroids[...] = (column(mass) * centroids[...].astype(F32) + total) / column(new)


def update(keep, keep_count, got, others, masses, centroids):
    n, width = centroids.shape
    out = (jax.ShapeDtypeStruct((n, width), F32), jax.ShapeDtypeStruct((1, n), F32))
    return call(
        functools.partial(update_kernel, n), out, keep, keep_count, got, *others, masses.reshape(1, n), centroids
    )


def shards(embeddings, centroids, masses):
    z, y, c = (lax.axis_index(a) for a in ("z", "y", "c"))
    rows, width = embeddings.shape
    half, sub = rows // 2, rows // 4
    h = lax.rem(y, 2)

    near = {d: shift_x(centroids, -d) for d in (2, 1, 3)}

    mine = lax.dynamic_slice_in_dim(embeddings, h * half, half, 0)
    one = along_z(mine, 1)
    own = lax.dynamic_slice_in_dim(embeddings.reshape(2, 2, sub, width), c, 1, 1).reshape(half, width)
    two = along_z(one, 1)
    three = along_z(two, 1)

    late = lax.optimization_barrier([near[1], near[2], near[3], two])
    near = {0: centroids, 1: late[0], 2: late[1], 3: late[2]}
    table = [v for d in ORDER for v in (near[d], swap_cores(near[d]))]

    fixed = lambda v: pltpu.with_memory_space_constraint(v, pltpu.HBM) if PIN else v
    logits, local, pieces = [], [], []

    def scored(*rows):
        scores, energy = score(table, rows)
        logits.append(fixed(scores))
        local.append(energy)
        pieces.extend(rows)
        return energy

    done = scored(own, one, swap_halves(one))
    last, _ = lax.optimization_barrier((lax.dynamic_slice_in_dim(three, c * sub, sub, 0), done))
    four = along_z(last, 1)
    done = scored(two, swap_halves(two))
    last, _ = lax.optimization_barrier((four, done))
    scored(three)
    scored(swap_halves(three), four)
    scored(swap_halves(last))

    local = jnp.concatenate(local, axis=1).reshape(-1, sub)
    cut = lambda at, n, *shape: local[at : at + n].reshape(*shape, sub)
    steps = [cut(0, 2, 2, 1)] + [cut(2 + 4 * k, 4, 2, 2) for k in range(3)] + [cut(14, 2, 2, 1)]
    energy, row_energy = energies(steps, h, y, z, c)
    pieces = [fixed(p) for p in pieces]

    message, keep, keep_count = weigh(0, NX - 1, logits, energy, pieces)
    sent = add(swap_cores(message), keep, keep_count)
    message, keep, keep_count = weigh(NX - 1, 1, logits, energy, pieces)
    others = [shift_x(m, d) for m, d in zip(sent, ORDER)]
    new_centroids, new_masses = update(keep, keep_count, swap_cores(message), others, masses, centroids)
    return new_centroids, new_masses.reshape(-1), row_energy


def solution(mesh):
    grid = Mesh(mesh.devices.reshape(NX, NZ, NY, NC), ("x", "z", "y", "c"))
    rows, cents = ("x", "z"), ("y", "c", "x", "z")
    return jax.shard_map(
        shards,
        mesh=grid,
        in_specs=(P(rows, None), P(cents, None), P(cents)),
        out_specs=(P(cents, None), P(cents), P(rows)),
        check_vma=False,
    )
```

```python
import functools

import jax
import jax.numpy as jnp
from jax import lax
from jax.experimental import pallas as pl
from jax.experimental.pallas import tpu as pltpu
from jax.sharding import Mesh, PartitionSpec as P

NX, NZ, NY, NC = 4, 8, 4, 2
BF16, F32 = jnp.bfloat16, jnp.float32
TAIL = 16
ORDER = (2, 1, 3, 0)
VMEM_LIMIT = 30 * 1024 * 1024
PIN = True


def shift_x(value, by):
    return lax.ppermute(value, "x", [(i, (i + by) % NX) for i in range(NX)])


def swap_cores(value):
    return lax.ppermute(value, "c", [(0, 1), (1, 0)])


def along_z(value, by):
    pairs = []
    for z in range(NZ):
        pairs.append((z * NC, (z + by) % NZ * NC))
        pairs.append((z * NC + 1, (z - by) % NZ * NC + 1))
    return lax.ppermute(value, ("z", "c"), pairs)


def along_y(value, by):
    pairs = []
    for y in range(NY):
        pairs.append((y * NC, (y + by) % NY * NC))
        pairs.append((y * NC + 1, (y - by) % NY * NC + 1))
    return lax.ppermute(value, ("y", "c"), pairs)


def swap_halves(value):
    pairs = []
    for y in range(NY):
        pairs.append((y * NC, (y ^ 1) * NC))
        pairs.append((y * NC + 1, (y + 1 if y % 2 else y - 1) % NY * NC + 1))
    return lax.ppermute(value, ("y", "c"), pairs)


def pick(place, first, second):
    return jnp.where(place == 0, first, second)


def combine(parts):
    high = functools.reduce(jnp.maximum, parts)
    return high + jnp.log(sum(jnp.exp(p - high) for p in parts))


def energies(local, h, y, z, c):
    steps = [local[0]] + [pick(h, v, v[::-1]) for v in local[1:]]
    mine = jnp.concatenate([v.reshape(-1, v.shape[-1]) for v in steps])
    other = swap_cores(mine)

    def split(flat):
        out, at = [], 0
        for v in steps:
            n = v.shape[0] * v.shape[1]
            out.append(flat[at : at + n].reshape(v.shape))
            at += n
        return out

    back, ahead = split(pick(c, mine, other)), split(pick(c, other, mine))
    both = lambda k: jnp.concatenate([back[k], ahead[k]], axis=1)
    block = jnp.stack([both(0), ahead[1], ahead[2], ahead[3], both(4), back[3], back[2], back[1]])

    near = along_z(block, 1)
    near = pick(c, jnp.roll(near, -1, axis=0), jnp.roll(near, 1, axis=0))
    far = swap_cores(near)
    three = combine([block, near, far])
    got = along_z(pick(c, three, combine([block, far])), 3)
    got = pick(c, jnp.roll(got, -3, axis=0), jnp.roll(got, 3, axis=0))
    block = combine([three, got, swap_cores(got)])

    none = jnp.full_like(block, -1e30)
    parts = [pick(c, block, none), along_y(block, 1), pick(c, along_y(block, 2), none)]
    part = combine(parts)
    block = combine([part, swap_cores(part)])

    own = lambda v: pick(c, v[:, :1], v[:, 1:])
    out = [own(block[0])]
    for k in range(1, 4):
        v = pick(c, block[NZ - k], block[k])
        out.append(pick(h, v, v[::-1]))
    v = own(block[4])
    out.append(pick(h, v, v[::-1]))
    return jnp.concatenate([v.reshape(1, -1) for v in out], axis=1), block[0].reshape(-1)


def turned(column):
    n = column.shape[0]
    return jnp.transpose(jnp.broadcast_to(column, (n, n)))


def write_message(message, at, total, row):
    n, width = total.shape
    message[at : at + n, :] = total.astype(BF16)
    high = row.astype(BF16)
    tail = [high, (row - high.astype(F32)).astype(BF16)]
    if width > 2 * n:
        tail.append(jnp.zeros((TAIL, width - 2 * n), BF16))
    message[at + n : at + n + TAIL, :] = jnp.concatenate(tail, axis=1)


def read_message(message, at, n):
    total = message[at : at + n, :].astype(F32)
    tail = message[at + n : at + n + TAIL, :].astype(F32)
    return total, tail[:, :n] + tail[:, n : 2 * n]


def score_kernel(parts, sizes, given, *refs):
    table, refs = refs[:parts], refs[parts:]
    pieces, refs = refs[: len(sizes)], refs[len(sizes) :]
    squares, logits, energy = refs
    n = table[0].shape[0]
    span = n * NC
    blocks = [jnp.concatenate([table[p + i][...] for i in range(NC)]) for p in range(0, parts, NC)]
    if not given:
        for p, block in enumerate(blocks):
            wide = block.astype(F32)
            total = jnp.sum(wide * wide, axis=1, keepdims=True)
            squares[p * span : (p + 1) * span, :] = jnp.broadcast_to(total, (span, squares.shape[1]))
    at = 0
    for piece, size in zip(pieces, sizes):
        rows, lot = piece[...], slice(at, at + size)
        at += size
        high = None
        for p, block in enumerate(blocks):
            product = lax.dot_general(block, rows, (((1,), (1,)), ((), ())), preferred_element_type=F32)
            scores = 2.0 * product - squares[p * span : (p + 1) * span, :1]
            logits[p * span : (p + 1) * span, lot] = scores
            top = jnp.max(scores, axis=0, keepdims=True)
            high = top if high is None else jnp.maximum(high, top)
        total = None
        for p in range(len(blocks)):
            part = jnp.sum(jnp.exp(logits[p * span : (p + 1) * span, lot] - high), axis=0, keepdims=True)
            total = part if total is None else total + part
        energy[:, lot] = high + jnp.log(total)


def score(table, pieces, squares=None):
    count, width = sum(t.shape[0] for t in table), table[0].shape[1]
    sizes = tuple(p.shape[0] for p in pieces)
    rows, given = sum(sizes), squares is not None
    out = [
        pltpu.HBM((count, rows), F32) if PIN else jax.ShapeDtypeStruct((count, rows), F32),
        jax.ShapeDtypeStruct((1, rows), F32),
    ]
    if not given:
        out.insert(0, jax.ShapeDtypeStruct((count, 128), F32))
    got = pl.pallas_call(
        functools.partial(score_kernel, len(table), sizes, given),
        out_shape=out,
        compiler_params=pltpu.CompilerParams(vmem_limit_bytes=VMEM_LIMIT),
        cost_estimate=pl.CostEstimate(
            flops=4 * count * rows * width,
            bytes_accessed=4 * count * rows + 2 * (count + rows) * width,
            transcendentals=count * rows,
        ),
    )(*table, *pieces, *([squares] if given else []))
    return (squares, *got) if given else got


def weigh_kernel(first, groups, sizes, energy, *refs):
    logits, refs = refs[: len(groups)], refs[len(groups) :]
    slab, refs = refs[: len(sizes)], refs[len(sizes) :]
    message, keep, keep_count, scores, rows, sums, counts, sems = refs
    height, width = sums.shape
    n = keep_count.shape[1]
    span = n * NC
    starts = [sum(sizes[:p]) for p in range(len(sizes))]
    edges = [sum(groups[:g]) for g in range(len(groups))]
    copies = []
    for p, (at, size) in enumerate(zip(starts, sizes)):
        g = max(i for i, edge in enumerate(edges) if edge <= at)
        part = logits[g].at[first * span : first * span + height, at - edges[g] : at - edges[g] + size]
        pair = (
            pltpu.make_async_copy(part, scores.at[:, at : at + size], sems.at[0, p]),
            pltpu.make_async_copy(slab[p], rows.at[at : at + size, :], sems.at[1, p]),
        )
        for copy in pair:
            copy.start()
        copies.append(pair)
    tile = min(256, width)
    for step in range(0, len(sizes) - 1, 2):
        last = step + 3 >= len(sizes)
        stop = len(sizes) if last else step + 2
        for p in range(step, stop):
            for copy in copies[p]:
                copy.wait()
        at, end = starts[step], starts[stop - 1] + sizes[stop - 1]
        for lot in range(0, height, span):
            block = slice(lot, lot + span)
            w = jnp.exp(scores[block, at:end] - energy[:, at:end])
            part = functools.reduce(jnp.add, [w[:, k : k + 128] for k in range(0, end - at, 128)])
            counts[block, :] = part if step == 0 else counts[block, :] + part
            w = w.astype(BF16)
            for col in range(0, width, tile):
                term = jnp.dot(w, rows[at:end, col : col + tile], preferred_element_type=F32)
                sums[block, col : col + tile] = term if step == 0 else sums[block, col : col + tile] + term
        if last:
            break
    for i in range(height // span):
        column = jnp.sum(counts[i * span : (i + 1) * span, :], axis=1, keepdims=True)
        keep[i * n : (i + 1) * n, :] = sums[i * span : i * span + n, :]
        keep_count[i * TAIL : (i + 1) * TAIL, :] = turned(column[:n])[:TAIL]
        write_message(message, i * (n + TAIL), sums[i * span + n : (i + 1) * span, :], turned(column[n:])[:TAIL])


def weigh(first, count, logits, energy, slab):
    span, width = logits[0].shape[0] // NX, slab[0].shape[1]
    n = span // NC
    sizes, groups = tuple(p.shape[0] for p in slab), tuple(v.shape[1] for v in logits)
    total, height = sum(sizes), count * span
    away = pl.BlockSpec(memory_space=pl.ANY)
    return pl.pallas_call(
        functools.partial(weigh_kernel, first, groups, sizes),
        in_specs=[pl.BlockSpec(memory_space=pltpu.VMEM)] + [away] * (len(groups) + len(sizes)),
        out_shape=(
            jax.ShapeDtypeStruct((count * (n + TAIL), width), BF16),
            jax.ShapeDtypeStruct((count * n, width), F32),
            jax.ShapeDtypeStruct((count * TAIL, n), F32),
        ),
        scratch_shapes=[
            pltpu.VMEM((height, total), F32),
            pltpu.VMEM((total, width), BF16),
            pltpu.VMEM((height, width), F32),
            pltpu.VMEM((height, 128), F32),
            pltpu.SemaphoreType.DMA((2, len(sizes))),
        ],
        compiler_params=pltpu.CompilerParams(vmem_limit_bytes=VMEM_LIMIT),
        cost_estimate=pl.CostEstimate(
            flops=2 * height * total * width,
            bytes_accessed=4 * height * total + 2 * total * width,
            transcendentals=height * total,
        ),
    )(energy, *logits, *slab)


def call(kernel, out_shape, *args):
    return pl.pallas_call(
        kernel,
        out_shape=out_shape,
        compiler_params=pltpu.CompilerParams(vmem_limit_bytes=VMEM_LIMIT),
    )(*args)


def add_kernel(n, got, keep, keep_count, *messages):
    for i, message in enumerate(messages):
        total, row = read_message(got, i * (n + TAIL), n)
        total = total + keep[i * n : (i + 1) * n, :]
        write_message(message, 0, total, row + keep_count[i * TAIL : (i + 1) * TAIL, :])


def add(got, keep, keep_count):
    n = keep_count.shape[1]
    shape = jax.ShapeDtypeStruct((n + TAIL, got.shape[1]), BF16)
    return call(functools.partial(add_kernel, n), (shape,) * (NX - 1), got, keep, keep_count)


def update_kernel(n, keep, keep_count, got, one, two, three, masses, centroids, new_centroids, new_masses):
    total, row = keep[...], keep_count[...]
    for message in (got, one, two, three):
        t, r = read_message(message, 0, n)
        total, row = total + t, row + r
    mass = masses[...]
    new = mass + row[:1]
    new_masses[...] = new
    column = lambda v: jnp.transpose(jnp.broadcast_to(v, (n, n)))[:, :1]
    new_centroids[...] = (column(mass) * centroids[...].astype(F32) + total) / column(new)


def update(keep, keep_count, got, others, masses, centroids):
    n, width = centroids.shape
    out = (jax.ShapeDtypeStruct((n, width), F32), jax.ShapeDtypeStruct((1, n), F32))
    return call(
        functools.partial(update_kernel, n), out, keep, keep_count, got, *others, masses.reshape(1, n), centroids
    )


def shards(embeddings, centroids, masses):
    z, y, c = (lax.axis_index(a) for a in ("z", "y", "c"))
    rows, width = embeddings.shape
    half, sub = rows // 2, rows // 4
    h = lax.rem(y, 2)

    near = {0: centroids, 1: shift_x(centroids, -1), 3: shift_x(centroids, 1)}

    mine = lax.dynamic_slice_in_dim(embeddings, h * half, half, 0)
    one = along_z(mine, 1)
    own = lax.dynamic_slice_in_dim(embeddings.reshape(2, 2, sub, width), c, 1, 1).reshape(half, width)
    one, near[1], near[3] = lax.optimization_barrier((one, near[1], near[3]))
    two = along_z(one, 1)
    near[2] = shift_x(near[1], -1)
    first = swap_halves(one)
    two, near[2], first = lax.optimization_barrier((two, near[2], first))
    three = along_z(two, 1)

    table = [v for d in ORDER for v in (near[d], swap_cores(near[d]))]

    fixed = lambda v: pltpu.with_memory_space_constraint(v, pltpu.HBM) if PIN else v
    four = along_z(lax.dynamic_slice_in_dim(three, c * sub, sub, 0), 1)
    lots = [(own, one, first, two, swap_halves(two))]
    squares, scores, energy = score(table, lots[0])
    logits, local = [scores], [energy]
    last, _ = lax.optimization_barrier((four, energy))
    last = swap_halves(last)
    lots.append((three, swap_halves(three), four))
    _, scores, energy = score(table, lots[1], squares)
    last, _ = lax.optimization_barrier((last, energy))
    logits.append(scores)
    local.append(energy)
    lots.append((last,))
    _, scores, energy = score(table, lots[2], squares)
    logits.append(scores)
    local.append(energy)
    logits, pieces = [fixed(v) for v in logits], [fixed(v) for lot in lots for v in lot]

    local = jnp.concatenate(local, axis=1).reshape(-1, sub)
    cut = lambda at, n, *shape: local[at : at + n].reshape(*shape, sub)
    steps = [cut(0, 2, 2, 1)] + [cut(2 + 4 * k, 4, 2, 2) for k in range(3)] + [cut(14, 2, 2, 1)]
    energy, row_energy = energies(steps, h, y, z, c)
    pieces = [fixed(p) for p in pieces]

    message, keep, keep_count = weigh(0, NX - 1, logits, energy, pieces)
    sent = add(swap_cores(message), keep, keep_count)
    message, keep, keep_count = weigh(NX - 1, 1, logits, energy, pieces)
    others = [shift_x(m, d) for m, d in zip(sent, ORDER)]
    new_centroids, new_masses = update(keep, keep_count, swap_cores(message), others, masses, centroids)
    return new_centroids, new_masses.reshape(-1), row_energy


def solution(mesh):
    grid = Mesh(mesh.devices.reshape(NX, NZ, NY, NC), ("x", "z", "y", "c"))
    rows, cents = ("x", "z"), ("y", "c", "x", "z")
    return jax.shard_map(
        shards,
        mesh=grid,
        in_specs=(P(rows, None), P(cents, None), P(cents)),
        out_specs=(P(cents, None), P(cents), P(rows)),
        check_vma=False,
    )
```

```python
import functools

import jax
import jax.numpy as jnp
from jax import lax
from jax.experimental import pallas as pl
from jax.experimental.pallas import tpu as pltpu
from jax.sharding import Mesh, PartitionSpec as P

NX, NZ, NY, NC = 4, 8, 4, 2
BF16, F32 = jnp.bfloat16, jnp.float32
TAIL = 16
ORDER = (2, 1, 3, 0)
VMEM_LIMIT = 30 * 1024 * 1024
PIN = True


def shift_x(value, by):
    return lax.ppermute(value, "x", [(i, (i + by) % NX) for i in range(NX)])


def swap_cores(value):
    return lax.ppermute(value, "c", [(0, 1), (1, 0)])


def along_z(value, by):
    pairs = []
    for z in range(NZ):
        pairs.append((z * NC, (z + by) % NZ * NC))
        pairs.append((z * NC + 1, (z - by) % NZ * NC + 1))
    return lax.ppermute(value, ("z", "c"), pairs)


def along_y(value, by):
    pairs = []
    for y in range(NY):
        pairs.append((y * NC, (y + by) % NY * NC))
        pairs.append((y * NC + 1, (y - by) % NY * NC + 1))
    return lax.ppermute(value, ("y", "c"), pairs)


def swap_halves(value):
    pairs = []
    for y in range(NY):
        pairs.append((y * NC, (y ^ 1) * NC))
        pairs.append((y * NC + 1, (y + 1 if y % 2 else y - 1) % NY * NC + 1))
    return lax.ppermute(value, ("y", "c"), pairs)


def pick(place, first, second):
    return jnp.where(place == 0, first, second)


def combine(parts):
    high = functools.reduce(jnp.maximum, parts)
    return high + jnp.log(sum(jnp.exp(p - high) for p in parts))


def energies(local, h, y, z, c):
    steps = [local[0]] + [pick(h, v, v[::-1]) for v in local[1:]]
    mine = jnp.concatenate([v.reshape(-1, v.shape[-1]) for v in steps])
    other = swap_cores(mine)

    def split(flat):
        out, at = [], 0
        for v in steps:
            n = v.shape[0] * v.shape[1]
            out.append(flat[at : at + n].reshape(v.shape))
            at += n
        return out

    back, ahead = split(pick(c, mine, other)), split(pick(c, other, mine))
    both = lambda k: jnp.concatenate([back[k], ahead[k]], axis=1)
    block = jnp.stack([both(0), ahead[1], ahead[2], ahead[3], both(4), back[3], back[2], back[1]])

    near = along_z(block, 1)
    near = pick(c, jnp.roll(near, -1, axis=0), jnp.roll(near, 1, axis=0))
    far = swap_cores(near)
    three = combine([block, near, far])
    got = along_z(pick(c, three, combine([block, far])), 3)
    got = pick(c, jnp.roll(got, -3, axis=0), jnp.roll(got, 3, axis=0))
    block = combine([three, got, swap_cores(got)])

    none = jnp.full_like(block, -1e30)
    parts = [pick(c, block, none), along_y(block, 1), pick(c, along_y(block, 2), none)]
    part = combine(parts)
    block = combine([part, swap_cores(part)])

    own = lambda v: pick(c, v[:, :1], v[:, 1:])
    out = [own(block[0])]
    for k in range(1, 4):
        v = pick(c, block[NZ - k], block[k])
        out.append(pick(h, v, v[::-1]))
    v = own(block[4])
    out.append(pick(h, v, v[::-1]))
    return jnp.concatenate([v.reshape(1, -1) for v in out], axis=1), block[0].reshape(-1)


def turned(column):
    n = column.shape[0]
    return jnp.transpose(jnp.broadcast_to(column, (n, n)))


def write_message(message, at, total, row):
    n, width = total.shape
    message[at : at + n, :] = total.astype(BF16)
    high = row.astype(BF16)
    tail = [high, (row - high.astype(F32)).astype(BF16)]
    if width > 2 * n:
        tail.append(jnp.zeros((TAIL, width - 2 * n), BF16))
    message[at + n : at + n + TAIL, :] = jnp.concatenate(tail, axis=1)


def read_message(message, at, n):
    total = message[at : at + n, :].astype(F32)
    tail = message[at + n : at + n + TAIL, :].astype(F32)
    return total, tail[:, :n] + tail[:, n : 2 * n]


def score_kernel(parts, sizes, given, *refs):
    table, refs = refs[:parts], refs[parts:]
    pieces, refs = refs[: len(sizes)], refs[len(sizes) :]
    if given:
        known, logits, energy, block, squares, rows, scores, sems = refs
    else:
        squares, logits, energy, block, rows, scores, sems = refs
    n = table[0].shape[0]
    starts = [sum(sizes[:p]) for p in range(len(sizes))]
    loads = [pltpu.make_async_copy(t, block.at[p * n : (p + 1) * n, :], sems.at[p]) for p, t in enumerate(table)]
    if given:
        loads.append(pltpu.make_async_copy(known, squares, sems.at[parts]))
    arrivals = [
        pltpu.make_async_copy(piece, rows.at[at : at + size, :], sems.at[parts + 1 + p])
        for p, (piece, at, size) in enumerate(zip(pieces, starts, sizes))
    ]
    for copy in loads + arrivals:
        copy.start()
    for copy in loads:
        copy.wait()
    span = n * NC
    height = parts * n
    if not given:
        for at in range(0, height, span):
            wide = block[at : at + span, :].astype(F32)
            total = jnp.sum(wide * wide, axis=1, keepdims=True)
            squares[at : at + span, :] = jnp.broadcast_to(total, (span, squares.shape[1]))
    leaving = []
    for p, (at, size) in enumerate(zip(starts, sizes)):
        arrivals[p].wait()
        lot = slice(at, at + size)
        high = None
        for k in range(0, height, span):
            product = lax.dot_general(
                block[k : k + span, :], rows[lot, :], (((1,), (1,)), ((), ())), preferred_element_type=F32
            )
            part = 2.0 * product - squares[k : k + span, :1]
            scores[k : k + span, lot] = part
            top = jnp.max(part, axis=0, keepdims=True)
            high = top if high is None else jnp.maximum(high, top)
        copy = pltpu.make_async_copy(scores.at[:, lot], logits.at[:, lot], sems.at[parts + 1 + len(sizes) + p])
        copy.start()
        leaving.append(copy)
        total = None
        for k in range(0, height, span):
            part = jnp.sum(jnp.exp(scores[k : k + span, lot] - high), axis=0, keepdims=True)
            total = part if total is None else total + part
        energy[:, lot] = high + jnp.log(total)
    for copy in leaving:
        copy.wait()


def score(table, pieces, squares=None):
    count, width = sum(t.shape[0] for t in table), table[0].shape[1]
    sizes = tuple(p.shape[0] for p in pieces)
    rows, given = sum(sizes), squares is not None
    away, near = pl.BlockSpec(memory_space=pl.ANY), pl.BlockSpec(memory_space=pltpu.VMEM)
    out = [
        pltpu.HBM((count, rows), F32) if PIN else jax.ShapeDtypeStruct((count, rows), F32),
        jax.ShapeDtypeStruct((1, rows), F32),
    ]
    if not given:
        out.insert(0, jax.ShapeDtypeStruct((count, 128), F32))
    got = pl.pallas_call(
        functools.partial(score_kernel, len(table), sizes, given),
        in_specs=[away] * (len(table) + len(sizes) + given),
        out_specs=[away, near] if given else [near, away, near],
        out_shape=out,
        scratch_shapes=[pltpu.VMEM((count, width), BF16)]
        + [pltpu.VMEM((count, 128), F32)] * given
        + [
            pltpu.VMEM((rows, width), BF16),
            pltpu.VMEM((count, rows), F32),
            pltpu.SemaphoreType.DMA((len(table) + 1 + 2 * len(sizes),)),
        ],
        compiler_params=pltpu.CompilerParams(vmem_limit_bytes=VMEM_LIMIT),
        cost_estimate=pl.CostEstimate(
            flops=4 * count * rows * width,
            bytes_accessed=4 * count * rows + 2 * (count + rows) * width,
            transcendentals=count * rows,
        ),
    )(*table, *pieces, *([squares] if given else []))
    return (squares, *got) if given else got


def weigh_kernel(first, groups, sizes, energy, *refs):
    logits, refs = refs[: len(groups)], refs[len(groups) :]
    slab, refs = refs[: len(sizes)], refs[len(sizes) :]
    message, keep, keep_count, scores, rows, sums, counts, sems = refs
    height, width = sums.shape
    n = keep_count.shape[1]
    span = n * NC
    starts = [sum(sizes[:p]) for p in range(len(sizes))]
    edges = [sum(groups[:g]) for g in range(len(groups))]
    copies = []
    for p, (at, size) in enumerate(zip(starts, sizes)):
        g = max(i for i, edge in enumerate(edges) if edge <= at)
        part = logits[g].at[first * span : first * span + height, at - edges[g] : at - edges[g] + size]
        pair = (
            pltpu.make_async_copy(part, scores.at[:, at : at + size], sems.at[0, p]),
            pltpu.make_async_copy(slab[p], rows.at[at : at + size, :], sems.at[1, p]),
        )
        for copy in pair:
            copy.start()
        copies.append(pair)
    tile = min(256, width)
    for step in range(0, len(sizes) - 1, 2):
        last = step + 3 >= len(sizes)
        stop = len(sizes) if last else step + 2
        for p in range(step, stop):
            for copy in copies[p]:
                copy.wait()
        at, end = starts[step], starts[stop - 1] + sizes[stop - 1]
        for lot in range(0, height, span):
            block = slice(lot, lot + span)
            w = jnp.exp(scores[block, at:end] - energy[:, at:end])
            part = functools.reduce(jnp.add, [w[:, k : k + 128] for k in range(0, end - at, 128)])
            counts[block, :] = part if step == 0 else counts[block, :] + part
            w = w.astype(BF16)
            for col in range(0, width, tile):
                term = jnp.dot(w, rows[at:end, col : col + tile], preferred_element_type=F32)
                sums[block, col : col + tile] = term if step == 0 else sums[block, col : col + tile] + term
        if last:
            break
    for i in range(height // span):
        column = jnp.sum(counts[i * span : (i + 1) * span, :], axis=1, keepdims=True)
        keep[i * n : (i + 1) * n, :] = sums[i * span : i * span + n, :]
        keep_count[i * TAIL : (i + 1) * TAIL, :] = turned(column[:n])[:TAIL]
        write_message(message, i * (n + TAIL), sums[i * span + n : (i + 1) * span, :], turned(column[n:])[:TAIL])


def weigh(first, count, logits, energy, slab):
    span, width = logits[0].shape[0] // NX, slab[0].shape[1]
    n = span // NC
    sizes, groups = tuple(p.shape[0] for p in slab), tuple(v.shape[1] for v in logits)
    total, height = sum(sizes), count * span
    away = pl.BlockSpec(memory_space=pl.ANY)
    return pl.pallas_call(
        functools.partial(weigh_kernel, first, groups, sizes),
        in_specs=[pl.BlockSpec(memory_space=pltpu.VMEM)] + [away] * (len(groups) + len(sizes)),
        out_shape=(
            jax.ShapeDtypeStruct((count * (n + TAIL), width), BF16),
            jax.ShapeDtypeStruct((count * n, width), F32),
            jax.ShapeDtypeStruct((count * TAIL, n), F32),
        ),
        scratch_shapes=[
            pltpu.VMEM((height, total), F32),
            pltpu.VMEM((total, width), BF16),
            pltpu.VMEM((height, width), F32),
            pltpu.VMEM((height, 128), F32),
            pltpu.SemaphoreType.DMA((2, len(sizes))),
        ],
        compiler_params=pltpu.CompilerParams(vmem_limit_bytes=VMEM_LIMIT),
        cost_estimate=pl.CostEstimate(
            flops=2 * height * total * width,
            bytes_accessed=4 * height * total + 2 * total * width,
            transcendentals=height * total,
        ),
    )(energy, *logits, *slab)


def call(kernel, out_shape, *args):
    return pl.pallas_call(
        kernel,
        out_shape=out_shape,
        compiler_params=pltpu.CompilerParams(vmem_limit_bytes=VMEM_LIMIT),
    )(*args)


def add_kernel(n, got, keep, keep_count, *messages):
    for i, message in enumerate(messages):
        total, row = read_message(got, i * (n + TAIL), n)
        total = total + keep[i * n : (i + 1) * n, :]
        write_message(message, 0, total, row + keep_count[i * TAIL : (i + 1) * TAIL, :])


def add(got, keep, keep_count):
    n = keep_count.shape[1]
    shape = jax.ShapeDtypeStruct((n + TAIL, got.shape[1]), BF16)
    return call(functools.partial(add_kernel, n), (shape,) * (NX - 1), got, keep, keep_count)


def update_kernel(n, keep, keep_count, got, one, two, three, masses, centroids, new_centroids, new_masses):
    total, row = keep[...], keep_count[...]
    for message in (got, one, two, three):
        t, r = read_message(message, 0, n)
        total, row = total + t, row + r
    mass = masses[...]
    new = mass + row[:1]
    new_masses[...] = new
    column = lambda v: jnp.transpose(jnp.broadcast_to(v, (n, n)))[:, :1]
    new_centroids[...] = (column(mass) * centroids[...].astype(F32) + total) / column(new)


def update(keep, keep_count, got, others, masses, centroids):
    n, width = centroids.shape
    out = (jax.ShapeDtypeStruct((n, width), F32), jax.ShapeDtypeStruct((1, n), F32))
    return call(
        functools.partial(update_kernel, n), out, keep, keep_count, got, *others, masses.reshape(1, n), centroids
    )


def shards(embeddings, centroids, masses):
    z, y, c = (lax.axis_index(a) for a in ("z", "y", "c"))
    rows, width = embeddings.shape
    half, sub = rows // 2, rows // 4
    h = lax.rem(y, 2)

    near = {0: centroids, 1: shift_x(centroids, -1), 3: shift_x(centroids, 1)}

    mine = lax.dynamic_slice_in_dim(embeddings, h * half, half, 0)
    one = along_z(mine, 1)
    own = lax.dynamic_slice_in_dim(embeddings.reshape(2, 2, sub, width), c, 1, 1).reshape(half, width)
    one, near[1], near[3] = lax.optimization_barrier((one, near[1], near[3]))
    two = along_z(one, 1)
    near[2] = shift_x(near[1], -1)
    first = swap_halves(one)
    two, near[2], first = lax.optimization_barrier((two, near[2], first))
    three = along_z(two, 1)

    fixed = lambda v: pltpu.with_memory_space_constraint(v, pltpu.HBM) if PIN else v
    table = [fixed(v) for d in ORDER for v in (near[d], swap_cores(near[d]))]

    four = along_z(lax.dynamic_slice_in_dim(three, c * sub, sub, 0), 1)
    lots = [(own, one, first, two, swap_halves(two))]
    squares, scores, energy = score(table, [fixed(v) for v in lots[0]])
    squares = fixed(squares)
    logits, local = [scores], [energy]
    last, _ = lax.optimization_barrier((four, energy))
    last = swap_halves(last)
    lots.append((three, swap_halves(three), four))
    _, scores, energy = score(table, [fixed(v) for v in lots[1]], squares)
    last, _ = lax.optimization_barrier((last, energy))
    logits.append(scores)
    local.append(energy)
    lots.append((last,))
    _, scores, energy = score(table, [fixed(v) for v in lots[2]], squares)
    logits.append(scores)
    local.append(energy)
    logits, pieces = [fixed(v) for v in logits], [fixed(v) for lot in lots for v in lot]

    local = jnp.concatenate(local, axis=1).reshape(-1, sub)
    cut = lambda at, n, *shape: local[at : at + n].reshape(*shape, sub)
    steps = [cut(0, 2, 2, 1)] + [cut(2 + 4 * k, 4, 2, 2) for k in range(3)] + [cut(14, 2, 2, 1)]
    energy, row_energy = energies(steps, h, y, z, c)
    pieces = [fixed(p) for p in pieces]

    message, keep, keep_count = weigh(0, NX - 1, logits, energy, pieces)
    sent = add(swap_cores(message), keep, keep_count)
    message, keep, keep_count = weigh(NX - 1, 1, logits, energy, pieces)
    others = [shift_x(m, d) for m, d in zip(sent, ORDER)]
    new_centroids, new_masses = update(keep, keep_count, swap_cores(message), others, masses, centroids)
    return new_centroids, new_masses.reshape(-1), row_energy


def solution(mesh):
    grid = Mesh(mesh.devices.reshape(NX, NZ, NY, NC), ("x", "z", "y", "c"))
    rows, cents = ("x", "z"), ("y", "c", "x", "z")
    return jax.shard_map(
        shards,
        mesh=grid,
        in_specs=(P(rows, None), P(cents, None), P(cents)),
        out_specs=(P(cents, None), P(cents), P(rows)),
        check_vma=False,
    )
```

```python
import functools

import jax
import jax.numpy as jnp
from jax import lax
from jax.experimental import pallas as pl
from jax.experimental.pallas import tpu as pltpu
from jax.sharding import Mesh, PartitionSpec as P

NX, NZ, NY, NC = 4, 8, 4, 2
BF16, F32 = jnp.bfloat16, jnp.float32
TAIL = 16
ORDER = (2, 1, 3, 0)
VMEM_LIMIT = 20 * 1024 * 1024
SMALL_LIMIT = 4 * 1024 * 1024
PIN = True


def shift_x(value, by):
    return lax.ppermute(value, "x", [(i, (i + by) % NX) for i in range(NX)])


def swap_cores(value):
    return lax.ppermute(value, "c", [(0, 1), (1, 0)])


def along_z(value, by):
    pairs = []
    for z in range(NZ):
        pairs.append((z * NC, (z + by) % NZ * NC))
        pairs.append((z * NC + 1, (z - by) % NZ * NC + 1))
    return lax.ppermute(value, ("z", "c"), pairs)


def along_y(value, by):
    pairs = []
    for y in range(NY):
        pairs.append((y * NC, (y + by) % NY * NC))
        pairs.append((y * NC + 1, (y - by) % NY * NC + 1))
    return lax.ppermute(value, ("y", "c"), pairs)


def swap_halves(value):
    pairs = []
    for y in range(NY):
        pairs.append((y * NC, (y ^ 1) * NC))
        pairs.append((y * NC + 1, (y + 1 if y % 2 else y - 1) % NY * NC + 1))
    return lax.ppermute(value, ("y", "c"), pairs)


def combine(parts):
    high = functools.reduce(jnp.maximum, parts)
    return high + jnp.log(sum(jnp.exp(p - high) for p in parts))


def pick(place, first, second):
    return jnp.where(place == 0, first, second)


def small(kernel, place, out, *args):
    return pl.pallas_call(
        kernel,
        in_specs=[pl.BlockSpec(memory_space=pltpu.SMEM)] + [pl.BlockSpec(memory_space=pltpu.VMEM)] * len(args),
        out_shape=[jax.ShapeDtypeStruct(shape, F32) for shape in out],
        compiler_params=pltpu.CompilerParams(vmem_limit_bytes=SMALL_LIMIT),
    )(place, *args)


def turn(v, by):
    by %= NZ
    return jnp.concatenate([v[:, NZ - by :], v[:, : NZ - by]], axis=1)


def pack_kernel(place, first, second, third, out):
    sub = out.shape[1]
    given = [v[:, k : k + sub] for v in (first, second, third) for k in range(0, v.shape[1], sub)]
    h = place[1]
    out[0:1, :] = given[0]
    out[1:2, :] = given[1]
    at = 2
    for mine, other in ((given[2:4], given[4:6]), (given[6:8], given[8:10]), (given[10:12], given[12:14]), (given[14:15], given[15:16])):
        for v, w in ((mine, other), (other, mine)):
            for i in range(len(v)):
                out[at : at + 1, :] = pick(h, v[i], w[i])
                at += 1


def block_kernel(place, mine, other, out):
    c = place[0]
    back = lambda i: pick(c, mine[i : i + 1, :], other[i : i + 1, :])
    ahead = lambda i: pick(c, other[i : i + 1, :], mine[i : i + 1, :])
    for half in range(2):
        for sub in range(2):
            q = 2 * half + sub
            side = ahead if sub else back
            out[q, 0:1, :] = side(half)
            out[q, 4:5, :] = side(14 + half)
            for k in range(1, 4):
                out[q, k : k + 1, :] = ahead(4 * k - 2 + q)
                out[q, NZ - k : NZ - k + 1, :] = back(4 * k - 2 + q)


def near_kernel(place, block, near, far, three, message):
    c = place[0]
    own = block[...]
    from_back = turn(pick(c, near[...], far[...]), -1)
    from_ahead = turn(pick(c, far[...], near[...]), 1)
    both = combine([own, from_back, from_ahead])
    three[...] = both
    message[...] = pick(c, both, combine([own, from_back]))


def far_kernel(place, three, got, other, out):
    c = place[0]
    from_back = turn(pick(c, got[...], other[...]), -3)
    from_ahead = turn(pick(c, other[...], got[...]), 3)
    out[...] = combine([three[...], from_back, from_ahead])


def side_kernel(place, block, one, two, out):
    out[...] = pick(place[0], combine([block[...], one[...], two[...]]), one[...])


def last_kernel(place, part, other, energy, own):
    c, h = place[0], place[1]
    block = combine([part[...], other[...]])
    n = block.shape[2]
    own[...] = block[:, 0]

    def steps(half, step):
        return [pick(c, block[2 * half + i, NZ - step : NZ - step + 1], block[2 * half + i, step : step + 1]) for i in range(2)]

    out = [pick(c, block[2 * half, 0:1], block[2 * half + 1, 0:1]) for half in range(2)]
    for step in range(1, 4):
        low, top = steps(0, step), steps(1, step)
        out += [pick(h, low[i], top[i]) for i in range(2)] + [pick(h, top[i], low[i]) for i in range(2)]
    low, top = (pick(c, block[2 * half, 4:5], block[2 * half + 1, 4:5]) for half in range(2))
    out += [pick(h, low, top), pick(h, top, low)]
    for i, v in enumerate(out):
        energy[:, i * n : (i + 1) * n] = v


def energies(local, place, sub):
    (mine,) = small(pack_kernel, place, [(16, sub)], *local)
    shape = (4, NZ, sub)
    (block,) = small(block_kernel, place, [shape], mine, swap_cores(mine))
    near = along_z(block, 1)
    three, message = small(near_kernel, place, [shape] * 2, block, near, swap_cores(near))
    got = along_z(message, 3)
    (block,) = small(far_kernel, place, [shape], three, got, swap_cores(got))
    (part,) = small(side_kernel, place, [shape], block, along_y(block, 1), along_y(block, 2))
    energy, own = small(last_kernel, place, [(1, 16 * sub), (4, sub)], part, swap_cores(part))
    return energy, own.reshape(-1)


def turned(column):
    n = column.shape[0]
    return jnp.transpose(jnp.broadcast_to(column, (n, n)))


def write_message(message, at, total, row):
    n, width = total.shape
    message[at : at + n, :] = total.astype(BF16)
    high = row.astype(BF16)
    tail = [high, (row - high.astype(F32)).astype(BF16)]
    if width > 2 * n:
        tail.append(jnp.zeros((TAIL, width - 2 * n), BF16))
    message[at + n : at + n + TAIL, :] = jnp.concatenate(tail, axis=1)


def read_message(message, at, n):
    total = message[at : at + n, :].astype(F32)
    tail = message[at + n : at + n + TAIL, :].astype(F32)
    return total, tail[:, :n] + tail[:, n : 2 * n]


def score_kernel(parts, sizes, given, *refs):
    table, refs = refs[:parts], refs[parts:]
    pieces, refs = refs[: len(sizes)], refs[len(sizes) :]
    squares, logits, energy = refs
    n = table[0].shape[0]
    span = n * NC
    blocks = [jnp.concatenate([table[p + i][...] for i in range(NC)]) for p in range(0, parts, NC)]
    if not given:
        for p, block in enumerate(blocks):
            wide = block.astype(F32)
            total = jnp.sum(wide * wide, axis=1, keepdims=True)
            squares[p * span : (p + 1) * span, :] = jnp.broadcast_to(total, (span, squares.shape[1]))
    at = 0
    for piece, size in zip(pieces, sizes):
        rows, lot = piece[...], slice(at, at + size)
        at += size
        high = None
        for p, block in enumerate(blocks):
            product = lax.dot_general(block, rows, (((1,), (1,)), ((), ())), preferred_element_type=F32)
            scores = 2.0 * product - squares[p * span : (p + 1) * span, :1]
            logits[p * span : (p + 1) * span, lot] = scores
            top = jnp.max(scores, axis=0, keepdims=True)
            high = top if high is None else jnp.maximum(high, top)
        total = None
        for p in range(len(blocks)):
            part = jnp.sum(jnp.exp(logits[p * span : (p + 1) * span, lot] - high), axis=0, keepdims=True)
            total = part if total is None else total + part
        energy[:, lot] = high + jnp.log(total)


def score(table, pieces, squares=None):
    count, width = sum(t.shape[0] for t in table), table[0].shape[1]
    sizes = tuple(p.shape[0] for p in pieces)
    rows, given = sum(sizes), squares is not None
    out = [
        pltpu.VMEM((count, rows), F32) if PIN else jax.ShapeDtypeStruct((count, rows), F32),
        jax.ShapeDtypeStruct((1, rows), F32),
    ]
    if not given:
        out.insert(0, jax.ShapeDtypeStruct((count, 128), F32))
    got = pl.pallas_call(
        functools.partial(score_kernel, len(table), sizes, given),
        out_shape=out,
        compiler_params=pltpu.CompilerParams(vmem_limit_bytes=VMEM_LIMIT),
        cost_estimate=pl.CostEstimate(
            flops=4 * count * rows * width,
            bytes_accessed=4 * count * rows + 2 * (count + rows) * width,
            transcendentals=count * rows,
        ),
    )(*table, *pieces, *([squares] if given else []))
    return (squares, *got) if given else got


def weigh_kernel(first, groups, sizes, energy, *refs):
    logits, refs = refs[: len(groups)], refs[len(groups) :]
    slab, (message, keep, keep_count) = refs[: len(sizes)], refs[len(sizes) :]
    n, width = keep_count.shape[1], keep.shape[1]
    span, step = n * NC, min(sizes)
    tile = min(256, width)
    for i in range(keep.shape[0] // n):
        lot = slice((first + i) * span, (first + i + 1) * span)
        counts, sets, at = None, [], 0
        for p, size in enumerate(groups):
            for cut in range(0, size, step):
                w = jnp.exp(logits[p][lot, cut : cut + step] - energy[:, at + cut : at + cut + step])
                counts = w if counts is None else counts + w
                sets.append(w.astype(BF16))
            at += size
        column = jnp.sum(counts, axis=1, keepdims=True)
        pairs = [jnp.concatenate(sets[p : p + 2], axis=1) for p in range(0, len(sets), 2)]
        totals = []
        for at in range(0, width, tile):
            acc = None
            for p, pair in enumerate(pairs):
                rows = slab[p][:, at : at + tile]
                if rows.shape[0] < pair.shape[1]:
                    rows = jnp.concatenate([rows, slab[p + 1][:, at : at + tile]])
                term = jnp.dot(pair, rows, preferred_element_type=F32)
                acc = term if acc is None else acc + term
            keep[i * n : (i + 1) * n, at : at + tile] = acc[:n]
            totals.append(acc[n:])
        keep_count[i * TAIL : (i + 1) * TAIL, :] = turned(column[:n])[:TAIL]
        write_message(message, i * (n + TAIL), jnp.concatenate(totals, axis=1), turned(column[n:])[:TAIL])


def weigh(first, count, logits, energy, slab):
    span, width = logits[0].shape[0] // NX, slab[0].shape[1]
    n = span // NC
    sizes, groups = tuple(p.shape[0] for p in slab), tuple(v.shape[1] for v in logits)
    total, height = sum(sizes), count * span
    return pl.pallas_call(
        functools.partial(weigh_kernel, first, groups, sizes),
        out_shape=(
            jax.ShapeDtypeStruct((count * (n + TAIL), width), BF16),
            jax.ShapeDtypeStruct((count * n, width), F32),
            jax.ShapeDtypeStruct((count * TAIL, n), F32),
        ),
        compiler_params=pltpu.CompilerParams(vmem_limit_bytes=VMEM_LIMIT),
        cost_estimate=pl.CostEstimate(
            flops=2 * height * total * width,
            bytes_accessed=4 * height * total + 2 * total * width,
            transcendentals=height * total,
        ),
    )(energy, *logits, *slab)


def call(kernel, out_shape, *args):
    return pl.pallas_call(
        kernel,
        out_shape=out_shape,
        compiler_params=pltpu.CompilerParams(vmem_limit_bytes=VMEM_LIMIT),
    )(*args)


def add_kernel(n, got, keep, keep_count, *messages):
    for i, message in enumerate(messages):
        total, row = read_message(got, i * (n + TAIL), n)
        total = total + keep[i * n : (i + 1) * n, :]
        write_message(message, 0, total, row + keep_count[i * TAIL : (i + 1) * TAIL, :])


def add(got, keep, keep_count):
    n = keep_count.shape[1]
    shape = jax.ShapeDtypeStruct((n + TAIL, got.shape[1]), BF16)
    return call(functools.partial(add_kernel, n), (shape,) * (NX - 1), got, keep, keep_count)


def update_kernel(n, keep, keep_count, got, one, two, three, masses, centroids, new_centroids, new_masses):
    total, row = keep[...], keep_count[...]
    for message in (got, one, two, three):
        t, r = read_message(message, 0, n)
        total, row = total + t, row + r
    mass = masses[...]
    new = mass + row[:1]
    new_masses[...] = new
    column = lambda v: jnp.transpose(jnp.broadcast_to(v, (n, n)))[:, :1]
    new_centroids[...] = (column(mass) * centroids[...].astype(F32) + total) / column(new)


def update(keep, keep_count, got, others, masses, centroids):
    n, width = centroids.shape
    out = (jax.ShapeDtypeStruct((n, width), F32), jax.ShapeDtypeStruct((1, n), F32))
    return call(
        functools.partial(update_kernel, n), out, keep, keep_count, got, *others, masses.reshape(1, n), centroids
    )


def shards(embeddings, centroids, masses):
    y, c = lax.axis_index("y"), lax.axis_index("c")
    rows, width = embeddings.shape
    half, sub = rows // 2, rows // 4
    h = lax.rem(y, 2)
    place, embeddings = lax.optimization_barrier((jnp.stack([c, h]), embeddings))

    near = {0: centroids, 1: shift_x(centroids, -1), 3: shift_x(centroids, 1)}

    mine = lax.dynamic_slice_in_dim(embeddings, h * half, half, 0)
    one = along_z(mine, 1)
    own = lax.dynamic_slice_in_dim(embeddings.reshape(2, 2, sub, width), c, 1, 1).reshape(half, width)
    one, near[1], near[3] = lax.optimization_barrier((one, near[1], near[3]))
    two = along_z(one, 1)
    near[2] = shift_x(near[1], -1)
    first = swap_halves(one)
    two, near[2], first = lax.optimization_barrier((two, near[2], first))
    three = along_z(two, 1)

    fixed = lambda v: pltpu.with_memory_space_constraint(v, pltpu.VMEM) if PIN else v
    table = [fixed(v) for d in ORDER for v in (near[d], swap_cores(near[d]))]

    four = along_z(lax.dynamic_slice_in_dim(three, c * sub, sub, 0), 1)
    lots = [[fixed(v) for v in (own, one, first, two, swap_halves(two))]]
    squares, scores, energy = score(table, lots[0])
    squares, logits, local = fixed(squares), [scores], [energy]
    last, _ = lax.optimization_barrier((four, energy))
    last = swap_halves(last)
    lots.append([fixed(v) for v in (three, swap_halves(three), four)])
    _, scores, energy = score(table, lots[1], squares)
    last, _ = lax.optimization_barrier((last, energy))
    logits.append(scores)
    local.append(energy)
    lots.append([fixed(last)])
    _, scores, energy = score(table, lots[2], squares)
    logits.append(scores)
    local.append(energy)
    energy, row_energy = energies(local, place, sub)
    logits, pieces = [fixed(v) for v in logits], [v for lot in lots for v in lot]

    message, keep, keep_count = weigh(0, NX - 1, logits, energy, pieces)
    sent = add(swap_cores(message), keep, keep_count)
    message, keep, keep_count = weigh(NX - 1, 1, logits, energy, pieces)
    others = [shift_x(m, d) for m, d in zip(sent, ORDER)]
    new_centroids, new_masses = update(keep, keep_count, swap_cores(message), others, masses, centroids)
    return new_centroids, new_masses.reshape(-1), row_energy


def solution(mesh):
    grid = Mesh(mesh.devices.reshape(NX, NZ, NY, NC), ("x", "z", "y", "c"))
    rows, cents = ("x", "z"), ("y", "c", "x", "z")
    return jax.shard_map(
        shards,
        mesh=grid,
        in_specs=(P(rows, None), P(cents, None), P(cents)),
        out_specs=(P(cents, None), P(cents), P(rows)),
        check_vma=False,
    )
```

```python
import functools

import jax
import jax.numpy as jnp
from jax import lax
from jax.experimental import pallas as pl
from jax.experimental.pallas import tpu as pltpu
from jax.sharding import Mesh, PartitionSpec as P

NX, NZ, NY, NC = 4, 8, 4, 2
BF16, F32 = jnp.bfloat16, jnp.float32
TAIL = 16
ORDER = (2, 1, 3, 0)
BATCH = 512
VMEM_LIMIT = 20 * 1024 * 1024
SMALL_LIMIT = 4 * 1024 * 1024
PIN = True


def shift_x(value, by):
    return lax.ppermute(value, "x", [(i, (i + by) % NX) for i in range(NX)])


def swap_cores(value):
    return lax.ppermute(value, "c", [(0, 1), (1, 0)])


def along_z(value, by):
    pairs = []
    for z in range(NZ):
        pairs.append((z * NC, (z + by) % NZ * NC))
        pairs.append((z * NC + 1, (z - by) % NZ * NC + 1))
    return lax.ppermute(value, ("z", "c"), pairs)


def along_y(value, by):
    pairs = []
    for y in range(NY):
        pairs.append((y * NC, (y + by) % NY * NC))
        pairs.append((y * NC + 1, (y - by) % NY * NC + 1))
    return lax.ppermute(value, ("y", "c"), pairs)


def swap_halves(value):
    pairs = []
    for y in range(NY):
        pairs.append((y * NC, (y ^ 1) * NC))
        pairs.append((y * NC + 1, (y + 1 if y % 2 else y - 1) % NY * NC + 1))
    return lax.ppermute(value, ("y", "c"), pairs)


def combine(parts):
    high = functools.reduce(jnp.maximum, parts)
    return high + jnp.log(sum(jnp.exp(p - high) for p in parts))


def pick(place, first, second):
    return jnp.where(place == 0, first, second)


def small(kernel, place, out, *args):
    return pl.pallas_call(
        kernel,
        out_shape=[jax.ShapeDtypeStruct(shape, F32) for shape in out],
        compiler_params=pltpu.CompilerParams(vmem_limit_bytes=SMALL_LIMIT),
    )(place, *args)


def turn(v, by):
    by %= NZ
    return jnp.concatenate([v[:, NZ - by :], v[:, : NZ - by]], axis=1)


def pack_kernel(place, first, second, third, out):
    sub = out.shape[1]
    given = [v[:, k : k + sub] for v in (first, second, third) for k in range(0, v.shape[1], sub)]
    h = place[4:5, :]
    out[0:1, :] = given[0]
    out[1:2, :] = given[1]
    at = 2
    for mine, other in ((given[2:4], given[4:6]), (given[6:8], given[8:10]), (given[10:12], given[12:14]), (given[14:15], given[15:16])):
        for v, w in ((mine, other), (other, mine)):
            for i in range(len(v)):
                out[at : at + 1, :] = pick(h, v[i], w[i])
                at += 1


def block_kernel(place, mine, other, out):
    c = place[0:1, :]
    back = lambda i: pick(c, mine[i : i + 1, :], other[i : i + 1, :])
    ahead = lambda i: pick(c, other[i : i + 1, :], mine[i : i + 1, :])
    for half in range(2):
        for sub in range(2):
            q = 2 * half + sub
            side = ahead if sub else back
            out[q, 0:1, :] = side(half)
            out[q, 4:5, :] = side(14 + half)
            for k in range(1, 4):
                out[q, k : k + 1, :] = ahead(4 * k - 2 + q)
                out[q, NZ - k : NZ - k + 1, :] = back(4 * k - 2 + q)


def near_kernel(place, block, near, far, three, message):
    c = place[0:1, :]
    own = block[...]
    from_back = turn(pick(c, near[...], far[...]), -1)
    from_ahead = turn(pick(c, far[...], near[...]), 1)
    both = combine([own, from_back, from_ahead])
    three[...] = both
    message[...] = pick(c, both, combine([own, from_back]))


def far_kernel(place, three, got, other, out):
    c = place[0:1, :]
    from_back = turn(pick(c, got[...], other[...]), -3)
    from_ahead = turn(pick(c, other[...], got[...]), 3)
    out[...] = combine([three[...], from_back, from_ahead])


def side_kernel(place, block, one, two, out):
    out[...] = pick(place[0:1, :], combine([block[...], one[...], two[...]]), one[...])


def last_kernel(place, part, other, energy, own):
    c, h = place[0:1, :], place[4:5, :]
    block = combine([part[...], other[...]])
    n = block.shape[2]
    own[...] = block[:, 0]

    def steps(half, step):
        return [pick(c, block[2 * half + i, NZ - step : NZ - step + 1], block[2 * half + i, step : step + 1]) for i in range(2)]

    out = [pick(c, block[2 * half, 0:1], block[2 * half + 1, 0:1]) for half in range(2)]
    for step in range(1, 4):
        low, top = steps(0, step), steps(1, step)
        out += [pick(h, low[i], top[i]) for i in range(2)] + [pick(h, top[i], low[i]) for i in range(2)]
    low, top = (pick(c, block[2 * half, 4:5], block[2 * half + 1, 4:5]) for half in range(2))
    out += [pick(h, low, top), pick(h, top, low)]
    for i, v in enumerate(out):
        energy[:, i * n : (i + 1) * n] = v


def energies(local, place, sub):
    (mine,) = small(pack_kernel, place, [(16, sub)], *local)
    shape = (4, NZ, sub)
    (block,) = small(block_kernel, place, [shape], mine, swap_cores(mine))
    near = along_z(block, 1)
    three, message = small(near_kernel, place, [shape] * 2, block, near, swap_cores(near))
    got = along_z(message, 3)
    (block,) = small(far_kernel, place, [shape], three, got, swap_cores(got))
    (part,) = small(side_kernel, place, [shape], block, along_y(block, 1), along_y(block, 2))
    energy, own = small(last_kernel, place, [(1, 16 * sub), (4, sub)], part, swap_cores(part))
    return energy, own.reshape(-1)


def turned(column):
    n = column.shape[0]
    return jnp.transpose(jnp.broadcast_to(column, (n, n)))


def write_message(message, at, total, row):
    n, width = total.shape
    message[at : at + n, :] = total.astype(BF16)
    high = row.astype(BF16)
    tail = [high, (row - high.astype(F32)).astype(BF16)]
    if width > 2 * n:
        tail.append(jnp.zeros((TAIL, width - 2 * n), BF16))
    message[at + n : at + n + TAIL, :] = jnp.concatenate(tail, axis=1)


def read_message(message, at, n):
    total = message[at : at + n, :].astype(F32)
    tail = message[at + n : at + n + TAIL, :].astype(F32)
    return total, tail[:, :n] + tail[:, n : 2 * n]


def score_kernel(parts, sizes, given, *refs):
    table, refs = refs[:parts], refs[parts:]
    pieces, refs = refs[: len(sizes)], refs[len(sizes) :]
    squares, logits, energy = refs
    n = table[0].shape[0]
    span = n * NC
    blocks = [jnp.concatenate([table[p + i][...] for i in range(NC)]) for p in range(0, parts, NC)]
    if not given:
        for p, block in enumerate(blocks):
            wide = block.astype(F32)
            total = jnp.sum(wide * wide, axis=1, keepdims=True)
            squares[p * span : (p + 1) * span, :] = jnp.broadcast_to(total, (span, squares.shape[1]))
    batches, at = [[]], 0
    for piece, size in zip(pieces, sizes):
        if sum(k for _, k in batches[-1]) >= BATCH:
            batches.append([])
        batches[-1].append((piece, size))
    for batch in batches:
        rows = jnp.concatenate([piece[...] for piece, _ in batch])
        lot = slice(at, at + rows.shape[0])
        at += rows.shape[0]
        high = None
        for p, block in enumerate(blocks):
            product = lax.dot_general(block, rows, (((1,), (1,)), ((), ())), preferred_element_type=F32)
            scores = 2.0 * product - squares[p * span : (p + 1) * span, :1]
            logits[p * span : (p + 1) * span, lot] = scores
            top = jnp.max(scores, axis=0, keepdims=True)
            high = top if high is None else jnp.maximum(high, top)
        total = None
        for p in range(len(blocks)):
            part = jnp.sum(jnp.exp(logits[p * span : (p + 1) * span, lot] - high), axis=0, keepdims=True)
            total = part if total is None else total + part
        energy[:, lot] = high + jnp.log(total)


def score(table, pieces, squares=None):
    count, width = sum(t.shape[0] for t in table), table[0].shape[1]
    sizes = tuple(p.shape[0] for p in pieces)
    rows, given = sum(sizes), squares is not None
    out = [
        pltpu.VMEM((count, rows), F32) if PIN else jax.ShapeDtypeStruct((count, rows), F32),
        jax.ShapeDtypeStruct((1, rows), F32),
    ]
    if not given:
        out.insert(0, jax.ShapeDtypeStruct((count, 128), F32))
    got = pl.pallas_call(
        functools.partial(score_kernel, len(table), sizes, given),
        out_shape=out,
        compiler_params=pltpu.CompilerParams(vmem_limit_bytes=VMEM_LIMIT),
        cost_estimate=pl.CostEstimate(
            flops=4 * count * rows * width,
            bytes_accessed=4 * count * rows + 2 * (count + rows) * width,
            transcendentals=count * rows,
        ),
    )(*table, *pieces, *([squares] if given else []))
    return (squares, *got) if given else got


def weigh_kernel(first, groups, sizes, energy, *refs):
    logits, refs = refs[: len(groups)], refs[len(groups) :]
    slab, (message, keep, keep_count) = refs[: len(sizes)], refs[len(sizes) :]
    n, width = keep_count.shape[1], keep.shape[1]
    span, step = n * NC, min(sizes)
    tile = min(256, width)
    for i in range(keep.shape[0] // n):
        lot = slice((first + i) * span, (first + i + 1) * span)
        counts, sets, at = None, [], 0
        for p, size in enumerate(groups):
            for cut in range(0, size, step):
                w = jnp.exp(logits[p][lot, cut : cut + step] - energy[:, at + cut : at + cut + step])
                counts = w if counts is None else counts + w
                sets.append(w.astype(BF16))
            at += size
        column = jnp.sum(counts, axis=1, keepdims=True)
        pairs = [jnp.concatenate(sets[p : p + 2], axis=1) for p in range(0, len(sets), 2)]
        totals = []
        for at in range(0, width, tile):
            acc = None
            for p, pair in enumerate(pairs):
                rows = slab[p][:, at : at + tile]
                if rows.shape[0] < pair.shape[1]:
                    rows = jnp.concatenate([rows, slab[p + 1][:, at : at + tile]])
                term = jnp.dot(pair, rows, preferred_element_type=F32)
                acc = term if acc is None else acc + term
            keep[i * n : (i + 1) * n, at : at + tile] = acc[:n]
            totals.append(acc[n:])
        keep_count[i * TAIL : (i + 1) * TAIL, :] = turned(column[:n])[:TAIL]
        write_message(message, i * (n + TAIL), jnp.concatenate(totals, axis=1), turned(column[n:])[:TAIL])


def weigh(first, count, logits, energy, slab):
    span, width = logits[0].shape[0] // NX, slab[0].shape[1]
    n = span // NC
    sizes, groups = tuple(p.shape[0] for p in slab), tuple(v.shape[1] for v in logits)
    total, height = sum(sizes), count * span
    return pl.pallas_call(
        functools.partial(weigh_kernel, first, groups, sizes),
        out_shape=(
            jax.ShapeDtypeStruct((count * (n + TAIL), width), BF16),
            jax.ShapeDtypeStruct((count * n, width), F32),
            jax.ShapeDtypeStruct((count * TAIL, n), F32),
        ),
        compiler_params=pltpu.CompilerParams(vmem_limit_bytes=VMEM_LIMIT),
        cost_estimate=pl.CostEstimate(
            flops=2 * height * total * width,
            bytes_accessed=4 * height * total + 2 * total * width,
            transcendentals=height * total,
        ),
    )(energy, *logits, *slab)


def call(kernel, out_shape, *args):
    return pl.pallas_call(
        kernel,
        out_shape=out_shape,
        compiler_params=pltpu.CompilerParams(vmem_limit_bytes=VMEM_LIMIT),
    )(*args)


def add_kernel(n, got, keep, keep_count, *out):
    messages, counts = out[: len(out) // 2], out[len(out) // 2 :]
    for i, (message, count) in enumerate(zip(messages, counts)):
        total, row = read_message(got, i * (n + TAIL), n)
        message[...] = (total + keep[i * n : (i + 1) * n, :]).astype(BF16)
        count[...] = (row + keep_count[i * TAIL : (i + 1) * TAIL, :])[:8]


def add(got, keep, keep_count):
    n = keep_count.shape[1]
    k = keep.shape[0] // n
    shapes = [jax.ShapeDtypeStruct((n, keep.shape[1]), BF16)] * k + [jax.ShapeDtypeStruct((8, n), F32)] * k
    out = call(functools.partial(add_kernel, n), shapes, got, keep, keep_count)
    return out[:k], out[k:]


def update_kernel(n, keep, keep_count, got, masses, centroids, *refs):
    others, (new_centroids, new_masses) = refs[:-2], refs[-2:]
    total, row = read_message(got, 0, n)
    total, row = total + keep[...], (row + keep_count[...])[:1]
    for message, count in zip(others[: NX - 1], others[NX - 1 :]):
        total, row = total + message[...].astype(F32), row + count[:1, :]
    mass = masses[...]
    new = mass + row
    new_masses[...] = new
    column = lambda v: jnp.transpose(jnp.broadcast_to(v, (n, n)))[:, :1]
    new_centroids[...] = (column(mass) * centroids[...].astype(F32) + total) / column(new)


def update(keep, keep_count, got, others, masses, centroids):
    n, width = centroids.shape
    out = (jax.ShapeDtypeStruct((n, width), F32), jax.ShapeDtypeStruct((1, n), F32))
    return call(
        functools.partial(update_kernel, n), out, keep, keep_count, got, masses.reshape(1, n), centroids, *others
    )


def shards(embeddings, centroids, masses):
    y, c = lax.axis_index("y"), lax.axis_index("c")
    rows, width = embeddings.shape
    half, sub = rows // 2, rows // 4
    h = lax.rem(y, 2)
    place = jnp.concatenate([jnp.full((4, sub), c, F32), jnp.full((4, sub), h, F32)])
    place, embeddings = lax.optimization_barrier((place, embeddings))

    near = {0: centroids, 1: shift_x(centroids, -1), 3: shift_x(centroids, 1)}

    mine = lax.dynamic_slice_in_dim(embeddings, h * half, half, 0)
    one = along_z(mine, 1)
    own = lax.dynamic_slice_in_dim(embeddings.reshape(2, 2, sub, width), c, 1, 1).reshape(half, width)
    one, near[1], near[3] = lax.optimization_barrier((one, near[1], near[3]))
    two = along_z(one, 1)
    near[2] = shift_x(near[1], -1)
    first = swap_halves(one)
    two, near[2], first = lax.optimization_barrier((two, near[2], first))
    three = along_z(two, 1)

    fixed = lambda v: pltpu.with_memory_space_constraint(v, pltpu.VMEM) if PIN else v
    table = [fixed(v) for d in ORDER for v in (near[d], swap_cores(near[d]))]

    four = along_z(lax.dynamic_slice_in_dim(three, c * sub, sub, 0), 1)
    lots = [[fixed(v) for v in (own, one, first, two, swap_halves(two))]]
    squares, scores, energy = score(table, lots[0])
    squares, logits, local = fixed(squares), [scores], [energy]
    last, _ = lax.optimization_barrier((four, energy))
    last = swap_halves(last)
    lots.append([fixed(v) for v in (three, swap_halves(three))])
    _, scores, energy = score(table, lots[1], squares)
    last, _ = lax.optimization_barrier((last, energy))
    logits.append(scores)
    local.append(energy)
    lots.append([fixed(four), fixed(last)])
    _, scores, energy = score(table, lots[2], squares)
    logits.append(scores)
    local.append(energy)
    energy, row_energy = energies(local, place, sub)
    logits, pieces = [fixed(v) for v in logits], [v for lot in lots for v in lot]

    message, keep, keep_count = weigh(0, NX - 1, logits, energy, pieces)
    sums, counts = add(swap_cores(message), keep, keep_count)
    sums = [shift_x(m, d) for m, d in zip(sums, ORDER)]
    message, keep, keep_count = weigh(NX - 1, 1, logits, energy, pieces)
    keep_count, *counts = lax.optimization_barrier([keep_count, *counts])
    counts = [shift_x(m, d) for m, d in zip(counts, ORDER)]
    new_centroids, new_masses = update(keep, keep_count, swap_cores(message), [*sums, *counts], masses, centroids)
    return new_centroids, new_masses.reshape(-1), row_energy


def solution(mesh):
    grid = Mesh(mesh.devices.reshape(NX, NZ, NY, NC), ("x", "z", "y", "c"))
    rows, cents = ("x", "z"), ("y", "c", "x", "z")
    return jax.shard_map(
        shards,
        mesh=grid,
        in_specs=(P(rows, None), P(cents, None), P(cents)),
        out_specs=(P(cents, None), P(cents), P(rows)),
        check_vma=False,
    )
```

```python
import functools

import jax
import jax.numpy as jnp
from jax import lax
from jax.experimental import pallas as pl
from jax.experimental.pallas import tpu as pltpu
from jax.sharding import Mesh, PartitionSpec as P

NX, NZ, NY, NC = 4, 8, 4, 2
BF16, F32 = jnp.bfloat16, jnp.float32
TAIL = 16
ORDER = (2, 1, 3, 0)
BATCH = 512
VMEM_LIMIT = 20 * 1024 * 1024
SMALL_LIMIT = 4 * 1024 * 1024
PIN = True


def shift_x(value, by):
    return lax.ppermute(value, "x", [(i, (i + by) % NX) for i in range(NX)])


def swap_cores(value):
    return lax.ppermute(value, "c", [(0, 1), (1, 0)])


def along_z(value, by):
    pairs = []
    for z in range(NZ):
        pairs.append((z * NC, (z + by) % NZ * NC))
        pairs.append((z * NC + 1, (z - by) % NZ * NC + 1))
    return lax.ppermute(value, ("z", "c"), pairs)


def shift_y(value, by):
    return lax.ppermute(value, "y", [(i, (i + by) % NY) for i in range(NY)])


def swap_halves(value):
    pairs = []
    for y in range(NY):
        pairs.append((y * NC, (y ^ 1) * NC))
        pairs.append((y * NC + 1, (y + 1 if y % 2 else y - 1) % NY * NC + 1))
    return lax.ppermute(value, ("y", "c"), pairs)


def combine(parts):
    high = functools.reduce(jnp.maximum, parts)
    return high + jnp.log(sum(jnp.exp(p - high) for p in parts))


def pick(place, first, second):
    return jnp.where(place == 0, first, second)


def small(kernel, place, out, *args):
    return pl.pallas_call(
        kernel,
        out_shape=[jax.ShapeDtypeStruct(shape, F32) for shape in out],
        compiler_params=pltpu.CompilerParams(vmem_limit_bytes=SMALL_LIMIT),
    )(place, *args)


def turn(v, by):
    by %= NZ
    return jnp.concatenate([v[:, NZ - by :], v[:, : NZ - by]], axis=1)


def pack_kernel(place, first, second, third, out):
    sub = out.shape[1]
    given = [v[:, k : k + sub] for v in (first, second, third) for k in range(0, v.shape[1], sub)]
    h = place[4:5, :]
    out[0:1, :] = given[0]
    out[1:2, :] = given[1]
    at = 2
    for mine, other in ((given[2:4], given[4:6]), (given[6:8], given[8:10]), (given[10:12], given[12:14]), (given[14:15], given[15:16])):
        for v, w in ((mine, other), (other, mine)):
            for i in range(len(v)):
                out[at : at + 1, :] = pick(h, v[i], w[i])
                at += 1


def sum_kernel(place, own, *refs):
    refs[-1][...] = combine([own[...]] + [v[...] for v in refs[:-1]])


def block_kernel(place, mine, other, out):
    c = place[0:1, :]
    back = lambda i: pick(c, mine[i : i + 1, :], other[i : i + 1, :])
    ahead = lambda i: pick(c, other[i : i + 1, :], mine[i : i + 1, :])
    for half in range(2):
        for sub in range(2):
            q = 2 * half + sub
            side = ahead if sub else back
            out[q, 0:1, :] = side(half)
            out[q, 4:5, :] = side(14 + half)
            for k in range(1, 4):
                out[q, k : k + 1, :] = ahead(4 * k - 2 + q)
                out[q, NZ - k : NZ - k + 1, :] = back(4 * k - 2 + q)


def near_kernel(place, block, near, far, three, message):
    c = place[0:1, :]
    own = block[...]
    from_back = turn(pick(c, near[...], far[...]), -1)
    from_ahead = turn(pick(c, far[...], near[...]), 1)
    both = combine([own, from_back, from_ahead])
    three[...] = both
    message[...] = pick(c, both, combine([own, from_back]))


def last_kernel(place, three, got, other, energy, own):
    c, h = place[0:1, :], place[4:5, :]
    from_back = turn(pick(c, got[...], other[...]), -3)
    from_ahead = turn(pick(c, other[...], got[...]), 3)
    block = combine([three[...], from_back, from_ahead])
    n = block.shape[2]
    own[...] = block[:, 0]

    def steps(half, step):
        return [pick(c, block[2 * half + i, NZ - step : NZ - step + 1], block[2 * half + i, step : step + 1]) for i in range(2)]

    out = [pick(c, block[2 * half, 0:1], block[2 * half + 1, 0:1]) for half in range(2)]
    for step in range(1, 4):
        low, top = steps(0, step), steps(1, step)
        out += [pick(h, low[i], top[i]) for i in range(2)] + [pick(h, top[i], low[i]) for i in range(2)]
    low, top = (pick(c, block[2 * half, 4:5], block[2 * half + 1, 4:5]) for half in range(2))
    out += [pick(h, low, top), pick(h, top, low)]
    for i, v in enumerate(out):
        energy[:, i * n : (i + 1) * n] = v


def energies(local, place, sub):
    (mine,) = small(pack_kernel, place, [(16, sub)], *local)
    (mine,) = small(sum_kernel, place, [(16, sub)], mine, *[shift_y(mine, d) for d in (1, 2, 3)])
    shape = (4, NZ, sub)
    (block,) = small(block_kernel, place, [shape], mine, swap_cores(mine))
    near = along_z(block, 1)
    three, message = small(near_kernel, place, [shape] * 2, block, near, swap_cores(near))
    got = along_z(message, 3)
    energy, own = small(last_kernel, place, [(1, 16 * sub), (4, sub)], three, got, swap_cores(got))
    return energy, own.reshape(-1)


def turned(column):
    n = column.shape[0]
    return jnp.transpose(jnp.broadcast_to(column, (n, n)))


def write_message(message, at, total, row):
    n, width = total.shape
    message[at : at + n, :] = total.astype(BF16)
    high = row.astype(BF16)
    tail = [high, (row - high.astype(F32)).astype(BF16)]
    if width > 2 * n:
        tail.append(jnp.zeros((TAIL, width - 2 * n), BF16))
    message[at + n : at + n + TAIL, :] = jnp.concatenate(tail, axis=1)


def read_message(message, at, n):
    total = message[at : at + n, :].astype(F32)
    tail = message[at + n : at + n + TAIL, :].astype(F32)
    return total, tail[:, :n] + tail[:, n : 2 * n]


def score_kernel(parts, sizes, given, *refs):
    table, refs = refs[:parts], refs[parts:]
    pieces, refs = refs[: len(sizes)], refs[len(sizes) :]
    squares, logits, energy = refs
    n = table[0].shape[0]
    span = n * NC
    blocks = [jnp.concatenate([table[p + i][...] for i in range(NC)]) for p in range(0, parts, NC)]
    if not given:
        for p, block in enumerate(blocks):
            wide = block.astype(F32)
            total = jnp.sum(wide * wide, axis=1, keepdims=True)
            squares[p * span : (p + 1) * span, :] = jnp.broadcast_to(total, (span, squares.shape[1]))
    batches, at = [[]], 0
    for piece, size in zip(pieces, sizes):
        if sum(k for _, k in batches[-1]) >= BATCH:
            batches.append([])
        batches[-1].append((piece, size))
    for batch in batches:
        rows = jnp.concatenate([piece[...] for piece, _ in batch])
        lot = slice(at, at + rows.shape[0])
        at += rows.shape[0]
        high = None
        for p, block in enumerate(blocks):
            product = lax.dot_general(block, rows, (((1,), (1,)), ((), ())), preferred_element_type=F32)
            scores = 2.0 * product - squares[p * span : (p + 1) * span, :1]
            logits[p * span : (p + 1) * span, lot] = scores
            top = jnp.max(scores, axis=0, keepdims=True)
            high = top if high is None else jnp.maximum(high, top)
        total = None
        for p in range(len(blocks)):
            part = jnp.sum(jnp.exp(logits[p * span : (p + 1) * span, lot] - high), axis=0, keepdims=True)
            total = part if total is None else total + part
        energy[:, lot] = high + jnp.log(total)


def score(table, pieces, squares=None):
    count, width = sum(t.shape[0] for t in table), table[0].shape[1]
    sizes = tuple(p.shape[0] for p in pieces)
    rows, given = sum(sizes), squares is not None
    out = [
        pltpu.VMEM((count, rows), F32) if PIN else jax.ShapeDtypeStruct((count, rows), F32),
        jax.ShapeDtypeStruct((1, rows), F32),
    ]
    if not given:
        out.insert(0, jax.ShapeDtypeStruct((count, 128), F32))
    got = pl.pallas_call(
        functools.partial(score_kernel, len(table), sizes, given),
        out_shape=out,
        compiler_params=pltpu.CompilerParams(vmem_limit_bytes=VMEM_LIMIT),
        cost_estimate=pl.CostEstimate(
            flops=4 * count * rows * width,
            bytes_accessed=4 * count * rows + 2 * (count + rows) * width,
            transcendentals=count * rows,
        ),
    )(*table, *pieces, *([squares] if given else []))
    return (squares, *got) if given else got


def weigh_kernel(first, groups, sizes, energy, *refs):
    logits, refs = refs[: len(groups)], refs[len(groups) :]
    slab, (message, keep, keep_count) = refs[: len(sizes)], refs[len(sizes) :]
    n, width = keep_count.shape[1], keep.shape[1]
    span, step = n * NC, min(sizes)
    tile = min(256, width)
    for i in range(keep.shape[0] // n):
        lot = slice((first + i) * span, (first + i + 1) * span)
        counts, sets, at = None, [], 0
        for p, size in enumerate(groups):
            for cut in range(0, size, step):
                w = jnp.exp(logits[p][lot, cut : cut + step] - energy[:, at + cut : at + cut + step])
                counts = w if counts is None else counts + w
                sets.append(w.astype(BF16))
            at += size
        column = jnp.sum(counts, axis=1, keepdims=True)
        pairs = [jnp.concatenate(sets[p : p + 2], axis=1) for p in range(0, len(sets), 2)]
        totals = []
        for at in range(0, width, tile):
            acc = None
            for p, pair in enumerate(pairs):
                rows = slab[p][:, at : at + tile]
                if rows.shape[0] < pair.shape[1]:
                    rows = jnp.concatenate([rows, slab[p + 1][:, at : at + tile]])
                term = jnp.dot(pair, rows, preferred_element_type=F32)
                acc = term if acc is None else acc + term
            keep[i * n : (i + 1) * n, at : at + tile] = acc[:n]
            totals.append(acc[n:])
        keep_count[i * TAIL : (i + 1) * TAIL, :] = turned(column[:n])[:TAIL]
        write_message(message, i * (n + TAIL), jnp.concatenate(totals, axis=1), turned(column[n:])[:TAIL])


def weigh(first, count, logits, energy, slab):
    span, width = logits[0].shape[0] // NX, slab[0].shape[1]
    n = span // NC
    sizes, groups = tuple(p.shape[0] for p in slab), tuple(v.shape[1] for v in logits)
    total, height = sum(sizes), count * span
    return pl.pallas_call(
        functools.partial(weigh_kernel, first, groups, sizes),
        out_shape=(
            jax.ShapeDtypeStruct((count * (n + TAIL), width), BF16),
            jax.ShapeDtypeStruct((count * n, width), F32),
            jax.ShapeDtypeStruct((count * TAIL, n), F32),
        ),
        compiler_params=pltpu.CompilerParams(vmem_limit_bytes=VMEM_LIMIT),
        cost_estimate=pl.CostEstimate(
            flops=2 * height * total * width,
            bytes_accessed=4 * height * total + 2 * total * width,
            transcendentals=height * total,
        ),
    )(energy, *logits, *slab)


def call(kernel, out_shape, *args):
    return pl.pallas_call(
        kernel,
        out_shape=out_shape,
        compiler_params=pltpu.CompilerParams(vmem_limit_bytes=VMEM_LIMIT),
    )(*args)


def add_kernel(n, got, keep, keep_count, count, *messages):
    count[...] = jnp.zeros(count.shape, F32)
    for i, message in enumerate(messages):
        total, row = read_message(got, i * (n + TAIL), n)
        message[...] = (total + keep[i * n : (i + 1) * n, :]).astype(BF16)
        count[i : i + 1, :] = row[:1] + keep_count[i * TAIL : i * TAIL + 1, :]


def add(got, keep, keep_count):
    n = keep_count.shape[1]
    k = keep.shape[0] // n
    shapes = [jax.ShapeDtypeStruct((8, n), F32)] + [jax.ShapeDtypeStruct((n, keep.shape[1]), BF16)] * k
    return call(functools.partial(add_kernel, n), shapes, got, keep, keep_count)


def hand_on_kernel(count, one, out):
    out[...] = jnp.broadcast_to(count[0:1, :] + one[2:3, :], out.shape)


def update_kernel(n, keep, keep_count, got, one, two, masses, centroids, *refs):
    others, (new_centroids, new_masses) = refs[:-2], refs[-2:]
    total, row = read_message(got, 0, n)
    total, row = total + keep[...], (row + keep_count[...])[:1] + one[1:2, :] + two[:1, :]
    for message in others:
        total = total + message[...].astype(F32)
    mass = masses[...]
    new = mass + row
    new_masses[...] = new
    column = lambda v: jnp.transpose(jnp.broadcast_to(v, (n, n)))[:, :1]
    new_centroids[...] = (column(mass) * centroids[...].astype(F32) + total) / column(new)


def update(keep, keep_count, got, counts, others, masses, centroids):
    n, width = centroids.shape
    out = (jax.ShapeDtypeStruct((n, width), F32), jax.ShapeDtypeStruct((1, n), F32))
    args = (keep, keep_count, got, *counts, masses.reshape(1, n), centroids, *others)
    return call(functools.partial(update_kernel, n), out, *args)


def shards(embeddings, centroids, masses):
    y, c = lax.axis_index("y"), lax.axis_index("c")
    rows, width = embeddings.shape
    half, sub = rows // 2, rows // 4
    h = lax.rem(y, 2)
    place = jnp.concatenate([jnp.full((4, sub), c, F32), jnp.full((4, sub), h, F32)])
    place, embeddings = lax.optimization_barrier((place, embeddings))

    near = {0: centroids, 1: shift_x(centroids, -1), 3: shift_x(centroids, 1)}

    mine = lax.dynamic_slice_in_dim(embeddings, h * half, half, 0)
    one = along_z(mine, 1)
    own = lax.dynamic_slice_in_dim(embeddings.reshape(2, 2, sub, width), c, 1, 1).reshape(half, width)
    swapped = {0: swap_cores(centroids)}
    one, near[1], near[3], swapped[0] = lax.optimization_barrier((one, near[1], near[3], swapped[0]))
    swapped |= {1: swap_cores(near[1]), 3: swap_cores(near[3])}
    near[2] = shift_x(near[1], -1)
    first = swap_halves(one)
    two = along_z(one, 1)
    two, near[2], swapped[1], swapped[3] = lax.optimization_barrier((two, near[2], swapped[1], swapped[3]))
    swapped[2] = swap_cores(near[2])
    three = along_z(two, 1)
    two, first = lax.optimization_barrier((two, first))

    fixed = lambda v: pltpu.with_memory_space_constraint(v, pltpu.VMEM) if PIN else v
    table = [fixed(v) for d in ORDER for v in (near[d], swapped[d])]

    four = along_z(lax.dynamic_slice_in_dim(three, c * sub, sub, 0), 1)
    lots = [[fixed(v) for v in (own, one, first, two, swap_halves(two))]]
    squares, scores, energy = score(table, lots[0])
    squares, logits, local = fixed(squares), [scores], [energy]
    last, _ = lax.optimization_barrier((four, energy))
    last = swap_halves(last)
    lots.append([fixed(v) for v in (three, swap_halves(three))])
    _, scores, energy = score(table, lots[1], squares)
    last, _ = lax.optimization_barrier((last, energy))
    logits.append(scores)
    local.append(energy)
    lots.append([fixed(four), fixed(last)])
    _, scores, energy = score(table, lots[2], squares)
    logits.append(scores)
    local.append(energy)
    energy, row_energy = energies(local, place, sub)
    logits, pieces = [fixed(v) for v in logits], [v for lot in lots for v in lot]

    message, keep, keep_count = weigh(0, NX - 1, logits, energy, pieces)
    count, *sums = add(swap_cores(message), keep, keep_count)
    sums = [shift_x(m, d) for m, d in zip(sums, ORDER)]
    message, keep, keep_count = weigh(NX - 1, 1, logits, energy, pieces)
    keep_count, count = lax.optimization_barrier((keep_count, count))
    one = shift_x(count, 1)
    two = shift_x(call(hand_on_kernel, jax.ShapeDtypeStruct(count.shape, F32), count, one), 2)
    new_centroids, new_masses = update(keep, keep_count, swap_cores(message), (one, two), sums, masses, centroids)
    return new_centroids, new_masses.reshape(-1), row_energy


def solution(mesh):
    grid = Mesh(mesh.devices.reshape(NX, NZ, NY, NC), ("x", "z", "y", "c"))
    rows, cents = ("x", "z"), ("y", "c", "x", "z")
    return jax.shard_map(
        shards,
        mesh=grid,
        in_specs=(P(rows, None), P(cents, None), P(cents)),
        out_specs=(P(cents, None), P(cents), P(rows)),
        check_vma=False,
    )
```

```python
import functools

import jax
import jax.numpy as jnp
from jax import lax
from jax.experimental import pallas as pl
from jax.experimental.pallas import tpu as pltpu
from jax.sharding import Mesh, PartitionSpec as P

NX, NZ, NY, NC = 4, 8, 4, 2
BF16, F32 = jnp.bfloat16, jnp.float32
TAIL = 16
ORDER = (2, 1, 3, 0)
BATCH = 512
VMEM_LIMIT = 20 * 1024 * 1024
SMALL_LIMIT = 4 * 1024 * 1024
PIN = True


def shift_x(value, by):
    return lax.ppermute(value, "x", [(i, (i + by) % NX) for i in range(NX)])


def swap_cores(value):
    return lax.ppermute(value, "c", [(0, 1), (1, 0)])


def along_z(value, by):
    pairs = []
    for z in range(NZ):
        pairs.append((z * NC, (z + by) % NZ * NC))
        pairs.append((z * NC + 1, (z - by) % NZ * NC + 1))
    return lax.ppermute(value, ("z", "c"), pairs)


def shift_y(value, by):
    return lax.ppermute(value, "y", [(i, (i + by) % NY) for i in range(NY)])


def swap_halves(value):
    pairs = []
    for y in range(NY):
        pairs.append((y * NC, (y ^ 1) * NC))
        pairs.append((y * NC + 1, (y + 1 if y % 2 else y - 1) % NY * NC + 1))
    return lax.ppermute(value, ("y", "c"), pairs)


def combine(parts):
    high = functools.reduce(jnp.maximum, parts)
    return high + jnp.log(sum(jnp.exp(p - high) for p in parts))


def pick(place, first, second):
    return jnp.where(place == 0, first, second)


def small(kernel, place, out, *args):
    return pl.pallas_call(
        kernel,
        out_shape=[jax.ShapeDtypeStruct(shape, F32) for shape in out],
        compiler_params=pltpu.CompilerParams(vmem_limit_bytes=SMALL_LIMIT),
    )(place, *args)


def turn(v, by):
    by %= NZ
    return jnp.concatenate([v[:, NZ - by :], v[:, : NZ - by]], axis=1)


def pack_kernel(place, first, second, third, out):
    sub = out.shape[1]
    given = [v[:, k : k + sub] for v in (first, second, third) for k in range(0, v.shape[1], sub)]
    h = place[4:5, :]
    out[0:1, :] = given[0]
    out[1:2, :] = given[1]
    at = 2
    for mine, other in ((given[2:4], given[4:6]), (given[6:8], given[8:10]), (given[10:12], given[12:14]), (given[14:15], given[15:16])):
        for v, w in ((mine, other), (other, mine)):
            for i in range(len(v)):
                out[at : at + 1, :] = pick(h, v[i], w[i])
                at += 1


def sum_kernel(place, own, *refs):
    refs[-1][...] = combine([own[...]] + [v[...] for v in refs[:-1]])


def block_kernel(place, mine, other, out):
    c = place[0:1, :]
    back = lambda i: pick(c, mine[i : i + 1, :], other[i : i + 1, :])
    ahead = lambda i: pick(c, other[i : i + 1, :], mine[i : i + 1, :])
    for half in range(2):
        for sub in range(2):
            q = 2 * half + sub
            side = ahead if sub else back
            out[q, 0:1, :] = side(half)
            out[q, 4:5, :] = side(14 + half)
            for k in range(1, 4):
                out[q, k : k + 1, :] = ahead(4 * k - 2 + q)
                out[q, NZ - k : NZ - k + 1, :] = back(4 * k - 2 + q)


def near_kernel(place, block, near, far, three, message):
    c = place[0:1, :]
    own = block[...]
    from_back = turn(pick(c, near[...], far[...]), -1)
    from_ahead = turn(pick(c, far[...], near[...]), 1)
    both = combine([own, from_back, from_ahead])
    three[...] = both
    message[...] = pick(c, both, combine([own, from_back]))


def last_kernel(place, three, got, other, energy, own):
    c, h = place[0:1, :], place[4:5, :]
    from_back = turn(pick(c, got[...], other[...]), -3)
    from_ahead = turn(pick(c, other[...], got[...]), 3)
    block = combine([three[...], from_back, from_ahead])
    n = block.shape[2]
    own[...] = block[:, 0]

    def steps(half, step):
        return [pick(c, block[2 * half + i, NZ - step : NZ - step + 1], block[2 * half + i, step : step + 1]) for i in range(2)]

    out = [pick(c, block[2 * half, 0:1], block[2 * half + 1, 0:1]) for half in range(2)]
    for step in range(1, 4):
        low, top = steps(0, step), steps(1, step)
        out += [pick(h, low[i], top[i]) for i in range(2)] + [pick(h, top[i], low[i]) for i in range(2)]
    low, top = (pick(c, block[2 * half, 4:5], block[2 * half + 1, 4:5]) for half in range(2))
    out += [pick(h, low, top), pick(h, top, low)]
    for i, v in enumerate(out):
        energy[:, i * n : (i + 1) * n] = v


def energies(local, place, sub):
    (mine,) = small(pack_kernel, place, [(16, sub)], *local)
    (mine,) = small(sum_kernel, place, [(16, sub)], mine, *[shift_y(mine, d) for d in (1, 2, 3)])
    shape = (4, NZ, sub)
    (block,) = small(block_kernel, place, [shape], mine, swap_cores(mine))
    near = along_z(block, 1)
    three, message = small(near_kernel, place, [shape] * 2, block, near, swap_cores(near))
    got = along_z(message, 3)
    energy, own = small(last_kernel, place, [(1, 16 * sub), (4, sub)], three, got, swap_cores(got))
    return energy, own.reshape(-1)


def turned(column):
    n = column.shape[0]
    return jnp.transpose(jnp.broadcast_to(column, (n, n)))


def write_message(message, at, total, row):
    n, width = total.shape
    message[at : at + n, :] = total.astype(BF16)
    high = row.astype(BF16)
    tail = [high, (row - high.astype(F32)).astype(BF16)]
    if width > 2 * n:
        tail.append(jnp.zeros((TAIL, width - 2 * n), BF16))
    message[at + n : at + n + TAIL, :] = jnp.concatenate(tail, axis=1)


def read_message(message, at, n):
    total = message[at : at + n, :].astype(F32)
    tail = message[at + n : at + n + TAIL, :].astype(F32)
    return total, tail[:, :n] + tail[:, n : 2 * n]


def score_kernel(parts, sizes, given, *refs):
    table, refs = refs[:parts], refs[parts:]
    pieces, refs = refs[: len(sizes)], refs[len(sizes) :]
    squares, logits, energy = refs
    n = table[0].shape[0]
    span = n * NC
    blocks = [jnp.concatenate([table[p + i][...] for i in range(NC)]) for p in range(0, parts, NC)]
    if not given:
        for p, block in enumerate(blocks):
            wide = block.astype(F32)
            total = jnp.sum(wide * wide, axis=1, keepdims=True)
            squares[p * span : (p + 1) * span, :] = jnp.broadcast_to(total, (span, squares.shape[1]))
    batches, at = [[]], 0
    for piece, size in zip(pieces, sizes):
        if sum(k for _, k in batches[-1]) >= BATCH:
            batches.append([])
        batches[-1].append((piece, size))
    for batch in batches:
        rows = jnp.concatenate([piece[...] for piece, _ in batch])
        lot = slice(at, at + rows.shape[0])
        at += rows.shape[0]
        high = None
        for p, block in enumerate(blocks):
            product = lax.dot_general(block, rows, (((1,), (1,)), ((), ())), preferred_element_type=F32)
            scores = 2.0 * product - squares[p * span : (p + 1) * span, :1]
            logits[p * span : (p + 1) * span, lot] = scores
            top = jnp.max(scores, axis=0, keepdims=True)
            high = top if high is None else jnp.maximum(high, top)
        total = None
        for p in range(len(blocks)):
            part = jnp.sum(jnp.exp(logits[p * span : (p + 1) * span, lot] - high), axis=0, keepdims=True)
            total = part if total is None else total + part
        energy[:, lot] = high + jnp.log(total)


def score(table, pieces, squares=None):
    count, width = sum(t.shape[0] for t in table), table[0].shape[1]
    sizes = tuple(p.shape[0] for p in pieces)
    rows, given = sum(sizes), squares is not None
    out = [
        pltpu.VMEM((count, rows), F32) if PIN else jax.ShapeDtypeStruct((count, rows), F32),
        jax.ShapeDtypeStruct((1, rows), F32),
    ]
    if not given:
        out.insert(0, jax.ShapeDtypeStruct((count, 128), F32))
    got = pl.pallas_call(
        functools.partial(score_kernel, len(table), sizes, given),
        out_shape=out,
        compiler_params=pltpu.CompilerParams(vmem_limit_bytes=VMEM_LIMIT),
        cost_estimate=pl.CostEstimate(
            flops=4 * count * rows * width,
            bytes_accessed=4 * count * rows + 2 * (count + rows) * width,
            transcendentals=count * rows,
        ),
    )(*table, *pieces, *([squares] if given else []))
    return (squares, *got) if given else got


def weigh_kernel(first, groups, sizes, energy, *refs):
    logits, refs = refs[: len(groups)], refs[len(groups) :]
    slab, (message, keep, keep_count) = refs[: len(sizes)], refs[len(sizes) :]
    n, width = keep_count.shape[1], keep.shape[1]
    span, step = n * NC, min(sizes)
    tile = min(256, width)
    for i in range(keep.shape[0] // n):
        lot = slice((first + i) * span, (first + i + 1) * span)
        counts, sets, at = None, [], 0
        for p, size in enumerate(groups):
            for cut in range(0, size, step):
                w = jnp.exp(logits[p][lot, cut : cut + step] - energy[:, at + cut : at + cut + step])
                counts = w if counts is None else counts + w
                sets.append(w.astype(BF16))
            at += size
        column = jnp.sum(counts, axis=1, keepdims=True)
        pairs = [jnp.concatenate(sets[p : p + 2], axis=1) for p in range(0, len(sets), 2)]
        totals = []
        for at in range(0, width, tile):
            acc = None
            for p, pair in enumerate(pairs):
                rows = slab[p][:, at : at + tile]
                if rows.shape[0] < pair.shape[1]:
                    rows = jnp.concatenate([rows, slab[p + 1][:, at : at + tile]])
                term = jnp.dot(pair, rows, preferred_element_type=F32)
                acc = term if acc is None else acc + term
            keep[i * n : (i + 1) * n, at : at + tile] = acc[:n]
            totals.append(acc[n:])
        keep_count[i * TAIL : (i + 1) * TAIL, :] = turned(column[:n])[:TAIL]
        write_message(message, i * (n + TAIL), jnp.concatenate(totals, axis=1), turned(column[n:])[:TAIL])


def weigh(first, count, logits, energy, slab):
    span, width = logits[0].shape[0] // NX, slab[0].shape[1]
    n = span // NC
    sizes, groups = tuple(p.shape[0] for p in slab), tuple(v.shape[1] for v in logits)
    total, height = sum(sizes), count * span
    return pl.pallas_call(
        functools.partial(weigh_kernel, first, groups, sizes),
        out_shape=(
            jax.ShapeDtypeStruct((count * (n + TAIL), width), BF16),
            jax.ShapeDtypeStruct((count * n, width), F32),
            jax.ShapeDtypeStruct((count * TAIL, n), F32),
        ),
        compiler_params=pltpu.CompilerParams(vmem_limit_bytes=VMEM_LIMIT),
        cost_estimate=pl.CostEstimate(
            flops=2 * height * total * width,
            bytes_accessed=4 * height * total + 2 * total * width,
            transcendentals=height * total,
        ),
    )(energy, *logits, *slab)


def call(kernel, out_shape, *args):
    return pl.pallas_call(
        kernel,
        out_shape=out_shape,
        compiler_params=pltpu.CompilerParams(vmem_limit_bytes=VMEM_LIMIT),
    )(*args)


def add_kernel(n, got, keep, keep_count, *messages):
    for i, message in enumerate(messages):
        total, row = read_message(got, i * (n + TAIL), n)
        total = total + keep[i * n : (i + 1) * n, :]
        write_message(message, 0, total, row + keep_count[i * TAIL : (i + 1) * TAIL, :])


def add(got, keep, keep_count):
    n = keep_count.shape[1]
    shape = jax.ShapeDtypeStruct((n + TAIL, got.shape[1]), BF16)
    return call(functools.partial(add_kernel, n), (shape,) * (NX - 1), got, keep, keep_count)


def update_kernel(n, keep, keep_count, got, one, two, three, masses, centroids, new_centroids, new_masses):
    total, row = keep[...], keep_count[...]
    for message in (got, one, two, three):
        t, r = read_message(message, 0, n)
        total, row = total + t, row + r
    mass = masses[...]
    new = mass + row[:1]
    new_masses[...] = new
    column = lambda v: jnp.transpose(jnp.broadcast_to(v, (n, n)))[:, :1]
    new_centroids[...] = (column(mass) * centroids[...].astype(F32) + total) / column(new)


def update(keep, keep_count, got, others, masses, centroids):
    n, width = centroids.shape
    out = (jax.ShapeDtypeStruct((n, width), F32), jax.ShapeDtypeStruct((1, n), F32))
    return call(
        functools.partial(update_kernel, n), out, keep, keep_count, got, *others, masses.reshape(1, n), centroids
    )


def shards(embeddings, centroids, masses):
    y, c = lax.axis_index("y"), lax.axis_index("c")
    rows, width = embeddings.shape
    half, sub = rows // 2, rows // 4
    h = lax.rem(y, 2)
    place = jnp.concatenate([jnp.full((4, sub), c, F32), jnp.full((4, sub), h, F32)])
    place, embeddings = lax.optimization_barrier((place, embeddings))

    near = {0: centroids, 1: shift_x(centroids, -1), 3: shift_x(centroids, 1)}

    mine = lax.dynamic_slice_in_dim(embeddings, h * half, half, 0)
    one = along_z(mine, 1)
    own = lax.dynamic_slice_in_dim(embeddings.reshape(2, 2, sub, width), c, 1, 1).reshape(half, width)
    one, near[1], near[3] = lax.optimization_barrier((one, near[1], near[3]))
    near[2] = shift_x(near[1], -1)
    first = swap_halves(one)
    two = along_z(one, 1)
    two, near[2] = lax.optimization_barrier((two, near[2]))
    three = along_z(two, 1)
    two, first = lax.optimization_barrier((two, first))

    fixed = lambda v: pltpu.with_memory_space_constraint(v, pltpu.VMEM) if PIN else v
    table = [fixed(v) for d in ORDER for v in (near[d], swap_cores(near[d]))]

    four = along_z(lax.dynamic_slice_in_dim(three, c * sub, sub, 0), 1)
    lots = [[fixed(v) for v in (own, one, first, two, swap_halves(two))]]
    squares, scores, energy = score(table, lots[0])
    squares, logits, local = fixed(squares), [scores], [energy]
    last, _ = lax.optimization_barrier((four, energy))
    last = swap_halves(last)
    lots.append([fixed(v) for v in (three, swap_halves(three))])
    _, scores, energy = score(table, lots[1], squares)
    last, _ = lax.optimization_barrier((last, energy))
    logits.append(scores)
    local.append(energy)
    lots.append([fixed(four), fixed(last)])
    _, scores, energy = score(table, lots[2], squares)
    logits.append(scores)
    local.append(energy)
    energy, row_energy = energies(local, place, sub)
    logits, pieces = [fixed(v) for v in logits], [v for lot in lots for v in lot]

    message, keep, keep_count = weigh(0, NX - 1, logits, energy, pieces)
    sent = add(swap_cores(message), keep, keep_count)
    message, keep, keep_count = weigh(NX - 1, 1, logits, energy, pieces)
    others = [shift_x(m, d) for m, d in zip(sent, ORDER)]
    new_centroids, new_masses = update(keep, keep_count, swap_cores(message), others, masses, centroids)
    return new_centroids, new_masses.reshape(-1), row_energy


def solution(mesh):
    grid = Mesh(mesh.devices.reshape(NX, NZ, NY, NC), ("x", "z", "y", "c"))
    rows, cents = ("x", "z"), ("y", "c", "x", "z")
    return jax.shard_map(
        shards,
        mesh=grid,
        in_specs=(P(rows, None), P(cents, None), P(cents)),
        out_specs=(P(cents, None), P(cents), P(rows)),
        check_vma=False,
    )
```

```python
import functools

import jax
import jax.numpy as jnp
from jax import lax
from jax.experimental import pallas as pl
from jax.experimental.pallas import tpu as pltpu
from jax.sharding import Mesh, PartitionSpec as P

NX, NZ, NY, NC = 4, 8, 4, 2
BF16, F32 = jnp.bfloat16, jnp.float32
TAIL = 16
ORDER = (1, 3, 2, 0)
BATCH = 512
VMEM_LIMIT = 20 * 1024 * 1024
SMALL_LIMIT = 4 * 1024 * 1024
PIN = True


def shift_x(value, by):
    return lax.ppermute(value, "x", [(i, (i + by) % NX) for i in range(NX)])


def swap_cores(value):
    return lax.ppermute(value, "c", [(0, 1), (1, 0)])


def along_z(value, by):
    pairs = []
    for z in range(NZ):
        pairs.append((z * NC, (z + by) % NZ * NC))
        pairs.append((z * NC + 1, (z - by) % NZ * NC + 1))
    return lax.ppermute(value, ("z", "c"), pairs)


def shift_y(value, by):
    return lax.ppermute(value, "y", [(i, (i + by) % NY) for i in range(NY)])


def swap_halves(value):
    pairs = []
    for y in range(NY):
        pairs.append((y * NC, (y ^ 1) * NC))
        pairs.append((y * NC + 1, (y + 1 if y % 2 else y - 1) % NY * NC + 1))
    return lax.ppermute(value, ("y", "c"), pairs)


def combine(parts):
    high = functools.reduce(jnp.maximum, parts)
    return high + jnp.log(sum(jnp.exp(p - high) for p in parts))


def pick(place, first, second):
    return jnp.where(place == 0, first, second)


def small(kernel, place, out, *args):
    return pl.pallas_call(
        kernel,
        out_shape=[jax.ShapeDtypeStruct(shape, F32) for shape in out],
        compiler_params=pltpu.CompilerParams(vmem_limit_bytes=SMALL_LIMIT),
    )(place, *args)


def turn(v, by):
    by %= NZ
    return jnp.concatenate([v[:, NZ - by :], v[:, : NZ - by]], axis=1)


def pack_kernel(place, first, second, third, out):
    sub = out.shape[1]
    given = [v[:, k : k + sub] for v in (first, second, third) for k in range(0, v.shape[1], sub)]
    h = place[4:5, :]
    out[0:1, :] = given[0]
    out[1:2, :] = given[1]
    at = 2
    for mine, other in ((given[2:4], given[4:6]), (given[6:8], given[8:10]), (given[10:12], given[12:14]), (given[14:15], given[15:16])):
        for v, w in ((mine, other), (other, mine)):
            for i in range(len(v)):
                out[at : at + 1, :] = pick(h, v[i], w[i])
                at += 1


def sum_kernel(place, own, *refs):
    refs[-1][...] = combine([own[...]] + [v[...] for v in refs[:-1]])


def block_kernel(place, mine, other, out):
    c = place[0:1, :]
    back = lambda i: pick(c, mine[i : i + 1, :], other[i : i + 1, :])
    ahead = lambda i: pick(c, other[i : i + 1, :], mine[i : i + 1, :])
    for half in range(2):
        for sub in range(2):
            q = 2 * half + sub
            side = ahead if sub else back
            out[q, 0:1, :] = side(half)
            out[q, 4:5, :] = side(14 + half)
            for k in range(1, 4):
                out[q, k : k + 1, :] = ahead(4 * k - 2 + q)
                out[q, NZ - k : NZ - k + 1, :] = back(4 * k - 2 + q)


def near_kernel(place, block, near, far, three, message):
    c = place[0:1, :]
    own = block[...]
    from_back = turn(pick(c, near[...], far[...]), -1)
    from_ahead = turn(pick(c, far[...], near[...]), 1)
    both = combine([own, from_back, from_ahead])
    three[...] = both
    message[...] = pick(c, both, combine([own, from_back]))


def last_kernel(place, three, got, other, energy, own):
    c, h = place[0:1, :], place[4:5, :]
    from_back = turn(pick(c, got[...], other[...]), -3)
    from_ahead = turn(pick(c, other[...], got[...]), 3)
    block = combine([three[...], from_back, from_ahead])
    n = block.shape[2]
    own[...] = block[:, 0]

    def steps(half, step):
        return [pick(c, block[2 * half + i, NZ - step : NZ - step + 1], block[2 * half + i, step : step + 1]) for i in range(2)]

    out = [pick(c, block[2 * half, 0:1], block[2 * half + 1, 0:1]) for half in range(2)]
    for step in range(1, 4):
        low, top = steps(0, step), steps(1, step)
        out += [pick(h, low[i], top[i]) for i in range(2)] + [pick(h, top[i], low[i]) for i in range(2)]
    low, top = (pick(c, block[2 * half, 4:5], block[2 * half + 1, 4:5]) for half in range(2))
    out += [pick(h, low, top), pick(h, top, low)]
    for i, v in enumerate(out):
        energy[:, i * n : (i + 1) * n] = v


def energies(local, place, sub):
    (mine,) = small(pack_kernel, place, [(16, sub)], *local)
    (mine,) = small(sum_kernel, place, [(16, sub)], mine, *[shift_y(mine, d) for d in (1, 2, 3)])
    shape = (4, NZ, sub)
    (block,) = small(block_kernel, place, [shape], mine, swap_cores(mine))
    near = along_z(block, 1)
    three, message = small(near_kernel, place, [shape] * 2, block, near, swap_cores(near))
    got = along_z(message, 3)
    energy, own = small(last_kernel, place, [(1, 16 * sub), (4, sub)], three, got, swap_cores(got))
    return energy, own.reshape(-1)


def turned(column):
    n = column.shape[0]
    return jnp.transpose(jnp.broadcast_to(column, (n, n)))


def write_message(message, at, total, row):
    n, width = total.shape
    message[at : at + n, :] = total.astype(BF16)
    high = row.astype(BF16)
    tail = [high, (row - high.astype(F32)).astype(BF16)]
    if width > 2 * n:
        tail.append(jnp.zeros((TAIL, width - 2 * n), BF16))
    message[at + n : at + n + TAIL, :] = jnp.concatenate(tail, axis=1)


def read_message(message, at, n):
    total = message[at : at + n, :].astype(F32)
    tail = message[at + n : at + n + TAIL, :].astype(F32)
    return total, tail[:, :n] + tail[:, n : 2 * n]


def score_kernel(parts, sizes, *refs):
    if parts:
        table, pieces, (block, squares, logits, energy) = refs[:parts], refs[parts:-4], refs[-4:]
    else:
        block, squares, *pieces = refs[:-2]
        logits, energy = refs[-2:]
    height = block.shape[0]
    span = height // NX
    if parts:
        n = table[0].shape[0]
        for p in range(parts):
            lot = slice(p * n, (p + 1) * n)
            part = table[p][...]
            block[lot, :] = part
            wide = part.astype(F32)
            total = jnp.sum(wide * wide, axis=1, keepdims=True)
            squares[lot, :] = jnp.broadcast_to(total, (n, squares.shape[1]))
    batches, at = [[]], 0
    for piece, size in zip(pieces, sizes):
        if sum(k for _, k in batches[-1]) >= BATCH:
            batches.append([])
        batches[-1].append((piece, size))
    for batch in batches:
        rows = jnp.concatenate([piece[...] for piece, _ in batch])
        lot = slice(at, at + rows.shape[0])
        at += rows.shape[0]
        high = None
        for k in range(0, height, span):
            product = lax.dot_general(
                block[k : k + span, :], rows, (((1,), (1,)), ((), ())), preferred_element_type=F32
            )
            scores = 2.0 * product - squares[k : k + span, :1]
            logits[k : k + span, lot] = scores
            top = jnp.max(scores, axis=0, keepdims=True)
            high = top if high is None else jnp.maximum(high, top)
        total = None
        for k in range(0, height, span):
            part = jnp.sum(jnp.exp(logits[k : k + span, lot] - high), axis=0, keepdims=True)
            total = part if total is None else total + part
        energy[:, lot] = high + jnp.log(total)


def score(table, pieces):
    whole = len(table) == 2
    count = table[0].shape[0] if whole else sum(t.shape[0] for t in table)
    width, sizes = table[0].shape[1], tuple(p.shape[0] for p in pieces)
    rows = sum(sizes)
    out = [
        pltpu.VMEM((count, rows), F32) if PIN else jax.ShapeDtypeStruct((count, rows), F32),
        jax.ShapeDtypeStruct((1, rows), F32),
    ]
    if not whole:
        out = [jax.ShapeDtypeStruct((count, width), BF16), jax.ShapeDtypeStruct((count, 128), F32)] + out
    return pl.pallas_call(
        functools.partial(score_kernel, 0 if whole else len(table), sizes),
        out_shape=out,
        compiler_params=pltpu.CompilerParams(vmem_limit_bytes=VMEM_LIMIT),
        cost_estimate=pl.CostEstimate(
            flops=4 * count * rows * width,
            bytes_accessed=4 * count * rows + 2 * (count + rows) * width,
            transcendentals=count * rows,
        ),
    )(*table, *pieces)


def weigh_kernel(first, groups, sizes, energy, *refs):
    logits, refs = refs[: len(groups)], refs[len(groups) :]
    slab, (message, keep, keep_count) = refs[: len(sizes)], refs[len(sizes) :]
    n, width = keep_count.shape[1], keep.shape[1]
    span, step = n * NC, min(sizes)
    tile = min(256, width)
    for i in range(keep.shape[0] // n):
        lot = slice((first + i) * span, (first + i + 1) * span)
        counts, sets, at = None, [], 0
        for p, size in enumerate(groups):
            for cut in range(0, size, step):
                w = jnp.exp(logits[p][lot, cut : cut + step] - energy[:, at + cut : at + cut + step])
                counts = w if counts is None else counts + w
                sets.append(w.astype(BF16))
            at += size
        column = jnp.sum(counts, axis=1, keepdims=True)
        pairs = [jnp.concatenate(sets[p : p + 2], axis=1) for p in range(0, len(sets), 2)]
        totals = []
        for at in range(0, width, tile):
            acc = None
            for p, pair in enumerate(pairs):
                rows = slab[p][:, at : at + tile]
                if rows.shape[0] < pair.shape[1]:
                    rows = jnp.concatenate([rows, slab[p + 1][:, at : at + tile]])
                term = jnp.dot(pair, rows, preferred_element_type=F32)
                acc = term if acc is None else acc + term
            keep[i * n : (i + 1) * n, at : at + tile] = acc[:n]
            totals.append(acc[n:])
        keep_count[i * TAIL : (i + 1) * TAIL, :] = turned(column[:n])[:TAIL]
        write_message(message, i * (n + TAIL), jnp.concatenate(totals, axis=1), turned(column[n:])[:TAIL])


def weigh(first, count, logits, energy, slab):
    span, width = logits[0].shape[0] // NX, slab[0].shape[1]
    n = span // NC
    sizes, groups = tuple(p.shape[0] for p in slab), tuple(v.shape[1] for v in logits)
    total, height = sum(sizes), count * span
    return pl.pallas_call(
        functools.partial(weigh_kernel, first, groups, sizes),
        out_shape=(
            jax.ShapeDtypeStruct((count * (n + TAIL), width), BF16),
            jax.ShapeDtypeStruct((count * n, width), F32),
            jax.ShapeDtypeStruct((count * TAIL, n), F32),
        ),
        compiler_params=pltpu.CompilerParams(vmem_limit_bytes=VMEM_LIMIT),
        cost_estimate=pl.CostEstimate(
            flops=2 * height * total * width,
            bytes_accessed=4 * height * total + 2 * total * width,
            transcendentals=height * total,
        ),
    )(energy, *logits, *slab)


def call(kernel, out_shape, *args):
    return pl.pallas_call(
        kernel,
        out_shape=out_shape,
        compiler_params=pltpu.CompilerParams(vmem_limit_bytes=VMEM_LIMIT),
    )(*args)


def add_kernel(n, got, keep, keep_count, *messages):
    for i, message in enumerate(messages):
        total, row = read_message(got, i * (n + TAIL), n)
        total = total + keep[i * n : (i + 1) * n, :]
        write_message(message, 0, total, row + keep_count[i * TAIL : (i + 1) * TAIL, :])


def add(got, keep, keep_count):
    n = keep_count.shape[1]
    shape = jax.ShapeDtypeStruct((n + TAIL, got.shape[1]), BF16)
    return call(functools.partial(add_kernel, n), (shape,) * (NX - 1), got, keep, keep_count)


def update_kernel(n, keep, keep_count, got, one, two, three, masses, centroids, new_centroids, new_masses):
    total, row = keep[...], keep_count[...]
    for message in (got, one, two, three):
        t, r = read_message(message, 0, n)
        total, row = total + t, row + r
    mass = masses[...]
    new = mass + row[:1]
    new_masses[...] = new
    column = lambda v: jnp.transpose(jnp.broadcast_to(v, (n, n)))[:, :1]
    new_centroids[...] = (column(mass) * centroids[...].astype(F32) + total) / column(new)


def update(keep, keep_count, got, others, masses, centroids):
    n, width = centroids.shape
    out = (jax.ShapeDtypeStruct((n, width), F32), jax.ShapeDtypeStruct((1, n), F32))
    return call(
        functools.partial(update_kernel, n), out, keep, keep_count, got, *others, masses.reshape(1, n), centroids
    )


def shards(embeddings, centroids, masses):
    y, c = lax.axis_index("y"), lax.axis_index("c")
    rows, width = embeddings.shape
    half, sub = rows // 2, rows // 4
    h = lax.rem(y, 2)
    place = jnp.concatenate([jnp.full((4, sub), c, F32), jnp.full((4, sub), h, F32)])
    place, embeddings = lax.optimization_barrier((place, embeddings))

    near = {0: centroids, 1: shift_x(centroids, -1), 3: shift_x(centroids, 1)}

    mine = lax.dynamic_slice_in_dim(embeddings, h * half, half, 0)
    one = along_z(mine, 1)
    own = lax.dynamic_slice_in_dim(embeddings.reshape(2, 2, sub, width), c, 1, 1).reshape(half, width)
    one, near[1], near[3] = lax.optimization_barrier((one, near[1], near[3]))
    near[2] = shift_x(near[1], -1)
    first = swap_halves(one)
    two = along_z(one, 1)
    two, near[2] = lax.optimization_barrier((two, near[2]))
    three = along_z(two, 1)
    two, first = lax.optimization_barrier((two, first))

    fixed = lambda v: pltpu.with_memory_space_constraint(v, pltpu.VMEM) if PIN else v
    table = [fixed(v) for d in ORDER for v in (near[d], swap_cores(near[d]))]

    four = along_z(lax.dynamic_slice_in_dim(three, c * sub, sub, 0), 1)
    lots = [[fixed(v) for v in (own, one, first, two, swap_halves(two))]]
    *table, scores, energy = score(table, lots[0])
    table, logits, local = [fixed(v) for v in table], [scores], [energy]
    last, _ = lax.optimization_barrier((four, energy))
    last = swap_halves(last)
    lots.append([fixed(v) for v in (three, swap_halves(three))])
    scores, energy = score(table, lots[1])
    last, _ = lax.optimization_barrier((last, energy))
    logits.append(scores)
    local.append(energy)
    lots.append([fixed(four), fixed(last)])
    scores, energy = score(table, lots[2])
    logits.append(scores)
    local.append(energy)
    energy, row_energy = energies(local, place, sub)
    logits, pieces = [fixed(v) for v in logits], [v for lot in lots for v in lot]

    message, keep, keep_count = weigh(0, NX - 1, logits, energy, pieces)
    sent = add(swap_cores(message), keep, keep_count)
    message, keep, keep_count = weigh(NX - 1, 1, logits, energy, pieces)
    others = [shift_x(m, d) for m, d in zip(sent, ORDER)]
    new_centroids, new_masses = update(keep, keep_count, swap_cores(message), others, masses, centroids)
    return new_centroids, new_masses.reshape(-1), row_energy


def solution(mesh):
    grid = Mesh(mesh.devices.reshape(NX, NZ, NY, NC), ("x", "z", "y", "c"))
    rows, cents = ("x", "z"), ("y", "c", "x", "z")
    return jax.shard_map(
        shards,
        mesh=grid,
        in_specs=(P(rows, None), P(cents, None), P(cents)),
        out_specs=(P(cents, None), P(cents), P(rows)),
        check_vma=False,
    )
```

```python
import functools

import jax
import jax.numpy as jnp
from jax import lax
from jax.experimental import pallas as pl
from jax.experimental.pallas import tpu as pltpu
from jax.sharding import Mesh, PartitionSpec as P

NX, NZ, NY, NC = 4, 8, 4, 2
BF16, F32 = jnp.bfloat16, jnp.float32
TAIL = 16
ORDER = (1, 3, 2, 0)
BATCH = 512
VMEM_LIMIT = 20 * 1024 * 1024
SMALL_LIMIT = 4 * 1024 * 1024
PIN = True


def shift_x(value, by):
    return lax.ppermute(value, "x", [(i, (i + by) % NX) for i in range(NX)])


def swap_cores(value):
    return lax.ppermute(value, "c", [(0, 1), (1, 0)])


def along_z(value, by):
    pairs = []
    for z in range(NZ):
        pairs.append((z * NC, (z + by) % NZ * NC))
        pairs.append((z * NC + 1, (z - by) % NZ * NC + 1))
    return lax.ppermute(value, ("z", "c"), pairs)


def shift_y(value, by):
    return lax.ppermute(value, "y", [(i, (i + by) % NY) for i in range(NY)])


def swap_halves(value):
    pairs = []
    for y in range(NY):
        pairs.append((y * NC, (y ^ 1) * NC))
        pairs.append((y * NC + 1, (y + 1 if y % 2 else y - 1) % NY * NC + 1))
    return lax.ppermute(value, ("y", "c"), pairs)


def combine(parts):
    high = functools.reduce(jnp.maximum, parts)
    return high + jnp.log(sum(jnp.exp(p - high) for p in parts))


def pick(place, first, second):
    return jnp.where(place == 0, first, second)


def small(kernel, place, out, *args):
    return pl.pallas_call(
        kernel,
        out_shape=[jax.ShapeDtypeStruct(shape, F32) for shape in out],
        compiler_params=pltpu.CompilerParams(vmem_limit_bytes=SMALL_LIMIT),
    )(place, *args)


def turn(v, by):
    by %= NZ
    return jnp.concatenate([v[:, NZ - by :], v[:, : NZ - by]], axis=1)


def pack_kernel(place, first, second, third, out):
    sub = out.shape[1]
    given = [v[:, k : k + sub] for v in (first, second, third) for k in range(0, v.shape[1], sub)]
    h = place[4:5, :]
    out[0:1, :] = given[0]
    out[1:2, :] = given[1]
    at = 2
    for mine, other in ((given[2:4], given[4:6]), (given[6:8], given[8:10]), (given[10:12], given[12:14]), (given[14:15], given[15:16])):
        for v, w in ((mine, other), (other, mine)):
            for i in range(len(v)):
                out[at : at + 1, :] = pick(h, v[i], w[i])
                at += 1


def sum_kernel(place, own, *refs):
    refs[-1][...] = combine([own[...]] + [v[...] for v in refs[:-1]])


def block_kernel(place, mine, other, out):
    c = place[0:1, :]
    back = lambda i: pick(c, mine[i : i + 1, :], other[i : i + 1, :])
    ahead = lambda i: pick(c, other[i : i + 1, :], mine[i : i + 1, :])
    for half in range(2):
        for sub in range(2):
            q = 2 * half + sub
            side = ahead if sub else back
            out[q, 0:1, :] = side(half)
            out[q, 4:5, :] = side(14 + half)
            for k in range(1, 4):
                out[q, k : k + 1, :] = ahead(4 * k - 2 + q)
                out[q, NZ - k : NZ - k + 1, :] = back(4 * k - 2 + q)


def near_kernel(place, block, near, far, three, message):
    c = place[0:1, :]
    own = block[...]
    from_back = turn(pick(c, near[...], far[...]), -1)
    from_ahead = turn(pick(c, far[...], near[...]), 1)
    both = combine([own, from_back, from_ahead])
    three[...] = both
    message[...] = pick(c, both, combine([own, from_back]))


def last_kernel(place, three, got, other, energy, own):
    c, h = place[0:1, :], place[4:5, :]
    from_back = turn(pick(c, got[...], other[...]), -3)
    from_ahead = turn(pick(c, other[...], got[...]), 3)
    block = combine([three[...], from_back, from_ahead])
    n = block.shape[2]
    own[...] = block[:, 0]

    def steps(half, step):
        return [pick(c, block[2 * half + i, NZ - step : NZ - step + 1], block[2 * half + i, step : step + 1]) for i in range(2)]

    out = [pick(c, block[2 * half, 0:1], block[2 * half + 1, 0:1]) for half in range(2)]
    for step in range(1, 4):
        low, top = steps(0, step), steps(1, step)
        out += [pick(h, low[i], top[i]) for i in range(2)] + [pick(h, top[i], low[i]) for i in range(2)]
    low, top = (pick(c, block[2 * half, 4:5], block[2 * half + 1, 4:5]) for half in range(2))
    out += [pick(h, low, top), pick(h, top, low)]
    for i, v in enumerate(out):
        energy[:, i * n : (i + 1) * n] = v


def energies(local, place, sub):
    (mine,) = small(pack_kernel, place, [(16, sub)], *local)
    (mine,) = small(sum_kernel, place, [(16, sub)], mine, *[shift_y(mine, d) for d in (1, 2, 3)])
    shape = (4, NZ, sub)
    (block,) = small(block_kernel, place, [shape], mine, swap_cores(mine))
    near = along_z(block, 1)
    three, message = small(near_kernel, place, [shape] * 2, block, near, swap_cores(near))
    got = along_z(message, 3)
    energy, own = small(last_kernel, place, [(1, 16 * sub), (4, sub)], three, got, swap_cores(got))
    return energy, own.reshape(-1)


def turned(column):
    n = column.shape[0]
    return jnp.transpose(jnp.broadcast_to(column, (n, n)))


def write_message(message, at, total, row):
    n, width = total.shape
    message[at : at + n, :] = total.astype(BF16)
    high = row.astype(BF16)
    tail = [high, (row - high.astype(F32)).astype(BF16)]
    if width > 2 * n:
        tail.append(jnp.zeros((TAIL, width - 2 * n), BF16))
    message[at + n : at + n + TAIL, :] = jnp.concatenate(tail, axis=1)


def read_message(message, at, n):
    total = message[at : at + n, :].astype(F32)
    tail = message[at + n : at + n + TAIL, :].astype(F32)
    return total, tail[:, :n] + tail[:, n : 2 * n]


def score_kernel(parts, sizes, *refs):
    if parts:
        table, pieces, (block, squares, logits, energy) = refs[:parts], refs[parts:-4], refs[-4:]
    else:
        block, squares, *pieces = refs[:-2]
        logits, energy = refs[-2:]
    height = block.shape[0]
    span = height // NX
    if parts:
        n = table[0].shape[0]
        for p in range(parts):
            lot = slice(p * n, (p + 1) * n)
            part = table[p][...]
            block[lot, :] = part
            wide = part.astype(F32)
            total = jnp.sum(wide * wide, axis=1, keepdims=True)
            squares[lot, :] = jnp.broadcast_to(total, (n, squares.shape[1]))
    batches, at = [[]], 0
    for piece, size in zip(pieces, sizes):
        if sum(k for _, k in batches[-1]) >= BATCH:
            batches.append([])
        batches[-1].append((piece, size))
    for batch in batches:
        rows = jnp.concatenate([piece[...] for piece, _ in batch])
        lot = slice(at, at + rows.shape[0])
        at += rows.shape[0]
        high = None
        for k in range(0, height, span):
            product = lax.dot_general(
                block[k : k + span, :], rows, (((1,), (1,)), ((), ())), preferred_element_type=F32
            )
            scores = 2.0 * product - squares[k : k + span, :1]
            logits[k : k + span, lot] = scores
            top = jnp.max(scores, axis=0, keepdims=True)
            high = top if high is None else jnp.maximum(high, top)
        total = None
        for k in range(0, height, span):
            part = jnp.sum(jnp.exp(logits[k : k + span, lot] - high), axis=0, keepdims=True)
            total = part if total is None else total + part
        energy[:, lot] = high + jnp.log(total)


def score(table, pieces):
    whole = len(table) == 2
    count = table[0].shape[0] if whole else sum(t.shape[0] for t in table)
    width, sizes = table[0].shape[1], tuple(p.shape[0] for p in pieces)
    rows = sum(sizes)
    out = [
        pltpu.VMEM((count, rows), F32) if PIN else jax.ShapeDtypeStruct((count, rows), F32),
        jax.ShapeDtypeStruct((1, rows), F32),
    ]
    if not whole:
        out = [jax.ShapeDtypeStruct((count, width), BF16), jax.ShapeDtypeStruct((count, 128), F32)] + out
    return pl.pallas_call(
        functools.partial(score_kernel, 0 if whole else len(table), sizes),
        out_shape=out,
        compiler_params=pltpu.CompilerParams(vmem_limit_bytes=VMEM_LIMIT),
        cost_estimate=pl.CostEstimate(
            flops=4 * count * rows * width,
            bytes_accessed=4 * count * rows + 2 * (count + rows) * width,
            transcendentals=count * rows,
        ),
    )(*table, *pieces)


def weigh_kernel(lots, groups, sizes, keeps, sends, energy, *refs):
    logits, refs = refs[: len(groups)], refs[len(groups) :]
    slab, out = refs[: len(sizes)], list(refs[len(sizes) :])
    n, width = logits[0].shape[0] // (NX * NC), slab[0].shape[1]
    step, tile = min(sizes), min(256, width)
    places, at, g, edge = [], 0, 0, 0
    for size in sizes:
        if at - edge == groups[g]:
            g, edge = g + 1, at
        places.append((logits[g], at - edge, at, size))
        at += size
    units = [[p] for p, size in enumerate(sizes) if size > step]
    units.append([p for p, size in enumerate(sizes) if size == step])
    counts, sets = [None] * len(lots), []
    for unit in units:
        parts = []
        for i, lot in enumerate(lots):
            row = []
            for ref, col, at, size in (places[p] for p in unit):
                for cut in range(0, size, step):
                    w = jnp.exp(ref[lot : lot + n, col + cut : col + cut + step] - energy[:, at + cut : at + cut + step])
                    counts[i] = w if counts[i] is None else counts[i] + w
                    row.append(w.astype(BF16))
            parts.append(jnp.concatenate(row, axis=1))
        sets.append(jnp.concatenate(parts))
    rows = [turned(jnp.sum(v, axis=1, keepdims=True))[:TAIL] for v in counts]
    message = out.pop(0) if sends else None
    if keeps:
        keep, keep_count = out
        for i in range(keeps):
            keep_count[i * TAIL : (i + 1) * TAIL, :] = rows[i]
    for i, row in enumerate(rows[keeps:]):
        at = i * (n + TAIL) + n
        high = row.astype(BF16)
        message[at : at + TAIL, :n] = high
        message[at : at + TAIL, n : 2 * n] = (row - high.astype(F32)).astype(BF16)
        if width > 2 * n:
            message[at : at + TAIL, 2 * n :] = jnp.zeros((TAIL, width - 2 * n), BF16)
    for at in range(0, width, tile):
        acc = None
        for unit, w in zip(units, sets):
            block = jnp.concatenate([slab[p][:, at : at + tile] for p in unit])
            term = jnp.dot(w, block, preferred_element_type=F32)
            acc = term if acc is None else acc + term
        if keeps:
            keep[:, at : at + tile] = acc[: keeps * n]
        for i in range(sends):
            part = acc[(keeps + i) * n : (keeps + i + 1) * n]
            message[i * (n + TAIL) : i * (n + TAIL) + n, at : at + tile] = part.astype(BF16)


def weigh(keeps, sends, logits, energy, slab):
    n, width = logits[0].shape[0] // (NX * NC), slab[0].shape[1]
    sizes, groups = tuple(p.shape[0] for p in slab), tuple(v.shape[1] for v in logits)
    lots = [k * NC * n for k in keeps] + [k * NC * n + n for k in sends]
    out = []
    if sends:
        out.append(jax.ShapeDtypeStruct((len(sends) * (n + TAIL), width), BF16))
    if keeps:
        out.append(jax.ShapeDtypeStruct((len(keeps) * n, width), F32))
        out.append(jax.ShapeDtypeStruct((len(keeps) * TAIL, n), F32))
    total, height = sum(sizes), len(lots) * n
    return pl.pallas_call(
        functools.partial(weigh_kernel, lots, groups, sizes, len(keeps), len(sends)),
        out_shape=out,
        compiler_params=pltpu.CompilerParams(vmem_limit_bytes=VMEM_LIMIT),
        cost_estimate=pl.CostEstimate(
            flops=2 * height * total * width,
            bytes_accessed=4 * height * total + 2 * total * width,
            transcendentals=height * total,
        ),
    )(energy, *logits, *slab)


def call(kernel, out_shape, *args):
    return pl.pallas_call(
        kernel,
        out_shape=out_shape,
        compiler_params=pltpu.CompilerParams(vmem_limit_bytes=VMEM_LIMIT),
    )(*args)


def add_kernel(n, got, keep, keep_count, *messages):
    for i, message in enumerate(messages):
        total, row = read_message(got, i * (n + TAIL), n)
        total = total + keep[i * n : (i + 1) * n, :]
        write_message(message, 0, total, row + keep_count[i * TAIL : (i + 1) * TAIL, :])


def add(got, keep, keep_count):
    n = keep_count.shape[1]
    shape = jax.ShapeDtypeStruct((n + TAIL, got.shape[1]), BF16)
    return call(functools.partial(add_kernel, n), (shape,) * (NX - 1), got, keep, keep_count)


def update_kernel(n, keep, keep_count, got, one, two, three, masses, centroids, new_centroids, new_masses):
    total, row = keep[...], keep_count[...]
    for message in (got, one, two, three):
        t, r = read_message(message, 0, n)
        total, row = total + t, row + r
    mass = masses[...]
    new = mass + row[:1]
    new_masses[...] = new
    column = lambda v: jnp.transpose(jnp.broadcast_to(v, (n, n)))[:, :1]
    new_centroids[...] = (column(mass) * centroids[...].astype(F32) + total) / column(new)


def update(keep, keep_count, got, others, masses, centroids):
    n, width = centroids.shape
    out = (jax.ShapeDtypeStruct((n, width), F32), jax.ShapeDtypeStruct((1, n), F32))
    return call(
        functools.partial(update_kernel, n), out, keep, keep_count, got, *others, masses.reshape(1, n), centroids
    )


def shards(embeddings, centroids, masses):
    y, c = lax.axis_index("y"), lax.axis_index("c")
    rows, width = embeddings.shape
    half, sub = rows // 2, rows // 4
    h = lax.rem(y, 2)
    place = jnp.concatenate([jnp.full((4, sub), c, F32), jnp.full((4, sub), h, F32)])
    place, embeddings = lax.optimization_barrier((place, embeddings))

    near = {0: centroids, 1: shift_x(centroids, -1), 3: shift_x(centroids, 1)}

    mine = lax.dynamic_slice_in_dim(embeddings, h * half, half, 0)
    one = along_z(mine, 1)
    own = lax.dynamic_slice_in_dim(embeddings.reshape(2, 2, sub, width), c, 1, 1).reshape(half, width)
    one, near[1], near[3] = lax.optimization_barrier((one, near[1], near[3]))
    near[2] = shift_x(near[1], -1)
    first = swap_halves(one)
    two = along_z(one, 1)
    two, near[2] = lax.optimization_barrier((two, near[2]))
    three = along_z(two, 1)
    two, first = lax.optimization_barrier((two, first))

    fixed = lambda v: pltpu.with_memory_space_constraint(v, pltpu.VMEM) if PIN else v
    table = [fixed(v) for d in ORDER for v in (near[d], swap_cores(near[d]))]

    four = along_z(lax.dynamic_slice_in_dim(three, c * sub, sub, 0), 1)
    lots = [[fixed(v) for v in (own, one, first, two, swap_halves(two))]]
    *table, scores, energy = score(table, lots[0])
    table, logits, local = [fixed(v) for v in table], [scores], [energy]
    last, _ = lax.optimization_barrier((four, energy))
    last = swap_halves(last)
    lots.append([fixed(v) for v in (three, swap_halves(three))])
    scores, energy = score(table, lots[1])
    last, _ = lax.optimization_barrier((last, energy))
    logits.append(scores)
    local.append(energy)
    lots.append([fixed(four), fixed(last)])
    scores, energy = score(table, lots[2])
    logits.append(scores)
    local.append(energy)
    energy, row_energy = energies(local, place, sub)
    logits, pieces = [fixed(v) for v in logits], [v for lot in lots for v in lot]

    sent = list(range(NX - 1))
    (message,) = weigh([], sent, logits, energy, pieces)
    got = swap_cores(message)
    keep, keep_count = weigh(sent, [], logits, energy, pieces)
    others = [shift_x(m, d) for m, d in zip(add(got, keep, keep_count), ORDER)]
    energy, others[0] = lax.optimization_barrier((energy, others[0]))
    message, keep, keep_count = weigh([NX - 1], [NX - 1], logits, energy, pieces)
    new_centroids, new_masses = update(keep, keep_count, swap_cores(message), others, masses, centroids)
    return new_centroids, new_masses.reshape(-1), row_energy


def solution(mesh):
    grid = Mesh(mesh.devices.reshape(NX, NZ, NY, NC), ("x", "z", "y", "c"))
    rows, cents = ("x", "z"), ("y", "c", "x", "z")
    return jax.shard_map(
        shards,
        mesh=grid,
        in_specs=(P(rows, None), P(cents, None), P(cents)),
        out_specs=(P(cents, None), P(cents), P(rows)),
        check_vma=False,
    )
```

```python
import functools

import jax
import jax.numpy as jnp
from jax import lax
from jax.experimental import pallas as pl
from jax.experimental.pallas import tpu as pltpu
from jax.sharding import Mesh, PartitionSpec as P

NX, NZ, NY, NC = 4, 8, 4, 2
BF16, F32 = jnp.bfloat16, jnp.float32
TAIL = 16
ORDER = (2, 1, 3, 0)
BATCH = 512
VMEM_LIMIT = 20 * 1024 * 1024
SMALL_LIMIT = 4 * 1024 * 1024
PIN = True


def shift_x(value, by):
    return lax.ppermute(value, "x", [(i, (i + by) % NX) for i in range(NX)])


def swap_cores(value):
    return lax.ppermute(value, "c", [(0, 1), (1, 0)])


def along_z(value, by):
    pairs = []
    for z in range(NZ):
        pairs.append((z * NC, (z + by) % NZ * NC))
        pairs.append((z * NC + 1, (z - by) % NZ * NC + 1))
    return lax.ppermute(value, ("z", "c"), pairs)


def shift_y(value, by):
    return lax.ppermute(value, "y", [(i, (i + by) % NY) for i in range(NY)])


def swap_halves(value):
    pairs = []
    for y in range(NY):
        pairs.append((y * NC, (y ^ 1) * NC))
        pairs.append((y * NC + 1, (y + 1 if y % 2 else y - 1) % NY * NC + 1))
    return lax.ppermute(value, ("y", "c"), pairs)


def combine(parts):
    high = functools.reduce(jnp.maximum, parts)
    return high + jnp.log(sum(jnp.exp(p - high) for p in parts))


def pick(place, first, second):
    return jnp.where(place == 0, first, second)


def small(kernel, place, out, *args):
    return pl.pallas_call(
        kernel,
        out_shape=[jax.ShapeDtypeStruct(shape, F32) for shape in out],
        compiler_params=pltpu.CompilerParams(vmem_limit_bytes=SMALL_LIMIT),
    )(place, *args)


def turn(v, by):
    by %= NZ
    return jnp.concatenate([v[:, NZ - by :], v[:, : NZ - by]], axis=1)


def pack_kernel(place, first, second, third, out):
    sub = out.shape[1]
    given = [v[:, k : k + sub] for v in (first, second, third) for k in range(0, v.shape[1], sub)]
    h = place[4:5, :]
    out[0:1, :] = given[0]
    out[1:2, :] = given[1]
    at = 2
    for mine, other in ((given[2:4], given[4:6]), (given[6:8], given[8:10]), (given[10:12], given[12:14]), (given[14:15], given[15:16])):
        for v, w in ((mine, other), (other, mine)):
            for i in range(len(v)):
                out[at : at + 1, :] = pick(h, v[i], w[i])
                at += 1


def sum_kernel(place, own, *refs):
    refs[-1][...] = combine([own[...]] + [v[...] for v in refs[:-1]])


def block_kernel(place, mine, other, out):
    c = place[0:1, :]
    back = lambda i: pick(c, mine[i : i + 1, :], other[i : i + 1, :])
    ahead = lambda i: pick(c, other[i : i + 1, :], mine[i : i + 1, :])
    for half in range(2):
        for sub in range(2):
            q = 2 * half + sub
            side = ahead if sub else back
            out[q, 0:1, :] = side(half)
            out[q, 4:5, :] = side(14 + half)
            for k in range(1, 4):
                out[q, k : k + 1, :] = ahead(4 * k - 2 + q)
                out[q, NZ - k : NZ - k + 1, :] = back(4 * k - 2 + q)


def near_kernel(place, block, near, far, three, message):
    c = place[0:1, :]
    own = block[...]
    from_back = turn(pick(c, near[...], far[...]), -1)
    from_ahead = turn(pick(c, far[...], near[...]), 1)
    both = combine([own, from_back, from_ahead])
    three[...] = both
    message[...] = pick(c, both, combine([own, from_back]))


def last_kernel(place, three, got, other, energy, own):
    c, h = place[0:1, :], place[4:5, :]
    from_back = turn(pick(c, got[...], other[...]), -3)
    from_ahead = turn(pick(c, other[...], got[...]), 3)
    block = combine([three[...], from_back, from_ahead])
    n = block.shape[2]
    own[...] = block[:, 0]

    def steps(half, step):
        return [pick(c, block[2 * half + i, NZ - step : NZ - step + 1], block[2 * half + i, step : step + 1]) for i in range(2)]

    out = [pick(c, block[2 * half, 0:1], block[2 * half + 1, 0:1]) for half in range(2)]
    for step in range(1, 4):
        low, top = steps(0, step), steps(1, step)
        out += [pick(h, low[i], top[i]) for i in range(2)] + [pick(h, top[i], low[i]) for i in range(2)]
    low, top = (pick(c, block[2 * half, 4:5], block[2 * half + 1, 4:5]) for half in range(2))
    out += [pick(h, low, top), pick(h, top, low)]
    for i, v in enumerate(out):
        energy[:, i * n : (i + 1) * n] = v


def energies(local, place, sub):
    (mine,) = small(pack_kernel, place, [(16, sub)], *local)
    (mine,) = small(sum_kernel, place, [(16, sub)], mine, *[shift_y(mine, d) for d in (1, 2, 3)])
    shape = (4, NZ, sub)
    (block,) = small(block_kernel, place, [shape], mine, swap_cores(mine))
    near = along_z(block, 1)
    three, message = small(near_kernel, place, [shape] * 2, block, near, swap_cores(near))
    got = along_z(message, 3)
    energy, own = small(last_kernel, place, [(1, 16 * sub), (4, sub)], three, got, swap_cores(got))
    return energy, own.reshape(-1)


def turned(column):
    n = column.shape[0]
    return jnp.transpose(jnp.broadcast_to(column, (n, n)))


def write_message(message, at, total, row):
    n, width = total.shape
    message[at : at + n, :] = total.astype(BF16)
    high = row.astype(BF16)
    tail = [high, (row - high.astype(F32)).astype(BF16)]
    if width > 2 * n:
        tail.append(jnp.zeros((TAIL, width - 2 * n), BF16))
    message[at + n : at + n + TAIL, :] = jnp.concatenate(tail, axis=1)


def read_message(message, at, n):
    total = message[at : at + n, :].astype(F32)
    tail = message[at + n : at + n + TAIL, :].astype(F32)
    return total, tail[:, :n] + tail[:, n : 2 * n]


def score_kernel(parts, sizes, *refs):
    if parts:
        table, pieces, (block, squares, logits, energy) = refs[:parts], refs[parts:-4], refs[-4:]
    else:
        block, squares, *pieces = refs[:-2]
        logits, energy = refs[-2:]
    height = block.shape[0]
    span = height // NX
    if parts:
        n = table[0].shape[0]
        for p in range(parts):
            lot = slice(p * n, (p + 1) * n)
            part = table[p][...]
            block[lot, :] = part
            wide = part.astype(F32)
            total = jnp.sum(wide * wide, axis=1, keepdims=True)
            squares[lot, :] = jnp.broadcast_to(total, (n, squares.shape[1]))
    batches, at = [[]], 0
    for piece, size in zip(pieces, sizes):
        if sum(k for _, k in batches[-1]) >= BATCH:
            batches.append([])
        batches[-1].append((piece, size))
    for batch in batches:
        rows = jnp.concatenate([piece[...] for piece, _ in batch])
        lot = slice(at, at + rows.shape[0])
        at += rows.shape[0]
        high = None
        for k in range(0, height, span):
            product = lax.dot_general(
                block[k : k + span, :], rows, (((1,), (1,)), ((), ())), preferred_element_type=F32
            )
            scores = 2.0 * product - squares[k : k + span, :1]
            logits[k : k + span, lot] = scores
            top = jnp.max(scores, axis=0, keepdims=True)
            high = top if high is None else jnp.maximum(high, top)
        total = None
        for k in range(0, height, span):
            part = jnp.sum(jnp.exp(logits[k : k + span, lot] - high), axis=0, keepdims=True)
            total = part if total is None else total + part
        energy[:, lot] = high + jnp.log(total)


def score(table, pieces):
    whole = len(table) == 2
    count = table[0].shape[0] if whole else sum(t.shape[0] for t in table)
    width, sizes = table[0].shape[1], tuple(p.shape[0] for p in pieces)
    rows = sum(sizes)
    out = [
        pltpu.VMEM((count, rows), F32) if PIN else jax.ShapeDtypeStruct((count, rows), F32),
        jax.ShapeDtypeStruct((1, rows), F32),
    ]
    if not whole:
        out = [jax.ShapeDtypeStruct((count, width), BF16), jax.ShapeDtypeStruct((count, 128), F32)] + out
    return pl.pallas_call(
        functools.partial(score_kernel, 0 if whole else len(table), sizes),
        out_shape=out,
        compiler_params=pltpu.CompilerParams(vmem_limit_bytes=VMEM_LIMIT),
        cost_estimate=pl.CostEstimate(
            flops=4 * count * rows * width,
            bytes_accessed=4 * count * rows + 2 * (count + rows) * width,
            transcendentals=count * rows,
        ),
    )(*table, *pieces)


def weigh_kernel(lots, groups, sizes, keeps, sends, energy, *refs):
    logits, refs = refs[: len(groups)], refs[len(groups) :]
    slab, out = refs[: len(sizes)], list(refs[len(sizes) :])
    n, width = logits[0].shape[0] // (NX * NC), slab[0].shape[1]
    step, tile = min(sizes), min(256, width)
    places, at, g, edge = [], 0, 0, 0
    for size in sizes:
        if at - edge == groups[g]:
            g, edge = g + 1, at
        places.append((logits[g], at - edge, at, size))
        at += size
    units = [[p] for p, size in enumerate(sizes) if size > step]
    units.append([p for p, size in enumerate(sizes) if size == step])
    units = [units[k] + units[k + 1] for k in range(0, len(units), 2)]
    message = out.pop(0) if sends else None
    if keeps:
        keep, keep_count, total = out
    else:
        (total,) = out
    counts = [None] * len(lots)
    for k, unit in enumerate(units):
        parts = []
        for i, lot in enumerate(lots):
            row = []
            for ref, col, at, size in (places[p] for p in unit):
                for cut in range(0, size, step):
                    w = jnp.exp(ref[lot : lot + n, col + cut : col + cut + step] - energy[:, at + cut : at + cut + step])
                    counts[i] = w if counts[i] is None else counts[i] + w
                    row.append(w.astype(BF16))
            parts.append(jnp.concatenate(row, axis=1))
        w = jnp.concatenate(parts)
        for at in range(0, width, tile):
            block = jnp.concatenate([slab[p][:, at : at + tile] for p in unit])
            term = jnp.dot(w, block, preferred_element_type=F32)
            if k:
                term = total[:, at : at + tile] + term
            if k < len(units) - 1:
                total[:, at : at + tile] = term
                continue
            if keeps:
                keep[:, at : at + tile] = term[: keeps * n]
            for i in range(sends):
                part = term[(keeps + i) * n : (keeps + i + 1) * n]
                message[i * (n + TAIL) : i * (n + TAIL) + n, at : at + tile] = part.astype(BF16)
    rows = [turned(jnp.sum(v, axis=1, keepdims=True))[:TAIL] for v in counts]
    for i, row in enumerate(rows[:keeps]):
        keep_count[i * TAIL : (i + 1) * TAIL, :] = row
    for i, row in enumerate(rows[keeps:]):
        at = i * (n + TAIL) + n
        high = row.astype(BF16)
        message[at : at + TAIL, :n] = high
        message[at : at + TAIL, n : 2 * n] = (row - high.astype(F32)).astype(BF16)
        if width > 2 * n:
            message[at : at + TAIL, 2 * n :] = jnp.zeros((TAIL, width - 2 * n), BF16)


def weigh(keeps, sends, logits, energy, slab):
    n, width = logits[0].shape[0] // (NX * NC), slab[0].shape[1]
    sizes, groups = tuple(p.shape[0] for p in slab), tuple(v.shape[1] for v in logits)
    lots = [k * NC * n for k in keeps] + [k * NC * n + n for k in sends]
    out = []
    if sends:
        out.append(jax.ShapeDtypeStruct((len(sends) * (n + TAIL), width), BF16))
    if keeps:
        out.append(jax.ShapeDtypeStruct((len(keeps) * n, width), F32))
        out.append(jax.ShapeDtypeStruct((len(keeps) * TAIL, n), F32))
    total, height = sum(sizes), len(lots) * n
    return pl.pallas_call(
        functools.partial(weigh_kernel, lots, groups, sizes, len(keeps), len(sends)),
        out_shape=out,
        scratch_shapes=[pltpu.VMEM((height, width), F32)],
        compiler_params=pltpu.CompilerParams(vmem_limit_bytes=VMEM_LIMIT),
        cost_estimate=pl.CostEstimate(
            flops=2 * height * total * width,
            bytes_accessed=4 * height * total + 2 * total * width,
            transcendentals=height * total,
        ),
    )(energy, *logits, *slab)


def call(kernel, out_shape, *args):
    return pl.pallas_call(
        kernel,
        out_shape=out_shape,
        compiler_params=pltpu.CompilerParams(vmem_limit_bytes=VMEM_LIMIT),
    )(*args)


def add_kernel(n, got, keep, keep_count, *messages):
    for i, message in enumerate(messages):
        total, row = read_message(got, i * (n + TAIL), n)
        total = total + keep[i * n : (i + 1) * n, :]
        write_message(message, 0, total, row + keep_count[i * TAIL : (i + 1) * TAIL, :])


def add(got, keep, keep_count):
    n = keep_count.shape[1]
    shape = jax.ShapeDtypeStruct((n + TAIL, got.shape[1]), BF16)
    return call(functools.partial(add_kernel, n), (shape,) * (NX - 1), got, keep, keep_count)


def update_kernel(n, keep, keep_count, got, one, two, three, masses, centroids, new_centroids, new_masses):
    total, row = keep[...], keep_count[...]
    for message in (got, one, two, three):
        t, r = read_message(message, 0, n)
        total, row = total + t, row + r
    mass = masses[...]
    new = mass + row[:1]
    new_masses[...] = new
    column = lambda v: jnp.transpose(jnp.broadcast_to(v, (n, n)))[:, :1]
    new_centroids[...] = (column(mass) * centroids[...].astype(F32) + total) / column(new)


def update(keep, keep_count, got, others, masses, centroids):
    n, width = centroids.shape
    out = (jax.ShapeDtypeStruct((n, width), F32), jax.ShapeDtypeStruct((1, n), F32))
    return call(
        functools.partial(update_kernel, n), out, keep, keep_count, got, *others, masses.reshape(1, n), centroids
    )


def shards(embeddings, centroids, masses):
    y, c = lax.axis_index("y"), lax.axis_index("c")
    rows, width = embeddings.shape
    half, sub = rows // 2, rows // 4
    h = lax.rem(y, 2)
    place = jnp.concatenate([jnp.full((4, sub), c, F32), jnp.full((4, sub), h, F32)])
    place, embeddings = lax.optimization_barrier((place, embeddings))

    near = {0: centroids, 1: shift_x(centroids, -1), 3: shift_x(centroids, 1)}

    mine = lax.dynamic_slice_in_dim(embeddings, h * half, half, 0)
    one = along_z(mine, 1)
    own = lax.dynamic_slice_in_dim(embeddings.reshape(2, 2, sub, width), c, 1, 1).reshape(half, width)
    one, near[1], near[3] = lax.optimization_barrier((one, near[1], near[3]))
    near[2] = shift_x(near[1], -1)
    first = swap_halves(one)
    two = along_z(one, 1)
    two, near[2] = lax.optimization_barrier((two, near[2]))
    three = along_z(two, 1)
    two, first = lax.optimization_barrier((two, first))

    fixed = lambda v: pltpu.with_memory_space_constraint(v, pltpu.VMEM) if PIN else v
    table = [fixed(v) for d in ORDER for v in (near[d], swap_cores(near[d]))]

    four = along_z(lax.dynamic_slice_in_dim(three, c * sub, sub, 0), 1)
    lots = [[fixed(v) for v in (own, one, first, two, swap_halves(two))]]
    *table, scores, energy = score(table, lots[0])
    table, logits, local = [fixed(v) for v in table], [scores], [energy]
    last, _ = lax.optimization_barrier((four, energy))
    last = swap_halves(last)
    lots.append([fixed(v) for v in (three, swap_halves(three))])
    scores, energy = score(table, lots[1])
    last, _ = lax.optimization_barrier((last, energy))
    logits.append(scores)
    local.append(energy)
    lots.append([fixed(four), fixed(last)])
    scores, energy = score(table, lots[2])
    logits.append(scores)
    local.append(energy)
    energy, row_energy = energies(local, place, sub)
    logits, pieces = [fixed(v) for v in logits], [v for lot in lots for v in lot]

    sent = list(range(NX - 1))
    (message,) = weigh([], sent, logits, energy, pieces)
    got = swap_cores(message)
    keep, keep_count = weigh(sent, [], logits, energy, pieces)
    others = [shift_x(m, d) for m, d in zip(add(got, keep, keep_count), ORDER)]
    energy, others[0] = lax.optimization_barrier((energy, others[0]))
    message, keep, keep_count = weigh([NX - 1], [NX - 1], logits, energy, pieces)
    new_centroids, new_masses = update(keep, keep_count, swap_cores(message), others, masses, centroids)
    return new_centroids, new_masses.reshape(-1), row_energy


def solution(mesh):
    grid = Mesh(mesh.devices.reshape(NX, NZ, NY, NC), ("x", "z", "y", "c"))
    rows, cents = ("x", "z"), ("y", "c", "x", "z")
    return jax.shard_map(
        shards,
        mesh=grid,
        in_specs=(P(rows, None), P(cents, None), P(cents)),
        out_specs=(P(cents, None), P(cents), P(rows)),
        check_vma=False,
    )
```

```python
import functools

import jax
import jax.numpy as jnp
from jax import lax
from jax.experimental import pallas as pl
from jax.experimental.pallas import tpu as pltpu
from jax.sharding import Mesh, PartitionSpec as P

NX, NZ, NY, NC = 4, 8, 4, 2
BF16, F32 = jnp.bfloat16, jnp.float32
TAIL = 16
ORDER = (2, 1, 3, 0)
BATCH = 512
VMEM_LIMIT = 20 * 1024 * 1024
SMALL_LIMIT = 4 * 1024 * 1024
PIN = True


def shift_x(value, by):
    return lax.ppermute(value, "x", [(i, (i + by) % NX) for i in range(NX)])


def swap_cores(value):
    return lax.ppermute(value, "c", [(0, 1), (1, 0)])


def along_z(value, by):
    pairs = []
    for z in range(NZ):
        pairs.append((z * NC, (z + by) % NZ * NC))
        pairs.append((z * NC + 1, (z - by) % NZ * NC + 1))
    return lax.ppermute(value, ("z", "c"), pairs)


def shift_y(value, by):
    return lax.ppermute(value, "y", [(i, (i + by) % NY) for i in range(NY)])


def swap_halves(value):
    pairs = []
    for y in range(NY):
        pairs.append((y * NC, (y ^ 1) * NC))
        pairs.append((y * NC + 1, (y + 1 if y % 2 else y - 1) % NY * NC + 1))
    return lax.ppermute(value, ("y", "c"), pairs)


def combine(parts):
    high = functools.reduce(jnp.maximum, parts)
    return high + jnp.log(sum(jnp.exp(p - high) for p in parts))


def pick(place, first, second):
    return jnp.where(place == 0, first, second)


def small(kernel, place, out, *args):
    return pl.pallas_call(
        kernel,
        out_shape=[jax.ShapeDtypeStruct(shape, F32) for shape in out],
        compiler_params=pltpu.CompilerParams(vmem_limit_bytes=SMALL_LIMIT),
    )(place, *args)


def turn(v, by):
    by %= NZ
    return jnp.concatenate([v[:, NZ - by :], v[:, : NZ - by]], axis=1)


def pack_kernel(place, first, second, third, out):
    sub = out.shape[1]
    given = [v[:, k : k + sub] for v in (first, second, third) for k in range(0, v.shape[1], sub)]
    h = place[4:5, :]
    out[0:1, :] = given[0]
    out[1:2, :] = given[1]
    at = 2
    for mine, other in ((given[2:4], given[4:6]), (given[6:8], given[8:10]), (given[10:12], given[12:14]), (given[14:15], given[15:16])):
        for v, w in ((mine, other), (other, mine)):
            for i in range(len(v)):
                out[at : at + 1, :] = pick(h, v[i], w[i])
                at += 1


def sum_kernel(place, own, *refs):
    refs[-1][...] = combine([own[...]] + [v[...] for v in refs[:-1]])


def block_kernel(place, mine, other, out):
    c = place[0:1, :]
    back = lambda i: pick(c, mine[i : i + 1, :], other[i : i + 1, :])
    ahead = lambda i: pick(c, other[i : i + 1, :], mine[i : i + 1, :])
    for half in range(2):
        for sub in range(2):
            q = 2 * half + sub
            side = ahead if sub else back
            out[q, 0:1, :] = side(half)
            out[q, 4:5, :] = side(14 + half)
            for k in range(1, 4):
                out[q, k : k + 1, :] = ahead(4 * k - 2 + q)
                out[q, NZ - k : NZ - k + 1, :] = back(4 * k - 2 + q)


def near_kernel(place, block, near, far, three, message):
    c = place[0:1, :]
    own = block[...]
    from_back = turn(pick(c, near[...], far[...]), -1)
    from_ahead = turn(pick(c, far[...], near[...]), 1)
    both = combine([own, from_back, from_ahead])
    three[...] = both
    message[...] = pick(c, both, combine([own, from_back]))


def last_kernel(place, three, got, other, energy, own):
    c, h = place[0:1, :], place[4:5, :]
    from_back = turn(pick(c, got[...], other[...]), -3)
    from_ahead = turn(pick(c, other[...], got[...]), 3)
    block = combine([three[...], from_back, from_ahead])
    n = block.shape[2]
    own[...] = block[:, 0]

    def steps(half, step):
        return [pick(c, block[2 * half + i, NZ - step : NZ - step + 1], block[2 * half + i, step : step + 1]) for i in range(2)]

    out = [pick(c, block[2 * half, 0:1], block[2 * half + 1, 0:1]) for half in range(2)]
    for step in range(1, 4):
        low, top = steps(0, step), steps(1, step)
        out += [pick(h, low[i], top[i]) for i in range(2)] + [pick(h, top[i], low[i]) for i in range(2)]
    low, top = (pick(c, block[2 * half, 4:5], block[2 * half + 1, 4:5]) for half in range(2))
    out += [pick(h, low, top), pick(h, top, low)]
    for i, v in enumerate(out):
        energy[:, i * n : (i + 1) * n] = v


def energies(local, place, sub):
    (mine,) = small(pack_kernel, place, [(16, sub)], *local)
    (mine,) = small(sum_kernel, place, [(16, sub)], mine, *[shift_y(mine, d) for d in (1, 2, 3)])
    shape = (4, NZ, sub)
    (block,) = small(block_kernel, place, [shape], mine, swap_cores(mine))
    near = along_z(block, 1)
    three, message = small(near_kernel, place, [shape] * 2, block, near, swap_cores(near))
    got = along_z(message, 3)
    energy, own = small(last_kernel, place, [(1, 16 * sub), (4, sub)], three, got, swap_cores(got))
    return energy, own.reshape(-1)


def turned(column):
    n = column.shape[0]
    return jnp.transpose(jnp.broadcast_to(column, (n, n)))


def write_message(message, at, total, row):
    n, width = total.shape
    message[at : at + n, :] = total.astype(BF16)
    high = row.astype(BF16)
    tail = [high, (row - high.astype(F32)).astype(BF16)]
    if width > 2 * n:
        tail.append(jnp.zeros((TAIL, width - 2 * n), BF16))
    message[at + n : at + n + TAIL, :] = jnp.concatenate(tail, axis=1)


def read_message(message, at, n):
    total = message[at : at + n, :].astype(F32)
    tail = message[at + n : at + n + TAIL, :].astype(F32)
    return total, tail[:, :n] + tail[:, n : 2 * n]


def score_kernel(parts, sizes, *refs):
    if parts:
        table, pieces, (block, squares, logits, energy) = refs[:parts], refs[parts:-4], refs[-4:]
    else:
        block, squares, *pieces = refs[:-2]
        logits, energy = refs[-2:]
    height = block.shape[0]
    span = height // NX
    if parts:
        n = table[0].shape[0]
        for p in range(parts):
            lot = slice(p * n, (p + 1) * n)
            part = table[p][...]
            block[lot, :] = part
            wide = part.astype(F32)
            total = jnp.sum(wide * wide, axis=1, keepdims=True)
            squares[lot, :] = jnp.broadcast_to(total, (n, squares.shape[1]))
    batches, at = [[]], 0
    for piece, size in zip(pieces, sizes):
        if sum(k for _, k in batches[-1]) >= BATCH:
            batches.append([])
        batches[-1].append((piece, size))
    for batch in batches:
        rows = jnp.concatenate([piece[...] for piece, _ in batch])
        lot = slice(at, at + rows.shape[0])
        at += rows.shape[0]
        high = None
        for k in range(0, height, span):
            product = lax.dot_general(
                block[k : k + span, :], rows, (((1,), (1,)), ((), ())), preferred_element_type=F32
            )
            scores = 2.0 * product - squares[k : k + span, :1]
            logits[k : k + span, lot] = scores
            top = jnp.max(scores, axis=0, keepdims=True)
            high = top if high is None else jnp.maximum(high, top)
        total = None
        for k in range(0, height, span):
            part = jnp.sum(jnp.exp(logits[k : k + span, lot] - high), axis=0, keepdims=True)
            total = part if total is None else total + part
        energy[:, lot] = high + jnp.log(total)


def score(table, pieces):
    whole = len(table) == 2
    count = table[0].shape[0] if whole else sum(t.shape[0] for t in table)
    width, sizes = table[0].shape[1], tuple(p.shape[0] for p in pieces)
    rows = sum(sizes)
    out = [
        pltpu.VMEM((count, rows), F32) if PIN else jax.ShapeDtypeStruct((count, rows), F32),
        jax.ShapeDtypeStruct((1, rows), F32),
    ]
    if not whole:
        out = [jax.ShapeDtypeStruct((count, width), BF16), jax.ShapeDtypeStruct((count, 128), F32)] + out
    return pl.pallas_call(
        functools.partial(score_kernel, 0 if whole else len(table), sizes),
        out_shape=out,
        compiler_params=pltpu.CompilerParams(vmem_limit_bytes=VMEM_LIMIT),
        cost_estimate=pl.CostEstimate(
            flops=4 * count * rows * width,
            bytes_accessed=4 * count * rows + 2 * (count + rows) * width,
            transcendentals=count * rows,
        ),
    )(*table, *pieces)


def weigh_kernel(lots, groups, sizes, keeps, sends, energy, *refs):
    logits, refs = refs[: len(groups)], refs[len(groups) :]
    slab, out = refs[: len(sizes)], list(refs[len(sizes) :])
    n, width = logits[0].shape[0] // (NX * NC), slab[0].shape[1]
    step, tile = min(sizes), min(256, width)
    places, at, g, edge = [], 0, 0, 0
    for size in sizes:
        if at - edge == groups[g]:
            g, edge = g + 1, at
        places.append((logits[g], at - edge, at, size))
        at += size
    units = [[p] for p, size in enumerate(sizes) if size > step]
    units.append([p for p, size in enumerate(sizes) if size == step])
    units = [units[k] + units[k + 1] for k in range(0, len(units), 2)]
    message = out.pop(0) if sends else None
    if keeps:
        keep, keep_count, total = out
    else:
        (total,) = out
    counts = [None] * len(lots)
    for k, unit in enumerate(units):
        parts = []
        for i, lot in enumerate(lots):
            row = []
            for ref, col, at, size in (places[p] for p in unit):
                for cut in range(0, size, step):
                    w = jnp.exp(ref[lot : lot + n, col + cut : col + cut + step] - energy[:, at + cut : at + cut + step])
                    counts[i] = w if counts[i] is None else counts[i] + w
                    row.append(w.astype(BF16))
            parts.append(jnp.concatenate(row, axis=1))
        w = jnp.concatenate(parts)
        for at in range(0, width, tile):
            block = jnp.concatenate([slab[p][:, at : at + tile] for p in unit])
            term = jnp.dot(w, block, preferred_element_type=F32)
            if k:
                term = total[:, at : at + tile] + term
            if k < len(units) - 1:
                total[:, at : at + tile] = term
                continue
            if keeps:
                keep[:, at : at + tile] = term[: keeps * n]
            for i in range(sends):
                part = term[(keeps + i) * n : (keeps + i + 1) * n]
                message[i * (n + TAIL) : i * (n + TAIL) + n, at : at + tile] = part.astype(BF16)
    rows = [turned(jnp.sum(v, axis=1, keepdims=True))[:TAIL] for v in counts]
    for i, row in enumerate(rows[:keeps]):
        keep_count[i * TAIL : (i + 1) * TAIL, :] = row
    for i, row in enumerate(rows[keeps:]):
        at = i * (n + TAIL) + n
        high = row.astype(BF16)
        message[at : at + TAIL, :n] = high
        message[at : at + TAIL, n : 2 * n] = (row - high.astype(F32)).astype(BF16)
        if width > 2 * n:
            message[at : at + TAIL, 2 * n :] = jnp.zeros((TAIL, width - 2 * n), BF16)


def weigh(keeps, sends, logits, energy, slab):
    n, width = logits[0].shape[0] // (NX * NC), slab[0].shape[1]
    sizes, groups = tuple(p.shape[0] for p in slab), tuple(v.shape[1] for v in logits)
    lots = [k * NC * n for k in keeps] + [k * NC * n + n for k in sends]
    out = []
    if sends:
        out.append(jax.ShapeDtypeStruct((len(sends) * (n + TAIL), width), BF16))
    if keeps:
        out.append(jax.ShapeDtypeStruct((len(keeps) * n, width), F32))
        out.append(jax.ShapeDtypeStruct((len(keeps) * TAIL, n), F32))
    total, height = sum(sizes), len(lots) * n
    return pl.pallas_call(
        functools.partial(weigh_kernel, lots, groups, sizes, len(keeps), len(sends)),
        out_shape=out,
        scratch_shapes=[pltpu.VMEM((height, width), F32)],
        compiler_params=pltpu.CompilerParams(vmem_limit_bytes=VMEM_LIMIT),
        cost_estimate=pl.CostEstimate(
            flops=2 * height * total * width,
            bytes_accessed=4 * height * total + 2 * total * width,
            transcendentals=height * total,
        ),
    )(energy, *logits, *slab)


def call(kernel, out_shape, *args):
    return pl.pallas_call(
        kernel,
        out_shape=out_shape,
        compiler_params=pltpu.CompilerParams(vmem_limit_bytes=VMEM_LIMIT),
    )(*args)


def add_kernel(n, got, keep, keep_count, *messages):
    for i, message in enumerate(messages):
        total, row = read_message(got, i * (n + TAIL), n)
        total = total + keep[i * n : (i + 1) * n, :]
        write_message(message, 0, total, row + keep_count[i * TAIL : (i + 1) * TAIL, :])


def add(got, keep, keep_count):
    n = keep_count.shape[1]
    shape = jax.ShapeDtypeStruct((n + TAIL, got.shape[1]), BF16)
    return call(functools.partial(add_kernel, n), (shape,) * (NX - 1), got, keep, keep_count)


def update_kernel(n, keep, keep_count, got, one, two, three, masses, centroids, new_centroids, new_masses):
    total, row = keep[...], keep_count[...]
    for message in (got, one, two, three):
        t, r = read_message(message, 0, n)
        total, row = total + t, row + r
    mass = masses[...]
    new = mass + row[:1]
    new_masses[...] = new
    column = lambda v: jnp.transpose(jnp.broadcast_to(v, (n, n)))[:, :1]
    new_centroids[...] = (column(mass) * centroids[...].astype(F32) + total) / column(new)


def update(keep, keep_count, got, others, masses, centroids):
    n, width = centroids.shape
    out = (jax.ShapeDtypeStruct((n, width), F32), jax.ShapeDtypeStruct((1, n), F32))
    return call(
        functools.partial(update_kernel, n), out, keep, keep_count, got, *others, masses.reshape(1, n), centroids
    )


def shards(embeddings, centroids, masses):
    y, c = lax.axis_index("y"), lax.axis_index("c")
    rows, width = embeddings.shape
    half, sub = rows // 2, rows // 4
    h = lax.rem(y, 2)
    place = jnp.concatenate([jnp.full((4, sub), c, F32), jnp.full((4, sub), h, F32)])
    core, start_c, start_h = (v.astype(jnp.uint32) for v in (c, c * sub, h * half))
    place, embeddings, core, start_c, start_h = lax.optimization_barrier((place, embeddings, core, start_c, start_h))

    near = {0: centroids, 1: shift_x(centroids, -1), 3: shift_x(centroids, 1)}

    mine = lax.dynamic_slice_in_dim(embeddings, start_h, half, 0)
    one = along_z(mine, 1)
    own = lax.dynamic_slice_in_dim(embeddings.reshape(2, 2, sub, width), core, 1, 1).reshape(half, width)
    one, near[1], near[3] = lax.optimization_barrier((one, near[1], near[3]))
    near[2] = shift_x(near[1], -1)
    first = swap_halves(one)
    two = along_z(one, 1)
    two, near[2] = lax.optimization_barrier((two, near[2]))
    three = along_z(two, 1)
    two, first = lax.optimization_barrier((two, first))

    fixed = lambda v: pltpu.with_memory_space_constraint(v, pltpu.VMEM) if PIN else v
    table = [fixed(v) for d in ORDER for v in (near[d], swap_cores(near[d]))]

    four = along_z(lax.dynamic_slice_in_dim(three, start_c, sub, 0), 1)
    lots = [[fixed(v) for v in (own, one, first, two, swap_halves(two))]]
    *table, scores, energy = score(table, lots[0])
    table, logits, local = [fixed(v) for v in table], [scores], [energy]
    last, _ = lax.optimization_barrier((four, energy))
    last = swap_halves(last)
    lots.append([fixed(v) for v in (three, swap_halves(three))])
    scores, energy = score(table, lots[1])
    last, _ = lax.optimization_barrier((last, energy))
    logits.append(scores)
    local.append(energy)
    lots.append([fixed(four), fixed(last)])
    scores, energy = score(table, lots[2])
    logits.append(scores)
    local.append(energy)
    energy, row_energy = energies(local, place, sub)
    logits, pieces = [fixed(v) for v in logits], [v for lot in lots for v in lot]

    sent = list(range(NX - 1))
    (message,) = weigh([], sent, logits, energy, pieces)
    got = swap_cores(message)
    keep, keep_count = weigh(sent, [], logits, energy, pieces)
    others = [shift_x(m, d) for m, d in zip(add(got, keep, keep_count), ORDER)]
    energy, others[0] = lax.optimization_barrier((energy, others[0]))
    message, keep, keep_count = weigh([NX - 1], [NX - 1], logits, energy, pieces)
    new_centroids, new_masses = update(keep, keep_count, swap_cores(message), others, masses, centroids)
    return new_centroids, new_masses.reshape(-1), row_energy


def solution(mesh):
    grid = Mesh(mesh.devices.reshape(NX, NZ, NY, NC), ("x", "z", "y", "c"))
    rows, cents = ("x", "z"), ("y", "c", "x", "z")
    return jax.shard_map(
        shards,
        mesh=grid,
        in_specs=(P(rows, None), P(cents, None), P(cents)),
        out_specs=(P(cents, None), P(cents), P(rows)),
        check_vma=False,
    )
```

```python
import functools

import jax
import jax.numpy as jnp
from jax import lax
from jax.experimental import pallas as pl
from jax.experimental.pallas import tpu as pltpu
from jax.sharding import Mesh, PartitionSpec as P

NX, NZ, NY, NC = 4, 8, 4, 2
BF16, F32 = jnp.bfloat16, jnp.float32
TAIL = 16
ORDER = (2, 1, 3, 0)
BATCH = 512
VMEM_LIMIT = 20 * 1024 * 1024
SMALL_LIMIT = 4 * 1024 * 1024
PIN = True


def shift_x(value, by):
    return lax.ppermute(value, "x", [(i, (i + by) % NX) for i in range(NX)])


def swap_cores(value):
    return lax.ppermute(value, "c", [(0, 1), (1, 0)])


def along_z(value, by):
    pairs = []
    for z in range(NZ):
        pairs.append((z * NC, (z + by) % NZ * NC))
        pairs.append((z * NC + 1, (z - by) % NZ * NC + 1))
    return lax.ppermute(value, ("z", "c"), pairs)


def shift_y(value, by):
    return lax.ppermute(value, "y", [(i, (i + by) % NY) for i in range(NY)])


def swap_halves(value):
    pairs = []
    for y in range(NY):
        pairs.append((y * NC, (y ^ 1) * NC))
        pairs.append((y * NC + 1, (y + 1 if y % 2 else y - 1) % NY * NC + 1))
    return lax.ppermute(value, ("y", "c"), pairs)


def combine(parts):
    high = functools.reduce(jnp.maximum, parts)
    return high + jnp.log(sum(jnp.exp(p - high) for p in parts))


def from_partner(value):
    pairs = []
    for z in range(NZ):
        for y in range(NY):
            for c, to, side in ((0, z + 1, y ^ 1), (1, z - 1, (y + 1 if y % 2 else y - 1) % NY)):
                pairs.append(((z * NY + y) * NC + c, (to % NZ * NY + side) * NC + c))
    return lax.ppermute(value, ("z", "y", "c"), pairs)


def pick(place, first, second):
    return jnp.where(place == 0, first, second)


def small(kernel, place, out, *args):
    return pl.pallas_call(
        kernel,
        out_shape=[jax.ShapeDtypeStruct(shape, F32) for shape in out],
        compiler_params=pltpu.CompilerParams(vmem_limit_bytes=SMALL_LIMIT),
    )(place, *args)


def turn(v, by):
    by %= NZ
    return jnp.concatenate([v[:, NZ - by :], v[:, : NZ - by]], axis=1)


def pack_kernel(place, first, second, third, out):
    sub = out.shape[1]
    given = [v[:, k : k + sub] for v in (first, second, third) for k in range(0, v.shape[1], sub)]
    h = place[4:5, :]
    out[0:1, :] = given[0]
    out[1:2, :] = given[1]
    at = 2
    for mine, other in ((given[2:4], given[4:6]), (given[6:8], given[8:10]), (given[10:12], given[12:14]), (given[14:15], given[15:16])):
        for v, w in ((mine, other), (other, mine)):
            for i in range(len(v)):
                out[at : at + 1, :] = pick(h, v[i], w[i])
                at += 1


def sum_kernel(place, own, *refs):
    refs[-1][...] = combine([own[...]] + [v[...] for v in refs[:-1]])


def block_kernel(place, mine, other, out):
    c = place[0:1, :]
    back = lambda i: pick(c, mine[i : i + 1, :], other[i : i + 1, :])
    ahead = lambda i: pick(c, other[i : i + 1, :], mine[i : i + 1, :])
    for half in range(2):
        for sub in range(2):
            q = 2 * half + sub
            side = ahead if sub else back
            out[q, 0:1, :] = side(half)
            out[q, 4:5, :] = side(14 + half)
            for k in range(1, 4):
                out[q, k : k + 1, :] = ahead(4 * k - 2 + q)
                out[q, NZ - k : NZ - k + 1, :] = back(4 * k - 2 + q)


def near_kernel(place, block, near, far, three, message):
    c = place[0:1, :]
    own = block[...]
    from_back = turn(pick(c, near[...], far[...]), -1)
    from_ahead = turn(pick(c, far[...], near[...]), 1)
    both = combine([own, from_back, from_ahead])
    three[...] = both
    message[...] = pick(c, both, combine([own, from_back]))


def last_kernel(place, three, got, other, energy, own):
    c, h = place[0:1, :], place[4:5, :]
    from_back = turn(pick(c, got[...], other[...]), -3)
    from_ahead = turn(pick(c, other[...], got[...]), 3)
    block = combine([three[...], from_back, from_ahead])
    n = block.shape[2]
    own[...] = block[:, 0]

    def steps(half, step):
        return [pick(c, block[2 * half + i, NZ - step : NZ - step + 1], block[2 * half + i, step : step + 1]) for i in range(2)]

    out = [pick(c, block[2 * half, 0:1], block[2 * half + 1, 0:1]) for half in range(2)]
    for step in range(1, 4):
        low, top = steps(0, step), steps(1, step)
        out += [pick(h, low[i], top[i]) for i in range(2)] + [pick(h, top[i], low[i]) for i in range(2)]
    low, top = (pick(c, block[2 * half, 4:5], block[2 * half + 1, 4:5]) for half in range(2))
    out += [pick(h, low, top), pick(h, top, low)]
    for i, v in enumerate(out):
        energy[:, i * n : (i + 1) * n] = v


def energies(local, place, sub):
    (mine,) = small(pack_kernel, place, [(16, sub)], *local)
    (mine,) = small(sum_kernel, place, [(16, sub)], mine, *[shift_y(mine, d) for d in (1, 2, 3)])
    shape = (4, NZ, sub)
    (block,) = small(block_kernel, place, [shape], mine, swap_cores(mine))
    near = along_z(block, 1)
    three, message = small(near_kernel, place, [shape] * 2, block, near, swap_cores(near))
    got = along_z(message, 3)
    energy, own = small(last_kernel, place, [(1, 16 * sub), (4, sub)], three, got, swap_cores(got))
    return energy, own.reshape(-1)


def turned(column):
    n = column.shape[0]
    return jnp.transpose(jnp.broadcast_to(column, (n, n)))


def write_message(message, at, total, row):
    n, width = total.shape
    message[at : at + n, :] = total.astype(BF16)
    high = row.astype(BF16)
    tail = [high, (row - high.astype(F32)).astype(BF16)]
    if width > 2 * n:
        tail.append(jnp.zeros((TAIL, width - 2 * n), BF16))
    message[at + n : at + n + TAIL, :] = jnp.concatenate(tail, axis=1)


def read_message(message, at, n):
    total = message[at : at + n, :].astype(F32)
    tail = message[at + n : at + n + TAIL, :].astype(F32)
    return total, tail[:, :n] + tail[:, n : 2 * n]


def score_kernel(parts, sizes, *refs):
    if parts:
        table, pieces, (block, squares, logits, energy) = refs[:parts], refs[parts:-4], refs[-4:]
    else:
        block, squares, *pieces = refs[:-2]
        logits, energy = refs[-2:]
    height = block.shape[0]
    span = height // NX
    if parts:
        n = table[0].shape[0]
        for p in range(parts):
            lot = slice(p * n, (p + 1) * n)
            part = table[p][...]
            block[lot, :] = part
            wide = part.astype(F32)
            total = jnp.sum(wide * wide, axis=1, keepdims=True)
            squares[lot, :] = jnp.broadcast_to(total, (n, squares.shape[1]))
    batches, at = [[]], 0
    for piece, size in zip(pieces, sizes):
        if sum(k for _, k in batches[-1]) >= BATCH:
            batches.append([])
        batches[-1].append((piece, size))
    for batch in batches:
        rows = jnp.concatenate([piece[...] for piece, _ in batch])
        lot = slice(at, at + rows.shape[0])
        at += rows.shape[0]
        high = None
        for k in range(0, height, span):
            product = lax.dot_general(
                block[k : k + span, :], rows, (((1,), (1,)), ((), ())), preferred_element_type=F32
            )
            scores = 2.0 * product - squares[k : k + span, :1]
            logits[k : k + span, lot] = scores
            top = jnp.max(scores, axis=0, keepdims=True)
            high = top if high is None else jnp.maximum(high, top)
        total = None
        for k in range(0, height, span):
            part = jnp.sum(jnp.exp(logits[k : k + span, lot] - high), axis=0, keepdims=True)
            total = part if total is None else total + part
        energy[:, lot] = high + jnp.log(total)


def score(table, pieces):
    whole = len(table) == 2
    count = table[0].shape[0] if whole else sum(t.shape[0] for t in table)
    width, sizes = table[0].shape[1], tuple(p.shape[0] for p in pieces)
    rows = sum(sizes)
    out = [
        pltpu.VMEM((count, rows), F32) if PIN else jax.ShapeDtypeStruct((count, rows), F32),
        jax.ShapeDtypeStruct((1, rows), F32),
    ]
    if not whole:
        out = [jax.ShapeDtypeStruct((count, width), BF16), jax.ShapeDtypeStruct((count, 128), F32)] + out
    return pl.pallas_call(
        functools.partial(score_kernel, 0 if whole else len(table), sizes),
        out_shape=out,
        compiler_params=pltpu.CompilerParams(vmem_limit_bytes=VMEM_LIMIT),
        cost_estimate=pl.CostEstimate(
            flops=4 * count * rows * width,
            bytes_accessed=4 * count * rows + 2 * (count + rows) * width,
            transcendentals=count * rows,
        ),
    )(*table, *pieces)


def weigh_kernel(lots, groups, sizes, keeps, sends, energy, *refs):
    logits, refs = refs[: len(groups)], refs[len(groups) :]
    slab, out = refs[: len(sizes)], list(refs[len(sizes) :])
    n, width = logits[0].shape[0] // (NX * NC), slab[0].shape[1]
    step, tile = min(sizes), min(256, width)
    places, at, g, edge = [], 0, 0, 0
    for size in sizes:
        if at - edge == groups[g]:
            g, edge = g + 1, at
        places.append((logits[g], at - edge, at, size))
        at += size
    units = [[p] for p, size in enumerate(sizes) if size > step]
    units.append([p for p, size in enumerate(sizes) if size == step])
    units = [units[k] + units[k + 1] for k in range(0, len(units), 2)]
    message = out.pop(0) if sends else None
    if keeps:
        keep, keep_count, total = out
    else:
        (total,) = out
    counts = [None] * len(lots)
    for k, unit in enumerate(units):
        parts = []
        for i, lot in enumerate(lots):
            row = []
            for ref, col, at, size in (places[p] for p in unit):
                for cut in range(0, size, step):
                    w = jnp.exp(ref[lot : lot + n, col + cut : col + cut + step] - energy[:, at + cut : at + cut + step])
                    counts[i] = w if counts[i] is None else counts[i] + w
                    row.append(w.astype(BF16))
            parts.append(jnp.concatenate(row, axis=1))
        w = jnp.concatenate(parts)
        for at in range(0, width, tile):
            block = jnp.concatenate([slab[p][:, at : at + tile] for p in unit])
            term = jnp.dot(w, block, preferred_element_type=F32)
            if k:
                term = total[:, at : at + tile] + term
            if k < len(units) - 1:
                total[:, at : at + tile] = term
                continue
            if keeps:
                keep[:, at : at + tile] = term[: keeps * n]
            for i in range(sends):
                part = term[(keeps + i) * n : (keeps + i + 1) * n]
                message[i * (n + TAIL) : i * (n + TAIL) + n, at : at + tile] = part.astype(BF16)
    rows = [turned(jnp.sum(v, axis=1, keepdims=True))[:TAIL] for v in counts]
    for i, row in enumerate(rows[:keeps]):
        keep_count[i * TAIL : (i + 1) * TAIL, :] = row
    for i, row in enumerate(rows[keeps:]):
        at = i * (n + TAIL) + n
        high = row.astype(BF16)
        message[at : at + TAIL, :n] = high
        message[at : at + TAIL, n : 2 * n] = (row - high.astype(F32)).astype(BF16)
        if width > 2 * n:
            message[at : at + TAIL, 2 * n :] = jnp.zeros((TAIL, width - 2 * n), BF16)


def weigh(keeps, sends, logits, energy, slab):
    n, width = logits[0].shape[0] // (NX * NC), slab[0].shape[1]
    sizes, groups = tuple(p.shape[0] for p in slab), tuple(v.shape[1] for v in logits)
    lots = [k * NC * n for k in keeps] + [k * NC * n + n for k in sends]
    out = []
    if sends:
        out.append(jax.ShapeDtypeStruct((len(sends) * (n + TAIL), width), BF16))
    if keeps:
        out.append(jax.ShapeDtypeStruct((len(keeps) * n, width), F32))
        out.append(jax.ShapeDtypeStruct((len(keeps) * TAIL, n), F32))
    total, height = sum(sizes), len(lots) * n
    return pl.pallas_call(
        functools.partial(weigh_kernel, lots, groups, sizes, len(keeps), len(sends)),
        out_shape=out,
        scratch_shapes=[pltpu.VMEM((height, width), F32)],
        compiler_params=pltpu.CompilerParams(vmem_limit_bytes=VMEM_LIMIT),
        cost_estimate=pl.CostEstimate(
            flops=2 * height * total * width,
            bytes_accessed=4 * height * total + 2 * total * width,
            transcendentals=height * total,
        ),
    )(energy, *logits, *slab)


def call(kernel, out_shape, *args):
    return pl.pallas_call(
        kernel,
        out_shape=out_shape,
        compiler_params=pltpu.CompilerParams(vmem_limit_bytes=VMEM_LIMIT),
    )(*args)


def add_kernel(n, got, keep, keep_count, *messages):
    for i, message in enumerate(messages):
        total, row = read_message(got, i * (n + TAIL), n)
        total = total + keep[i * n : (i + 1) * n, :]
        write_message(message, 0, total, row + keep_count[i * TAIL : (i + 1) * TAIL, :])


def add(got, keep, keep_count):
    n = keep_count.shape[1]
    shape = jax.ShapeDtypeStruct((n + TAIL, got.shape[1]), BF16)
    return call(functools.partial(add_kernel, n), (shape,) * (NX - 1), got, keep, keep_count)


def update_kernel(n, keep, keep_count, got, one, two, three, masses, centroids, new_centroids, new_masses):
    total, row = keep[...], keep_count[...]
    for message in (got, one, two, three):
        t, r = read_message(message, 0, n)
        total, row = total + t, row + r
    mass = masses[...]
    new = mass + row[:1]
    new_masses[...] = new
    column = lambda v: jnp.transpose(jnp.broadcast_to(v, (n, n)))[:, :1]
    new_centroids[...] = (column(mass) * centroids[...].astype(F32) + total) / column(new)


def update(keep, keep_count, got, others, masses, centroids):
    n, width = centroids.shape
    out = (jax.ShapeDtypeStruct((n, width), F32), jax.ShapeDtypeStruct((1, n), F32))
    return call(
        functools.partial(update_kernel, n), out, keep, keep_count, got, *others, masses.reshape(1, n), centroids
    )


def shards(embeddings, centroids, masses):
    y, c = lax.axis_index("y"), lax.axis_index("c")
    rows, width = embeddings.shape
    half, sub = rows // 2, rows // 4
    h = lax.rem(y, 2)
    place = jnp.concatenate([jnp.full((4, sub), c, F32), jnp.full((4, sub), h, F32)])
    core, start_c, start_h = (v.astype(jnp.uint32) for v in (c, c * sub, h * half))
    place, embeddings, core, start_c, start_h = lax.optimization_barrier((place, embeddings, core, start_c, start_h))

    near = {0: centroids, 1: shift_x(centroids, -1), 3: shift_x(centroids, 1)}

    mine = lax.dynamic_slice_in_dim(embeddings, start_h, half, 0)
    one = along_z(mine, 1)
    own = lax.dynamic_slice_in_dim(embeddings.reshape(2, 2, sub, width), core, 1, 1).reshape(half, width)
    one, near[1], near[3] = lax.optimization_barrier((one, near[1], near[3]))
    near[2] = shift_x(near[1], -1)
    first = swap_halves(one)
    two = along_z(one, 1)
    two, near[2] = lax.optimization_barrier((two, near[2]))
    three = along_z(two, 1)
    two, first = lax.optimization_barrier((two, first))

    fixed = lambda v: pltpu.with_memory_space_constraint(v, pltpu.VMEM) if PIN else v
    table = [fixed(v) for d in ORDER for v in (near[d], swap_cores(near[d]))]

    sides = [swap_halves(two), swap_halves(three)]
    part = lax.dynamic_slice_in_dim(three, start_c, sub, 0)
    four, last = along_z(part, 1), from_partner(part)
    lots = [[fixed(v) for v in (own, one, first, two, sides[0])]]
    *table, scores, energy = score(table, lots[0])
    table, logits, local = [fixed(v) for v in table], [scores], [energy]
    sides[1], _ = lax.optimization_barrier((sides[1], energy))
    lots.append([fixed(v) for v in (three, sides[1])])
    scores, energy = score(table, lots[1])
    last, _ = lax.optimization_barrier((last, energy))
    logits.append(scores)
    local.append(energy)
    lots.append([fixed(four), fixed(last)])
    scores, energy = score(table, lots[2])
    logits.append(scores)
    local.append(energy)
    energy, row_energy = energies(local, place, sub)
    logits, pieces = [fixed(v) for v in logits], [v for lot in lots for v in lot]

    sent = list(range(NX - 1))
    (message,) = weigh([], sent, logits, energy, pieces)
    got = swap_cores(message)
    keep, keep_count = weigh(sent, [], logits, energy, pieces)
    others = [shift_x(m, d) for m, d in zip(add(got, keep, keep_count), ORDER)]
    energy, others[0] = lax.optimization_barrier((energy, others[0]))
    message, keep, keep_count = weigh([NX - 1], [NX - 1], logits, energy, pieces)
    new_centroids, new_masses = update(keep, keep_count, swap_cores(message), others, masses, centroids)
    return new_centroids, new_masses.reshape(-1), row_energy


def solution(mesh):
    grid = Mesh(mesh.devices.reshape(NX, NZ, NY, NC), ("x", "z", "y", "c"))
    rows, cents = ("x", "z"), ("y", "c", "x", "z")
    return jax.shard_map(
        shards,
        mesh=grid,
        in_specs=(P(rows, None), P(cents, None), P(cents)),
        out_specs=(P(cents, None), P(cents), P(rows)),
        check_vma=False,
    )
```

```python
import functools

import jax
import jax.numpy as jnp
from jax import lax
from jax.experimental import pallas as pl
from jax.experimental.pallas import tpu as pltpu
from jax.sharding import Mesh, PartitionSpec as P

NX, NZ, NY, NC = 4, 8, 4, 2
BF16, F32 = jnp.bfloat16, jnp.float32
TAIL = 16
ORDER = (2, 1, 3, 0)
BATCH = 512
VMEM_LIMIT = 20 * 1024 * 1024
SMALL_LIMIT = 4 * 1024 * 1024
PIN = True


def shift_x(value, by):
    return lax.ppermute(value, "x", [(i, (i + by) % NX) for i in range(NX)])


def swap_cores(value):
    return lax.ppermute(value, "c", [(0, 1), (1, 0)])


def along_z(value, by):
    pairs = []
    for z in range(NZ):
        pairs.append((z * NC, (z + by) % NZ * NC))
        pairs.append((z * NC + 1, (z - by) % NZ * NC + 1))
    return lax.ppermute(value, ("z", "c"), pairs)


def shift_y(value, by):
    return lax.ppermute(value, "y", [(i, (i + by) % NY) for i in range(NY)])


def swap_halves(value):
    pairs = []
    for y in range(NY):
        pairs.append((y * NC, (y ^ 1) * NC))
        pairs.append((y * NC + 1, (y + 1 if y % 2 else y - 1) % NY * NC + 1))
    return lax.ppermute(value, ("y", "c"), pairs)


def combine(parts):
    high = functools.reduce(jnp.maximum, parts)
    return high + jnp.log(sum(jnp.exp(p - high) for p in parts))


def from_partner(value):
    pairs = []
    for z in range(NZ):
        for y in range(NY):
            for c, to, side in ((0, z + 1, y ^ 1), (1, z - 1, (y + 1 if y % 2 else y - 1) % NY)):
                pairs.append(((z * NY + y) * NC + c, (to % NZ * NY + side) * NC + c))
    return lax.ppermute(value, ("z", "y", "c"), pairs)


def pick(place, first, second):
    return jnp.where(place == 0, first, second)


def small(kernel, place, out, *args):
    return pl.pallas_call(
        kernel,
        out_shape=[jax.ShapeDtypeStruct(shape, F32) for shape in out],
        compiler_params=pltpu.CompilerParams(vmem_limit_bytes=SMALL_LIMIT),
    )(place, *args)


def turn(v, by):
    by %= NZ
    return jnp.concatenate([v[:, NZ - by :], v[:, : NZ - by]], axis=1)


def pack_kernel(place, first, second, third, out):
    sub = out.shape[1]
    given = [v[:, k : k + sub] for v in (first, second, third) for k in range(0, v.shape[1], sub)]
    h = place[4:5, :]
    out[0:1, :] = given[0]
    out[1:2, :] = given[1]
    at = 2
    for mine, other in ((given[2:4], given[4:6]), (given[6:8], given[8:10]), (given[10:12], given[12:14]), (given[14:15], given[15:16])):
        for v, w in ((mine, other), (other, mine)):
            for i in range(len(v)):
                out[at : at + 1, :] = pick(h, v[i], w[i])
                at += 1


def sum_kernel(place, own, *refs):
    refs[-1][...] = combine([own[...]] + [v[...] for v in refs[:-1]])


def block_kernel(place, mine, other, out):
    c = place[0:1, :]
    back = lambda i: pick(c, mine[i : i + 1, :], other[i : i + 1, :])
    ahead = lambda i: pick(c, other[i : i + 1, :], mine[i : i + 1, :])
    for half in range(2):
        for sub in range(2):
            q = 2 * half + sub
            side = ahead if sub else back
            out[q, 0:1, :] = side(half)
            out[q, 4:5, :] = side(14 + half)
            for k in range(1, 4):
                out[q, k : k + 1, :] = ahead(4 * k - 2 + q)
                out[q, NZ - k : NZ - k + 1, :] = back(4 * k - 2 + q)


def near_kernel(place, block, near, far, three, message):
    c = place[0:1, :]
    own = block[...]
    from_back = turn(pick(c, near[...], far[...]), -1)
    from_ahead = turn(pick(c, far[...], near[...]), 1)
    both = combine([own, from_back, from_ahead])
    three[...] = both
    message[...] = pick(c, both, combine([own, from_back]))


def last_kernel(place, three, got, other, energy, own):
    c, h = place[0:1, :], place[4:5, :]
    from_back = turn(pick(c, got[...], other[...]), -3)
    from_ahead = turn(pick(c, other[...], got[...]), 3)
    block = combine([three[...], from_back, from_ahead])
    n = block.shape[2]
    own[...] = block[:, 0]

    def steps(half, step):
        return [pick(c, block[2 * half + i, NZ - step : NZ - step + 1], block[2 * half + i, step : step + 1]) for i in range(2)]

    out = [pick(c, block[2 * half, 0:1], block[2 * half + 1, 0:1]) for half in range(2)]
    for step in range(1, 4):
        low, top = steps(0, step), steps(1, step)
        out += [pick(h, low[i], top[i]) for i in range(2)] + [pick(h, top[i], low[i]) for i in range(2)]
    low, top = (pick(c, block[2 * half, 4:5], block[2 * half + 1, 4:5]) for half in range(2))
    out += [pick(h, low, top), pick(h, top, low)]
    for i, v in enumerate(out):
        energy[:, i * n : (i + 1) * n] = v


def energies(local, place, sub):
    (mine,) = small(pack_kernel, place, [(16, sub)], *local)
    (mine,) = small(sum_kernel, place, [(16, sub)], mine, *[shift_y(mine, d) for d in (1, 2, 3)])
    shape = (4, NZ, sub)
    (block,) = small(block_kernel, place, [shape], mine, swap_cores(mine))
    near = along_z(block, 1)
    three, message = small(near_kernel, place, [shape] * 2, block, near, swap_cores(near))
    got = along_z(message, 3)
    energy, own = small(last_kernel, place, [(1, 16 * sub), (4, sub)], three, got, swap_cores(got))
    return energy, own.reshape(-1)


def turned(column):
    n = column.shape[0]
    return jnp.transpose(jnp.broadcast_to(column, (n, n)))


def write_message(message, at, total, row):
    n, width = total.shape
    message[at : at + n, :] = total.astype(BF16)
    high = row.astype(BF16)
    tail = [high, (row - high.astype(F32)).astype(BF16)]
    if width > 2 * n:
        tail.append(jnp.zeros((TAIL, width - 2 * n), BF16))
    message[at + n : at + n + TAIL, :] = jnp.concatenate(tail, axis=1)


def read_message(message, at, n):
    total = message[at : at + n, :].astype(F32)
    tail = message[at + n : at + n + TAIL, :].astype(F32)
    return total, tail[:, :n] + tail[:, n : 2 * n]


def score_kernel(parts, sizes, *refs):
    if parts:
        table, pieces, (block, squares, logits, energy) = refs[:parts], refs[parts:-4], refs[-4:]
    else:
        block, squares, *pieces = refs[:-2]
        logits, energy = refs[-2:]
    height = block.shape[0]
    span = height // NX
    if parts:
        n = table[0].shape[0]
        for p in range(parts):
            lot = slice(p * n, (p + 1) * n)
            part = table[p][...]
            block[lot, :] = part
            wide = part.astype(F32)
            total = jnp.sum(wide * wide, axis=1, keepdims=True)
            squares[lot, :] = jnp.broadcast_to(total, (n, squares.shape[1]))
    batches, at = [[]], 0
    for piece, size in zip(pieces, sizes):
        if sum(k for _, k in batches[-1]) >= BATCH:
            batches.append([])
        batches[-1].append((piece, size))
    for batch in batches:
        rows = jnp.concatenate([piece[...] for piece, _ in batch])
        lot = slice(at, at + rows.shape[0])
        at += rows.shape[0]
        high = None
        for k in range(0, height, span):
            product = lax.dot_general(
                block[k : k + span, :], rows, (((1,), (1,)), ((), ())), preferred_element_type=F32
            )
            scores = 2.0 * product - squares[k : k + span, :1]
            logits[k : k + span, lot] = scores
            top = jnp.max(scores, axis=0, keepdims=True)
            high = top if high is None else jnp.maximum(high, top)
        total = None
        for k in range(0, height, span):
            part = jnp.sum(jnp.exp(logits[k : k + span, lot] - high), axis=0, keepdims=True)
            total = part if total is None else total + part
        energy[:, lot] = high + jnp.log(total)


def score(table, pieces):
    whole = len(table) == 2
    count = table[0].shape[0] if whole else sum(t.shape[0] for t in table)
    width, sizes = table[0].shape[1], tuple(p.shape[0] for p in pieces)
    rows = sum(sizes)
    out = [
        pltpu.VMEM((count, rows), F32) if PIN else jax.ShapeDtypeStruct((count, rows), F32),
        jax.ShapeDtypeStruct((1, rows), F32),
    ]
    if not whole:
        out = [jax.ShapeDtypeStruct((count, width), BF16), jax.ShapeDtypeStruct((count, 128), F32)] + out
    return pl.pallas_call(
        functools.partial(score_kernel, 0 if whole else len(table), sizes),
        out_shape=out,
        compiler_params=pltpu.CompilerParams(vmem_limit_bytes=VMEM_LIMIT),
        cost_estimate=pl.CostEstimate(
            flops=4 * count * rows * width,
            bytes_accessed=4 * count * rows + 2 * (count + rows) * width,
            transcendentals=count * rows,
        ),
    )(*table, *pieces)


def weigh_kernel(lots, groups, sizes, keeps, sends, energy, *refs):
    logits, refs = refs[: len(groups)], refs[len(groups) :]
    slab, out = refs[: len(sizes)], list(refs[len(sizes) :])
    n, width = logits[0].shape[0] // (NX * NC), slab[0].shape[1]
    step, tile = min(sizes), min(256, width)
    places, at, g, edge = [], 0, 0, 0
    for size in sizes:
        if at - edge == groups[g]:
            g, edge = g + 1, at
        places.append((logits[g], at - edge, at, size))
        at += size
    units = [[p] for p, size in enumerate(sizes) if size > step]
    units.append([p for p, size in enumerate(sizes) if size == step])
    units = [units[k] + units[k + 1] for k in range(0, len(units), 2)]
    message = out.pop(0) if sends else None
    if keeps:
        keep, keep_count, total = out
    else:
        (total,) = out
    counts = [None] * len(lots)
    for k, unit in enumerate(units):
        parts = []
        for i, lot in enumerate(lots):
            row = []
            for ref, col, at, size in (places[p] for p in unit):
                for cut in range(0, size, step):
                    w = jnp.exp(ref[lot : lot + n, col + cut : col + cut + step] - energy[:, at + cut : at + cut + step])
                    counts[i] = w if counts[i] is None else counts[i] + w
                    row.append(w.astype(BF16))
            parts.append(jnp.concatenate(row, axis=1))
        w = jnp.concatenate(parts)
        for at in range(0, width, tile):
            block = jnp.concatenate([slab[p][:, at : at + tile] for p in unit])
            term = jnp.dot(w, block, preferred_element_type=F32)
            if k:
                term = total[:, at : at + tile] + term
            if k < len(units) - 1:
                total[:, at : at + tile] = term
                continue
            if keeps:
                keep[:, at : at + tile] = term[: keeps * n]
            for i in range(sends):
                part = term[(keeps + i) * n : (keeps + i + 1) * n]
                message[i * (n + TAIL) : i * (n + TAIL) + n, at : at + tile] = part.astype(BF16)
    rows = [turned(jnp.sum(v, axis=1, keepdims=True))[:TAIL] for v in counts]
    for i, row in enumerate(rows[:keeps]):
        keep_count[i * TAIL : (i + 1) * TAIL, :] = row
    for i, row in enumerate(rows[keeps:]):
        at = i * (n + TAIL) + n
        high = row.astype(BF16)
        message[at : at + TAIL, :n] = high
        message[at : at + TAIL, n : 2 * n] = (row - high.astype(F32)).astype(BF16)
        if width > 2 * n:
            message[at : at + TAIL, 2 * n :] = jnp.zeros((TAIL, width - 2 * n), BF16)


def weigh(keeps, sends, logits, energy, slab):
    n, width = logits[0].shape[0] // (NX * NC), slab[0].shape[1]
    sizes, groups = tuple(p.shape[0] for p in slab), tuple(v.shape[1] for v in logits)
    lots = [k * NC * n for k in keeps] + [k * NC * n + n for k in sends]
    out = []
    if sends:
        out.append(jax.ShapeDtypeStruct((len(sends) * (n + TAIL), width), BF16))
    if keeps:
        out.append(jax.ShapeDtypeStruct((len(keeps) * n, width), F32))
        out.append(jax.ShapeDtypeStruct((len(keeps) * TAIL, n), F32))
    total, height = sum(sizes), len(lots) * n
    return pl.pallas_call(
        functools.partial(weigh_kernel, lots, groups, sizes, len(keeps), len(sends)),
        out_shape=out,
        scratch_shapes=[pltpu.VMEM((height, width), F32)],
        compiler_params=pltpu.CompilerParams(vmem_limit_bytes=VMEM_LIMIT),
        cost_estimate=pl.CostEstimate(
            flops=2 * height * total * width,
            bytes_accessed=4 * height * total + 2 * total * width,
            transcendentals=height * total,
        ),
    )(energy, *logits, *slab)


def call(kernel, out_shape, *args):
    return pl.pallas_call(
        kernel,
        out_shape=out_shape,
        compiler_params=pltpu.CompilerParams(vmem_limit_bytes=VMEM_LIMIT),
    )(*args)


def add_kernel(n, got, keep, keep_count, *messages):
    for i, message in enumerate(messages):
        total, row = read_message(got, i * (n + TAIL), n)
        total = total + keep[i * n : (i + 1) * n, :]
        write_message(message, 0, total, row + keep_count[i * TAIL : (i + 1) * TAIL, :])


def add(got, keep, keep_count):
    n = keep_count.shape[1]
    shape = jax.ShapeDtypeStruct((n + TAIL, got.shape[1]), BF16)
    return call(functools.partial(add_kernel, n), (shape,) * (NX - 1), got, keep, keep_count)


def update_kernel(n, keep, keep_count, got, one, two, three, masses, centroids, new_centroids, new_masses):
    total, row = keep[...], keep_count[...]
    for message in (got, one, two, three):
        t, r = read_message(message, 0, n)
        total, row = total + t, row + r
    mass = masses[...]
    new = mass + row[:1]
    new_masses[...] = new
    column = lambda v: jnp.transpose(jnp.broadcast_to(v, (n, n)))[:, :1]
    new_centroids[...] = (column(mass) * centroids[...].astype(F32) + total) / column(new)


def update(keep, keep_count, got, others, masses, centroids):
    n, width = centroids.shape
    out = (jax.ShapeDtypeStruct((n, width), F32), jax.ShapeDtypeStruct((1, n), F32))
    return call(
        functools.partial(update_kernel, n), out, keep, keep_count, got, *others, masses.reshape(1, n), centroids
    )


def shards(embeddings, centroids, masses):
    y, c = lax.axis_index("y"), lax.axis_index("c")
    rows, width = embeddings.shape
    half, sub = rows // 2, rows // 4
    h = lax.rem(y, 2)
    place = jnp.concatenate([jnp.full((4, sub), c, F32), jnp.full((4, sub), h, F32)])
    core, start_c, start_h = (v.astype(jnp.uint32) for v in (c, c * sub, h * half))
    place, embeddings, core, start_c, start_h = lax.optimization_barrier((place, embeddings, core, start_c, start_h))

    near = {0: centroids, 1: shift_x(centroids, -1), 3: shift_x(centroids, 1)}

    mine = lax.dynamic_slice_in_dim(embeddings, start_h, half, 0)
    one = along_z(mine, 1)
    own = lax.dynamic_slice_in_dim(embeddings.reshape(2, 2, sub, width), core, 1, 1).reshape(half, width)
    one, near[1], near[3] = lax.optimization_barrier((one, near[1], near[3]))
    near[2] = shift_x(near[1], -1)
    first = swap_halves(one)
    two = along_z(one, 1)
    two, near[2] = lax.optimization_barrier((two, near[2]))
    three = along_z(two, 1)
    two, first = lax.optimization_barrier((two, first))

    fixed = lambda v: pltpu.with_memory_space_constraint(v, pltpu.VMEM) if PIN else v
    table = [fixed(v) for d in ORDER for v in (near[d], swap_cores(near[d]))]

    sides = [swap_halves(two), swap_halves(three)]
    part, *table = lax.optimization_barrier([three, *table])
    part = lax.dynamic_slice_in_dim(part, start_c, sub, 0)
    four, last = along_z(part, 1), from_partner(part)
    lots = [[fixed(v) for v in (own, one, first, two, sides[0])]]
    *table, scores, energy = score(table, lots[0])
    table, logits, local = [fixed(v) for v in table], [scores], [energy]
    middle, _ = lax.optimization_barrier((three, energy))
    lots.append([fixed(middle)])
    scores, energy = score(table, lots[1])
    last, _ = lax.optimization_barrier((last, energy))
    logits.append(scores)
    local.append(energy)
    lots.append([fixed(sides[1]), fixed(four), fixed(last)])
    scores, energy = score(table, lots[2])
    logits.append(scores)
    local.append(energy)
    energy, row_energy = energies(local, place, sub)
    logits, pieces = [fixed(v) for v in logits], [v for lot in lots for v in lot]

    sent = list(range(NX - 1))
    (message,) = weigh([], sent, logits, energy, pieces)
    got = swap_cores(message)
    keep, keep_count = weigh(sent, [], logits, energy, pieces)
    others = [shift_x(m, d) for m, d in zip(add(got, keep, keep_count), ORDER)]
    energy, others[0] = lax.optimization_barrier((energy, others[0]))
    message, keep, keep_count = weigh([NX - 1], [NX - 1], logits, energy, pieces)
    new_centroids, new_masses = update(keep, keep_count, swap_cores(message), others, masses, centroids)
    return new_centroids, new_masses.reshape(-1), row_energy


def solution(mesh):
    grid = Mesh(mesh.devices.reshape(NX, NZ, NY, NC), ("x", "z", "y", "c"))
    rows, cents = ("x", "z"), ("y", "c", "x", "z")
    return jax.shard_map(
        shards,
        mesh=grid,
        in_specs=(P(rows, None), P(cents, None), P(cents)),
        out_specs=(P(cents, None), P(cents), P(rows)),
        check_vma=False,
    )
```

```python
import functools

import jax
import jax.numpy as jnp
from jax import lax
from jax.experimental import pallas as pl
from jax.experimental.pallas import tpu as pltpu
from jax.sharding import Mesh, PartitionSpec as P

NX, NZ, NY, NC = 4, 8, 4, 2
BF16, F32 = jnp.bfloat16, jnp.float32
TAIL = 16
ORDER = (2, 1, 3, 0)
BATCH = 512
VMEM_LIMIT = 20 * 1024 * 1024
SMALL_LIMIT = 4 * 1024 * 1024
PIN = True


def shift_x(value, by):
    return lax.ppermute(value, "x", [(i, (i + by) % NX) for i in range(NX)])


def swap_cores(value):
    return lax.ppermute(value, "c", [(0, 1), (1, 0)])


def along_z(value, by):
    pairs = []
    for z in range(NZ):
        pairs.append((z * NC, (z + by) % NZ * NC))
        pairs.append((z * NC + 1, (z - by) % NZ * NC + 1))
    return lax.ppermute(value, ("z", "c"), pairs)


def shift_y(value, by):
    return lax.ppermute(value, "y", [(i, (i + by) % NY) for i in range(NY)])


def swap_halves(value):
    pairs = []
    for y in range(NY):
        pairs.append((y * NC, (y ^ 1) * NC))
        pairs.append((y * NC + 1, (y + 1 if y % 2 else y - 1) % NY * NC + 1))
    return lax.ppermute(value, ("y", "c"), pairs)


def combine(parts):
    high = functools.reduce(jnp.maximum, parts)
    return high + jnp.log(sum(jnp.exp(p - high) for p in parts))


def from_partner(value):
    pairs = []
    for z in range(NZ):
        for y in range(NY):
            for c, to, side in ((0, z + 1, y ^ 1), (1, z - 1, (y + 1 if y % 2 else y - 1) % NY)):
                pairs.append(((z * NY + y) * NC + c, (to % NZ * NY + side) * NC + c))
    return lax.ppermute(value, ("z", "y", "c"), pairs)


def pick(place, first, second):
    return jnp.where(place == 0, first, second)


def small(kernel, place, out, *args):
    return pl.pallas_call(
        kernel,
        out_shape=[jax.ShapeDtypeStruct(shape, F32) for shape in out],
        compiler_params=pltpu.CompilerParams(vmem_limit_bytes=SMALL_LIMIT),
    )(place, *args)


def turn(v, by):
    by %= NZ
    return jnp.concatenate([v[:, NZ - by :], v[:, : NZ - by]], axis=1)


def pack_kernel(place, first, second, third, out):
    sub = out.shape[1]
    given = [v[:, k : k + sub] for v in (first, second, third) for k in range(0, v.shape[1], sub)]
    h = place[4:5, :]
    out[0:1, :] = given[0]
    out[1:2, :] = given[1]
    at = 2
    for mine, other in ((given[2:4], given[4:6]), (given[6:8], given[8:10]), (given[10:12], given[12:14]), (given[14:15], given[15:16])):
        for v, w in ((mine, other), (other, mine)):
            for i in range(len(v)):
                out[at : at + 1, :] = pick(h, v[i], w[i])
                at += 1


def sum_kernel(place, own, *refs):
    refs[-1][...] = combine([own[...]] + [v[...] for v in refs[:-1]])


def block_kernel(place, mine, other, out):
    c = place[0:1, :]
    back = lambda i: pick(c, mine[i : i + 1, :], other[i : i + 1, :])
    ahead = lambda i: pick(c, other[i : i + 1, :], mine[i : i + 1, :])
    for half in range(2):
        for sub in range(2):
            q = 2 * half + sub
            side = ahead if sub else back
            out[q, 0:1, :] = side(half)
            out[q, 4:5, :] = side(14 + half)
            for k in range(1, 4):
                out[q, k : k + 1, :] = ahead(4 * k - 2 + q)
                out[q, NZ - k : NZ - k + 1, :] = back(4 * k - 2 + q)


def near_kernel(place, block, near, far, three, message):
    c = place[0:1, :]
    own = block[...]
    from_back = turn(pick(c, near[...], far[...]), -1)
    from_ahead = turn(pick(c, far[...], near[...]), 1)
    both = combine([own, from_back, from_ahead])
    three[...] = both
    message[...] = pick(c, both, combine([own, from_back]))


def last_kernel(place, three, got, other, energy, own):
    c, h = place[0:1, :], place[4:5, :]
    from_back = turn(pick(c, got[...], other[...]), -3)
    from_ahead = turn(pick(c, other[...], got[...]), 3)
    block = combine([three[...], from_back, from_ahead])
    n = block.shape[2]
    own[...] = block[:, 0]

    def steps(half, step):
        return [pick(c, block[2 * half + i, NZ - step : NZ - step + 1], block[2 * half + i, step : step + 1]) for i in range(2)]

    out = [pick(c, block[2 * half, 0:1], block[2 * half + 1, 0:1]) for half in range(2)]
    for step in range(1, 4):
        low, top = steps(0, step), steps(1, step)
        out += [pick(h, low[i], top[i]) for i in range(2)] + [pick(h, top[i], low[i]) for i in range(2)]
    low, top = (pick(c, block[2 * half, 4:5], block[2 * half + 1, 4:5]) for half in range(2))
    out += [pick(h, low, top), pick(h, top, low)]
    for i, v in enumerate(out):
        energy[:, i * n : (i + 1) * n] = v


def energies(local, place, sub):
    (mine,) = small(pack_kernel, place, [(16, sub)], *local)
    (mine,) = small(sum_kernel, place, [(16, sub)], mine, *[shift_y(mine, d) for d in (1, 3, 2)])
    shape = (4, NZ, sub)
    (block,) = small(block_kernel, place, [shape], mine, swap_cores(mine))
    near = along_z(block, 1)
    three, message = small(near_kernel, place, [shape] * 2, block, near, swap_cores(near))
    got = along_z(message, 3)
    energy, own = small(last_kernel, place, [(1, 16 * sub), (4, sub)], three, got, swap_cores(got))
    return energy, own.reshape(-1)


def turned(column):
    n = column.shape[0]
    return jnp.transpose(jnp.broadcast_to(column, (n, n)))


def write_message(message, at, total, row):
    n, width = total.shape
    message[at : at + n, :] = total.astype(BF16)
    high = row.astype(BF16)
    tail = [high, (row - high.astype(F32)).astype(BF16)]
    if width > 2 * n:
        tail.append(jnp.zeros((TAIL, width - 2 * n), BF16))
    message[at + n : at + n + TAIL, :] = jnp.concatenate(tail, axis=1)


def read_message(message, at, n):
    total = message[at : at + n, :].astype(F32)
    tail = message[at + n : at + n + TAIL, :].astype(F32)
    return total, tail[:, :n] + tail[:, n : 2 * n]


def score_kernel(parts, sizes, *refs):
    if parts:
        table, pieces, (block, squares, logits, energy) = refs[:parts], refs[parts:-4], refs[-4:]
    else:
        block, squares, *pieces = refs[:-2]
        logits, energy = refs[-2:]
    height = block.shape[0]
    span = height // NX
    if parts:
        n = table[0].shape[0]
        for p in range(parts):
            lot = slice(p * n, (p + 1) * n)
            part = table[p][...]
            block[lot, :] = part
            wide = part.astype(F32)
            total = jnp.sum(wide * wide, axis=1, keepdims=True)
            squares[lot, :] = jnp.broadcast_to(total, (n, squares.shape[1]))
    batches, at = [[]], 0
    for piece, size in zip(pieces, sizes):
        if sum(k for _, k in batches[-1]) >= BATCH:
            batches.append([])
        batches[-1].append((piece, size))
    for batch in batches:
        rows = jnp.concatenate([piece[...] for piece, _ in batch])
        lot = slice(at, at + rows.shape[0])
        at += rows.shape[0]
        high = None
        for k in range(0, height, span):
            product = lax.dot_general(
                block[k : k + span, :], rows, (((1,), (1,)), ((), ())), preferred_element_type=F32
            )
            scores = 2.0 * product - squares[k : k + span, :1]
            logits[k : k + span, lot] = scores
            top = jnp.max(scores, axis=0, keepdims=True)
            high = top if high is None else jnp.maximum(high, top)
        total = None
        for k in range(0, height, span):
            part = jnp.sum(jnp.exp(logits[k : k + span, lot] - high), axis=0, keepdims=True)
            total = part if total is None else total + part
        energy[:, lot] = high + jnp.log(total)


def score(table, pieces):
    whole = len(table) == 2
    count = table[0].shape[0] if whole else sum(t.shape[0] for t in table)
    width, sizes = table[0].shape[1], tuple(p.shape[0] for p in pieces)
    rows = sum(sizes)
    out = [
        pltpu.VMEM((count, rows), F32) if PIN else jax.ShapeDtypeStruct((count, rows), F32),
        jax.ShapeDtypeStruct((1, rows), F32),
    ]
    if not whole:
        out = [jax.ShapeDtypeStruct((count, width), BF16), jax.ShapeDtypeStruct((count, 128), F32)] + out
    return pl.pallas_call(
        functools.partial(score_kernel, 0 if whole else len(table), sizes),
        out_shape=out,
        compiler_params=pltpu.CompilerParams(vmem_limit_bytes=VMEM_LIMIT),
        cost_estimate=pl.CostEstimate(
            flops=4 * count * rows * width,
            bytes_accessed=4 * count * rows + 2 * (count + rows) * width,
            transcendentals=count * rows,
        ),
    )(*table, *pieces)


def weigh_kernel(lots, groups, sizes, keeps, sends, energy, *refs):
    logits, refs = refs[: len(groups)], refs[len(groups) :]
    slab, out = refs[: len(sizes)], list(refs[len(sizes) :])
    n, width = logits[0].shape[0] // (NX * NC), slab[0].shape[1]
    step, tile = min(sizes), min(256, width)
    places, at, g, edge = [], 0, 0, 0
    for size in sizes:
        if at - edge == groups[g]:
            g, edge = g + 1, at
        places.append((logits[g], at - edge, at, size))
        at += size
    units = [[p] for p, size in enumerate(sizes) if size > step]
    units.append([p for p, size in enumerate(sizes) if size == step])
    units = [units[k] + units[k + 1] for k in range(0, len(units), 2)]
    message = out.pop(0) if sends else None
    if keeps:
        keep, keep_count, total = out
    else:
        (total,) = out
    counts = [None] * len(lots)
    for k, unit in enumerate(units):
        parts = []
        for i, lot in enumerate(lots):
            row = []
            for ref, col, at, size in (places[p] for p in unit):
                for cut in range(0, size, step):
                    w = jnp.exp(ref[lot : lot + n, col + cut : col + cut + step] - energy[:, at + cut : at + cut + step])
                    counts[i] = w if counts[i] is None else counts[i] + w
                    row.append(w.astype(BF16))
            parts.append(jnp.concatenate(row, axis=1))
        w = jnp.concatenate(parts)
        for at in range(0, width, tile):
            block = jnp.concatenate([slab[p][:, at : at + tile] for p in unit])
            term = jnp.dot(w, block, preferred_element_type=F32)
            if k:
                term = total[:, at : at + tile] + term
            if k < len(units) - 1:
                total[:, at : at + tile] = term
                continue
            if keeps:
                keep[:, at : at + tile] = term[: keeps * n]
            for i in range(sends):
                part = term[(keeps + i) * n : (keeps + i + 1) * n]
                message[i * (n + TAIL) : i * (n + TAIL) + n, at : at + tile] = part.astype(BF16)
    rows = [turned(jnp.sum(v, axis=1, keepdims=True))[:TAIL] for v in counts]
    for i, row in enumerate(rows[:keeps]):
        keep_count[i * TAIL : (i + 1) * TAIL, :] = row
    for i, row in enumerate(rows[keeps:]):
        at = i * (n + TAIL) + n
        high = row.astype(BF16)
        message[at : at + TAIL, :n] = high
        message[at : at + TAIL, n : 2 * n] = (row - high.astype(F32)).astype(BF16)
        if width > 2 * n:
            message[at : at + TAIL, 2 * n :] = jnp.zeros((TAIL, width - 2 * n), BF16)


def weigh(keeps, sends, logits, energy, slab):
    n, width = logits[0].shape[0] // (NX * NC), slab[0].shape[1]
    sizes, groups = tuple(p.shape[0] for p in slab), tuple(v.shape[1] for v in logits)
    lots = [k * NC * n for k in keeps] + [k * NC * n + n for k in sends]
    out = []
    if sends:
        out.append(jax.ShapeDtypeStruct((len(sends) * (n + TAIL), width), BF16))
    if keeps:
        out.append(jax.ShapeDtypeStruct((len(keeps) * n, width), F32))
        out.append(jax.ShapeDtypeStruct((len(keeps) * TAIL, n), F32))
    total, height = sum(sizes), len(lots) * n
    return pl.pallas_call(
        functools.partial(weigh_kernel, lots, groups, sizes, len(keeps), len(sends)),
        out_shape=out,
        scratch_shapes=[pltpu.VMEM((height, width), F32)],
        compiler_params=pltpu.CompilerParams(vmem_limit_bytes=VMEM_LIMIT),
        cost_estimate=pl.CostEstimate(
            flops=2 * height * total * width,
            bytes_accessed=4 * height * total + 2 * total * width,
            transcendentals=height * total,
        ),
    )(energy, *logits, *slab)


def call(kernel, out_shape, *args):
    return pl.pallas_call(
        kernel,
        out_shape=out_shape,
        compiler_params=pltpu.CompilerParams(vmem_limit_bytes=VMEM_LIMIT),
    )(*args)


def add_kernel(n, got, keep, keep_count, *messages):
    for i, message in enumerate(messages):
        total, row = read_message(got, i * (n + TAIL), n)
        total = total + keep[i * n : (i + 1) * n, :]
        write_message(message, 0, total, row + keep_count[i * TAIL : (i + 1) * TAIL, :])


def add(got, keep, keep_count):
    n = keep_count.shape[1]
    shape = jax.ShapeDtypeStruct((n + TAIL, got.shape[1]), BF16)
    return call(functools.partial(add_kernel, n), (shape,) * (NX - 1), got, keep, keep_count)


def update_kernel(n, keep, keep_count, got, one, two, three, masses, centroids, new_centroids, new_masses):
    total, row = keep[...], keep_count[...]
    for message in (got, one, two, three):
        t, r = read_message(message, 0, n)
        total, row = total + t, row + r
    mass = masses[...]
    new = mass + row[:1]
    new_masses[...] = new
    column = lambda v: jnp.transpose(jnp.broadcast_to(v, (n, n)))[:, :1]
    new_centroids[...] = (column(mass) * centroids[...].astype(F32) + total) / column(new)


def update(keep, keep_count, got, others, masses, centroids):
    n, width = centroids.shape
    out = (jax.ShapeDtypeStruct((n, width), F32), jax.ShapeDtypeStruct((1, n), F32))
    return call(
        functools.partial(update_kernel, n), out, keep, keep_count, got, *others, masses.reshape(1, n), centroids
    )


def shards(embeddings, centroids, masses):
    y, c = lax.axis_index("y"), lax.axis_index("c")
    rows, width = embeddings.shape
    half, sub = rows // 2, rows // 4
    h = lax.rem(y, 2)
    place = jnp.concatenate([jnp.full((4, sub), c, F32), jnp.full((4, sub), h, F32)])
    core, start_c, start_h = (v.astype(jnp.uint32) for v in (c, c * sub, h * half))
    place, embeddings, core, start_c, start_h = lax.optimization_barrier((place, embeddings, core, start_c, start_h))

    near = {0: centroids, 1: shift_x(centroids, -1), 3: shift_x(centroids, 1)}

    mine = lax.dynamic_slice_in_dim(embeddings, start_h, half, 0)
    one = along_z(mine, 1)
    own = lax.dynamic_slice_in_dim(embeddings.reshape(2, 2, sub, width), core, 1, 1).reshape(half, width)
    one, near[1], near[3] = lax.optimization_barrier((one, near[1], near[3]))
    near[2] = shift_x(near[1], -1)
    first = swap_halves(one)
    two = along_z(one, 1)
    two, near[2] = lax.optimization_barrier((two, near[2]))
    three = along_z(two, 1)
    two, first = lax.optimization_barrier((two, first))

    fixed = lambda v: pltpu.with_memory_space_constraint(v, pltpu.VMEM) if PIN else v
    table = [fixed(v) for d in ORDER for v in (near[d], swap_cores(near[d]))]

    sides = [swap_halves(two), swap_halves(three)]
    part, *table = lax.optimization_barrier([three, *table])
    part = lax.dynamic_slice_in_dim(part, start_c, sub, 0)
    four, last = along_z(part, 1), from_partner(part)
    lots = [[fixed(v) for v in (own, one, first, two, sides[0])]]
    *table, scores, energy = score(table, lots[0])
    table, logits, local = [fixed(v) for v in table], [scores], [energy]
    middle, _ = lax.optimization_barrier((three, energy))
    lots.append([fixed(middle)])
    scores, energy = score(table, lots[1])
    last, _ = lax.optimization_barrier((last, energy))
    logits.append(scores)
    local.append(energy)
    lots.append([fixed(sides[1]), fixed(four), fixed(last)])
    scores, energy = score(table, lots[2])
    logits.append(scores)
    local.append(energy)
    energy, row_energy = energies(local, place, sub)
    logits, pieces = [fixed(v) for v in logits], [v for lot in lots for v in lot]

    sent = list(range(NX - 1))
    (message,) = weigh([], sent, logits, energy, pieces)
    got = swap_cores(message)
    keep, keep_count = weigh(sent, [], logits, energy, pieces)
    others = [shift_x(m, d) for m, d in zip(add(got, keep, keep_count), ORDER)]
    energy, others[0] = lax.optimization_barrier((energy, others[0]))
    message, keep, keep_count = weigh([NX - 1], [NX - 1], logits, energy, pieces)
    new_centroids, new_masses = update(keep, keep_count, swap_cores(message), others, masses, centroids)
    return new_centroids, new_masses.reshape(-1), row_energy


def solution(mesh):
    grid = Mesh(mesh.devices.reshape(NX, NZ, NY, NC), ("x", "z", "y", "c"))
    rows, cents = ("x", "z"), ("y", "c", "x", "z")
    return jax.shard_map(
        shards,
        mesh=grid,
        in_specs=(P(rows, None), P(cents, None), P(cents)),
        out_specs=(P(cents, None), P(cents), P(rows)),
        check_vma=False,
    )
```
